128 devices in a mesh: half: 2 (over z_lo), row: 8 (over x, z_hi), col: 8 (over y, core).
Axes of the slice: x: 4, y: 4, z: 4 (z_hi: 2, z_lo: 2; z = z_hi * 2 + z_lo), core: 2. Of those that a mesh axis runs over, the one named last changes fastest.
Arguments:
- child_pivot: float32 [2, 1024, 1024], P('half'), may hold values from 0 to 6, as said below
- child_border: float32 [2, 8, 8, 128, 1024], P('half', None, 'row'), may hold values from 0 to 6, as said below
- child_update: float32 [2, 8, 8, 128, 8, 8, 128], P('half', None, 'row', None, None, 'col'), may hold values from 0 to 6, as said below
- index_map: int32 [2, 64], replicated, may hold values from 0 to 79, as said below
- root_front: float32 [5, 16, 128, 10, 8, 128], P(None, ('half', 'row'), None, None, 'col'), may hold values from 0 to 6, as said below
Outputs:
- child_factor: float32 [2, 8, 8, 128, 1024], P('half', None, 'row')
- root_factor: float32 [5, 16, 128, 10, 8, 128], P(None, ('half', 'row'), None, None, 'col')
The draws below stay inside these ranges and needn't reach their ends.
Inputs may be any that keep to these rules, and one draw needn't show every extreme that they name: `index_map`: for each sibling the entries are distinct; entry p gives the root block that receives update block p. Among the entries p of one sibling with equal p modulo the row axis's device count (a class), no residue modulo that count occurs more than 2 times, and in every class one residue occurs exactly 2 times; within a class no residue modulo twice that count occurs more than once; in particular the two entries sharing a residue differ modulo twice that count. child_pivot[s], child_border[s] and child_update[s] are the pivot, border and update blocks of one symmetric positive definite front of order 1024 + 8192; entries are not negative. `child_border`: the border block of the front described for child_pivot. `child_update`: the update block of the front described for child_pivot. `root_front`: symmetric positive definite; entries are not negative.
All inputs are finite; a program needn't handle non-finite values.
Results may differ from the reference program's by a relative error of at most 0.00012.
Values sent between devices are 32-bit elements; how exact they have to be, the bound alone decides.
No kernel may reach another device: no remote copies, remote signals or barrier semaphores. Data moves between devices by JAX's collectives and lax.ppermute only.
A program may use at most 192 MiB of HBM per device.

```python
import jax
import jax.numpy as jnp
from jax import lax

NB = 128
PIV = 1024
UPD = 8192
ROOT = 10240
PANEL = 1024
LB = 8
LRR = 5
LRC = 10
N_ROW = 8
N_COL = 8


corr_length = 0.15


def site_points(key, copies, point_count, power, spread):
    coords = jax.random.uniform(jax.random.fold_in(key, 1), (copies, 3, point_count), jnp.float32) ** power
    scales = jnp.exp(spread * jax.random.uniform(jax.random.fold_in(key, 2), (copies, point_count), jnp.float32, -1.0, 1.0))
    nugget = jax.random.uniform(jax.random.fold_in(key, 3), (copies, point_count), jnp.float32, 0.5, 1.5)
    return (coords, scales, nugget)


def kernel_block(points, row_start, row_stop, col_start, col_stop, diagonal):
    coords, scales, nugget = points
    distance = jnp.zeros((coords.shape[0], row_stop - row_start, col_stop - col_start), jnp.float32)
    for axis_number in range(3):
        distance = distance + jnp.abs(coords[:, axis_number, row_start:row_stop, None] - coords[:, axis_number, None, col_start:col_stop])
    entries = scales[:, row_start:row_stop, None] * scales[:, None, col_start:col_stop] * jnp.exp(-distance / corr_length)
    if diagonal:
        same_index = jnp.arange(row_stop - row_start)[:, None] == jnp.arange(col_stop - col_start)[None, :]
        entries = entries + jnp.where(same_index[None], nugget[:, row_start:row_stop, None], 0.0)
    return entries


def draw_child_pivot(key, part):
    power, spread = (1.0, 0.35)
    points = site_points(key, 2, PIV + UPD, power, spread)
    return kernel_block(points, 0, PIV, 0, PIV, True)


def draw_child_border(key, part):
    power, spread = (1.0, 0.35)
    points = site_points(key, 2, PIV + UPD, power, spread)
    return kernel_block(points, PIV, PIV + UPD, 0, PIV, False).reshape(2, LB, N_ROW, NB, PIV)


def draw_child_update(key, part):
    power, spread = (1.0, 0.35)
    points = site_points(key, 2, PIV + UPD, power, spread)
    return kernel_block(points, PIV, PIV + UPD, PIV, PIV + UPD, True).reshape(2, LB, N_ROW, NB, LB, N_COL, NB)


def draw_root_front(key, part):
    key = jax.random.fold_in(key, 41)
    power, spread = (1.0, 0.35)
    points = site_points(key, 1, ROOT, power, spread)
    return kernel_block(points, 0, ROOT, 0, ROOT, True)[0].reshape(LRR, 2 * N_ROW, NB, LRC, N_COL, NB)


def draw_index_map(key, part):
    key = jax.random.fold_in(key, 11)
    buckets = N_ROW
    repeats = UPD // NB // (buckets * buckets)
    per_class = repeats * buckets
    half_blocks = ROOT // NB // (2 * buckets)
    maps = []
    for sibling in range(2):
        sibling_key = jax.random.fold_in(key, sibling)
        doubled = jax.random.permutation(jax.random.fold_in(sibling_key, 1), buckets).astype(jnp.int32)
        offset = jax.random.randint(jax.random.fold_in(sibling_key, 2), (), 1, buckets)
        missing = doubled[(jnp.arange(buckets, dtype=jnp.int32) + offset) % buckets]
        residues = jnp.tile(jnp.arange(buckets, dtype=jnp.int32), (buckets, repeats))
        position = jnp.arange(per_class, dtype=jnp.int32)[None, :]
        residues = jnp.where(position == missing[:, None], doubled[:, None], residues)
        class_keys = jax.random.split(jax.random.fold_in(sibling_key, 3), buckets)
        shuffles = jax.vmap(lambda one_key: jax.random.permutation(one_key, per_class))(class_keys)
        residues = jnp.take_along_axis(residues, shuffles.astype(jnp.int32), axis=1)
        class_hot = (residues[:, :, None] == jnp.arange(buckets, dtype=jnp.int32)[None, None, :]).astype(jnp.int32)
        class_rank = jnp.sum(class_hot * (jnp.cumsum(class_hot, axis=1) - class_hot), axis=2)
        parity = (class_rank + jnp.arange(buckets, dtype=jnp.int32)[:, None]) % 2
        flat_residue = residues.T.reshape(per_class * buckets)
        flat_parity = parity.T.reshape(per_class * buckets)
        slot_key = flat_residue * 2 + flat_parity
        onehot = (slot_key[:, None] == jnp.arange(2 * buckets, dtype=jnp.int32)[None, :]).astype(jnp.int32)
        earlier = jnp.cumsum(onehot, axis=0) - onehot
        rank = jnp.sum(onehot * earlier, axis=1)
        slot_keys = jax.random.split(jax.random.fold_in(sibling_key, 4), 2 * buckets)
        rests = jax.vmap(lambda one_key: jax.random.permutation(one_key, half_blocks - 1))(slot_keys).astype(jnp.int32)
        slot_parity = jnp.arange(2 * buckets, dtype=jnp.int32) % 2
        heads = jnp.where(slot_parity == 0, 0, half_blocks - 1).astype(jnp.int32)
        rests = rests + jnp.where(slot_parity == 0, 1, 0).astype(jnp.int32)[:, None]
        orders = jnp.concatenate([heads[:, None], rests], axis=1)
        chosen_block = 2 * orders[slot_key, rank] + flat_parity
        maps.append(chosen_block * buckets + flat_residue)
    return jnp.stack(maps).astype(jnp.int32)


def setup_inputs(seed: int = 0) -> dict:
    seeds = jax.random.split(jax.random.key(seed), 6)
    return {
        "child_pivot": draw_child_pivot(jax.random.fold_in(seeds[5], 71), 0),
        "child_border": draw_child_border(jax.random.fold_in(seeds[5], 71), 0),
        "child_update": draw_child_update(jax.random.fold_in(seeds[5], 71), 0),
        "index_map": draw_index_map(jax.random.fold_in(seeds[5], 71), 0),
        "root_front": draw_root_front(jax.random.fold_in(seeds[5], 71), 0),
    }


precise = lax.Precision.HIGHEST

def solve_right(lower_factor, right_side):
    return lax.linalg.triangular_solve(lower_factor, right_side, left_side=False, lower=True, transpose_a=True)

def reference(child_pivot, child_border, child_update, index_map, root_front):
    offsets = jnp.arange(NB, dtype=jnp.int32)
    scattered = jnp.zeros((ROOT, ROOT), jnp.float32)
    factors = []
    for sibling in range(2):
        pivot_factor = jnp.linalg.cholesky(child_pivot[sibling])
        child_rows = solve_right(pivot_factor, child_border[sibling].reshape(UPD, PIV))
        factors.append(child_rows.reshape(LB, N_ROW, NB, PIV))
        update = child_update[sibling].reshape(UPD, UPD) - jnp.dot(child_rows, child_rows.T, precision=precise)
        positions = (index_map[sibling].astype(jnp.int32)[:, None] * NB + offsets[None, :]).reshape(UPD).astype(jnp.int32)
        spread_rows = jnp.zeros((ROOT, UPD), jnp.float32).at[positions].set(update)
        scattered = scattered.at[:, positions].add(spread_rows)
    assembled = root_front.reshape(ROOT, ROOT) + scattered
    root_pivot = jnp.linalg.cholesky(assembled[:PANEL, :PANEL])
    lower_rows = solve_right(root_pivot, assembled[PANEL:, :PANEL])
    trailing = assembled[PANEL:, PANEL:] - jnp.dot(lower_rows, lower_rows.T, precision=precise)
    combined = jnp.zeros((ROOT, ROOT), jnp.float32)
    combined = combined.at[:PANEL, :PANEL].set(root_pivot)
    combined = combined.at[PANEL:, :PANEL].set(lower_rows)
    combined = combined.at[PANEL:, PANEL:].set(trailing)
    return (jnp.stack(factors), combined.reshape(LRR, 2 * N_ROW, NB, LRC, N_COL, NB))
```

```python
import functools

import jax
import jax.numpy as jnp
from jax import lax
from jax.experimental import pallas as pl
from jax.experimental.pallas import tpu as pltpu
from jax.sharding import PartitionSpec as P

PANEL = 1024
BLOCK = 128
STRIP = 32
F32 = jnp.float32
BF16 = jnp.bfloat16

exact = lax.Precision.HIGHEST
close = lax.Precision.HIGH


def split_three(values):
    high = values.astype(BF16)
    rest = values - high.astype(F32)
    middle = rest.astype(BF16)
    low = (rest - middle.astype(F32)).astype(BF16)
    return high, middle, low


def gram_strip(rows):
    high, middle, low = split_three(rows)
    left = jnp.concatenate([high, high, middle, high, middle, low], axis=0)
    right = jnp.concatenate([high, middle, high, low, middle, high], axis=0)
    return lax.dot_general(left, right, (((0,), (0,)), ((), ())), preferred_element_type=F32)


def inverse_root(pivot):
    guess = lax.rsqrt(pivot)
    return guess * (1.5 - 0.5 * pivot * guess * guess)


def eliminate_strip(rows, start):
    lanes = lax.broadcasted_iota(jnp.int32, (STRIP, BLOCK), 1)
    sublanes = lax.broadcasted_iota(jnp.int32, (STRIP, BLOCK), 0)
    columns = [
        jnp.broadcast_to(rows[:, start + j : start + j + 1], (STRIP, BLOCK)) for j in range(STRIP)
    ]
    inside = jnp.logical_and(lanes >= start, lanes < start + STRIP)
    rows = jnp.where(inside, jnp.where(lanes - start == sublanes, 1.0, 0.0), rows)
    for j in range(STRIP):
        scale = inverse_root(jnp.broadcast_to(columns[j][j : j + 1, :], (8, BLOCK)))
        factor = columns[j] * jnp.concatenate([scale] * (STRIP // 8), axis=0)
        for k in range(j + 1, STRIP):
            columns[k] = columns[k] - factor * jnp.broadcast_to(
                factor[k : k + 1, :], (STRIP, BLOCK)
            )
        solved = jnp.broadcast_to(rows[j : j + 1, :] * scale[0:1, :], (STRIP, BLOCK))
        rows = jnp.where(
            sublanes == j, solved, rows - jnp.where(sublanes > j, factor, 0.0) * solved
        )
    return rows


def eliminate_block(block):
    for start in range(0, BLOCK, STRIP):
        stop = start + STRIP
        rows = eliminate_strip(block[start:stop, :], start)
        block[start:stop, :] = rows
        if stop < BLOCK:
            change = gram_strip(rows)[stop:, :]
            lanes = lax.broadcasted_iota(jnp.int32, (BLOCK - stop, BLOCK), 1)
            inside = jnp.logical_and(lanes >= start, lanes < stop)
            block[stop:, :] = jnp.where(inside, 0.0, block[stop:, :]) - change


def inverse_factor_kernel(matrix, state, block, scaled):
    count = matrix.shape[0] // BLOCK
    state[...] = matrix[...]
    row_ids = lax.broadcasted_iota(jnp.int32, (BLOCK, BLOCK), 0)
    col_ids = lax.broadcasted_iota(jnp.int32, (BLOCK, BLOCK), 1)

    def step(j, _):
        here = pl.ds(pl.multiple_of(j * BLOCK, BLOCK), BLOCK)
        block[...] = state[here, here]
        eliminate_block(block)
        inverse = jnp.where(col_ids <= row_ids, block[...], 0.0)
        state[here, here] = jnp.where(col_ids == row_ids, 1.0, 0.0).astype(F32)
        scaled[...] = jnp.dot(
            inverse, state[here, :], precision=exact, preferred_element_type=F32
        )
        state[here, :] = scaled[...]

        def update(i, _):
            there = pl.ds(pl.multiple_of(i * BLOCK, BLOCK), BLOCK)
            state[there, here] = jnp.zeros((BLOCK, BLOCK), F32)
            state[there, :] = state[there, :] - lax.dot_general(
                scaled[:, there],
                scaled[...],
                (((0,), (0,)), ((), ())),
                precision=exact,
                preferred_element_type=F32,
            )
            return 0

        lax.fori_loop(j + 1, count, update, 0)
        return 0

    lax.fori_loop(0, count, step, 0)

    def clear(i, _):
        here = pl.ds(pl.multiple_of(i * BLOCK, BLOCK), BLOCK)

        def clear_block(k, _):
            right = pl.ds(pl.multiple_of(k * BLOCK, BLOCK), BLOCK)
            state[here, right] = jnp.zeros((BLOCK, BLOCK), F32)
            return 0

        lax.fori_loop(i + 1, count, clear_block, 0)
        return 0

    lax.fori_loop(0, count, clear, 0)


def inverse_factor(matrix):
    order = matrix.shape[0]
    whole = pl.BlockSpec(memory_space=pltpu.VMEM)
    return pl.pallas_call(
        inverse_factor_kernel,
        out_shape=jax.ShapeDtypeStruct((order, order), F32),
        in_specs=[whole],
        out_specs=whole,
        scratch_shapes=[pltpu.VMEM((BLOCK, BLOCK), F32), pltpu.VMEM((BLOCK, order), F32)],
        compiler_params=pltpu.CompilerParams(vmem_limit_bytes=32 * 1024 * 1024),
        cost_estimate=pl.CostEstimate(
            flops=60_000_000_000, bytes_accessed=8 * order * order, transcendentals=0
        ),
        name="inverse_factor",
    )(matrix)


def spread_kernel(slots, source, target):
    blocks = source.shape[0] // target.shape[1]
    for b in range(blocks):
        target[slots[b]] = source[pl.ds(b, target.shape[1], stride=blocks), :]


def spread_columns(slots, source, slot_total, blocks):
    rows = source.shape[0] // blocks
    tile = rows // 4
    return pl.pallas_call(
        spread_kernel,
        out_shape=jax.ShapeDtypeStruct((slot_total, rows, BLOCK), F32),
        grid_spec=pltpu.PrefetchScalarGridSpec(
            num_scalar_prefetch=1,
            grid=(4,),
            in_specs=[pl.BlockSpec((tile * blocks, BLOCK), lambda i, s: (i, 0))],
            out_specs=pl.BlockSpec((slot_total, tile, BLOCK), lambda i, s: (0, i, 0)),
        ),
        compiler_params=pltpu.CompilerParams(vmem_limit_bytes=32 * 1024 * 1024),
        cost_estimate=pl.CostEstimate(
            flops=0, bytes_accessed=4 * BLOCK * rows * (blocks + slot_total), transcendentals=0
        ),
        name="spread_columns",
    )(slots, source)


def ranks(targets):
    same = targets[..., :, None] == targets[..., None, :]
    length = targets.shape[-1]
    earlier = jnp.arange(length)[:, None] > jnp.arange(length)[None, :]
    return jnp.sum(jnp.logical_and(same, earlier).astype(jnp.int32), axis=-1)


def locate(matches, values):
    matches = matches.astype(jnp.int32)
    return (jnp.sum(matches * values, axis=-1), jnp.sum(matches, axis=-1) > 0)


def times_transposed(left, right, precision):
    return lax.dot_general(
        left, right, (((1,), (1,)), ((), ())), precision=precision, preferred_element_type=F32
    )


def per_device(child_pivot, child_border, child_update, index_map, root_front):
    n_rows = lax.axis_size("row")
    n_cols = lax.axis_size("col")
    groups = 2 * n_rows
    sibling = lax.axis_index("half")
    row_index = lax.axis_index("row")
    col_index = lax.axis_index("col")
    group = sibling * n_rows + row_index
    block_count = child_border.shape[1]
    pivots = child_border.shape[4]
    local_rows = block_count * BLOCK
    root_rows = root_front.shape[0]
    root_cols = root_front.shape[3]
    capacity = 2
    numbers = jnp.arange(block_count, dtype=jnp.int32)

    child_map = lax.dynamic_index_in_dim(index_map, sibling, 0, keepdims=False).reshape(
        block_count, n_rows
    )
    by_class = child_map.T
    class_dest = by_class % n_cols
    class_rank = ranks(class_dest)
    col_dest = lax.dynamic_index_in_dim(class_dest, col_index, 0, keepdims=False)
    col_rank = lax.dynamic_index_in_dim(class_rank, col_index, 0, keepdims=False)
    row_map = lax.dynamic_index_in_dim(by_class, row_index, 0, keepdims=False)
    row_dest = lax.dynamic_index_in_dim(class_dest, row_index, 0, keepdims=False)
    row_rank = lax.dynamic_index_in_dim(class_rank, row_index, 0, keepdims=False)

    border = child_border.reshape(block_count, BLOCK, pivots)
    wanted, _ = locate(
        jnp.logical_and(
            row_dest[None, :] == col_index,
            row_rank[None, :] == jnp.arange(capacity, dtype=jnp.int32)[:, None],
        ),
        numbers,
    )
    own_wanted = jnp.take(border, wanted, axis=0)
    every_wanted = lax.all_gather(own_wanted, "row", axis=0, tiled=True)

    sending = spread_columns(
        col_dest * capacity + col_rank,
        child_update.reshape(local_rows * block_count, BLOCK),
        n_cols * capacity,
        block_count,
    )
    arrived = lax.all_to_all(sending, "col", split_axis=0, concat_axis=0, tiled=True)

    flat_source = numbers[:, None] * capacity + class_rank
    wanted_roots = jnp.arange(root_cols, dtype=jnp.int32) * n_cols + col_index
    source_slots, source_there = locate(
        by_class.reshape(1, -1) == wanted_roots[:, None], flat_source.reshape(-1)
    )

    inverse = inverse_factor(child_pivot[0])
    own_factor = times_transposed(border.reshape(local_rows, pivots), inverse, exact)
    column_border = jnp.take(every_wanted, source_slots, axis=0)
    column_update = jnp.take(arrived, source_slots, axis=0)

    def schur(first, last):
        count = last - first
        factor = times_transposed(
            column_border[first:last].reshape(count * BLOCK, pivots), inverse, exact
        )
        product = lax.dot_general(
            factor.reshape(count, BLOCK, pivots),
            own_factor,
            (((2,), (1,)), ((), ())),
            precision=close,
            preferred_element_type=F32,
        )
        product = jnp.transpose(product, (0, 2, 1))
        there = source_there[first:last, None, None]
        return jnp.where(there, column_update[first:last] - product, 0.0).reshape(
            count, block_count, BLOCK, BLOCK
        )

    panel_update = schur(0, 1)[0]
    root_view = root_front.reshape(root_rows, BLOCK, root_cols, BLOCK)

    top_index, top_there = locate(row_map[None, :] == numbers[:, None], numbers)
    top_part = jnp.where(top_there[:, None, None], jnp.take(panel_update, top_index, axis=0), 0.0)
    is_owner = jnp.logical_and(sibling == 0, row_index == numbers)
    top_part = top_part + jnp.where(is_owner[:, None, None], root_view[0, :, 0, :][None], 0.0)
    leading_cols = lax.psum(top_part, ("half", "row")).reshape(PANEL, BLOCK)
    leading = lax.all_gather(leading_cols, "col", axis=1, tiled=True)

    sent_blocks, _ = locate(
        (row_map % groups)[None, :] == jnp.arange(groups, dtype=jnp.int32)[:, None], numbers
    )
    every_map = index_map.reshape(2, 1, block_count * n_rows)
    my_roots = jnp.arange(root_rows, dtype=jnp.int32) * groups + group
    sender = (
        jnp.arange(2, dtype=jnp.int32)[:, None, None] * n_rows
        + (jnp.arange(block_count * n_rows, dtype=jnp.int32) % n_rows)[None, None, :]
    )
    got_slots, got_there = locate(every_map == my_roots[None, :, None], sender)

    def extend_add(base, received):
        shape = (-1,) + (1,) * (received.ndim - 1)
        for half in range(2):
            picked = jnp.take(received, got_slots[half], axis=0)
            base = base + jnp.where(got_there[half].reshape(shape), picked, 0.0)
        return base

    panel_sent = jnp.take(panel_update, sent_blocks, axis=0)
    panel_got = lax.all_to_all(
        panel_sent, ("half", "row"), split_axis=0, concat_axis=0, tiled=True
    )
    own_panel = extend_add(root_view[:, :, 0, :], panel_got)
    panel_rows = lax.all_gather(own_panel, "col", axis=2, tiled=True)
    swaps = [(r * n_cols + c, c * n_rows + r) for r in range(n_rows) for c in range(n_cols)]
    swapped = lax.ppermute(own_panel, ("row", "col"), swaps)
    column_panel = lax.all_gather(swapped, ("half", "row"), axis=0, tiled=False).reshape(
        2, n_rows, root_rows, BLOCK, BLOCK
    )
    column_panel = jnp.transpose(column_panel, (2, 0, 3, 1, 4)).reshape(root_cols, BLOCK, PANEL)

    rest_update = schur(1, root_cols)
    rest_sent = jnp.take(jnp.transpose(rest_update, (1, 0, 2, 3)), sent_blocks, axis=0)
    rest_got = lax.all_to_all(rest_sent, ("half", "row"), split_axis=0, concat_axis=0, tiled=True)

    root_inverse = inverse_factor(leading)
    factor_rows = times_transposed(panel_rows.reshape(root_rows * BLOCK, PANEL), root_inverse, exact)
    column_factor = times_transposed(
        column_panel[1:].reshape((root_cols - 1) * BLOCK, PANEL), root_inverse, exact
    )
    global_rows = (
        my_roots[:, None] * BLOCK + jnp.arange(BLOCK, dtype=jnp.int32)[None, :]
    ).reshape(-1)
    is_top = global_rows < PANEL
    above = jnp.logical_and(
        is_top[:, None], jnp.arange(PANEL, dtype=jnp.int32)[None, :] > global_rows[:, None]
    )
    factor_rows = jnp.where(above, 0.0, factor_rows)
    rest = jnp.transpose(root_view[:, :, 1:, :], (0, 2, 1, 3))
    rest = extend_add(rest, rest_got)
    trailing = jnp.transpose(rest, (0, 2, 1, 3)).reshape(
        root_rows * BLOCK, -1
    ) - times_transposed(factor_rows, column_factor, close)
    panel_part = lax.dynamic_index_in_dim(
        factor_rows.reshape(-1, n_cols, BLOCK), col_index, 1, keepdims=False
    )
    remainder = jnp.where(is_top[:, None], 0.0, trailing)
    combined = jnp.concatenate([panel_part, remainder], axis=1)
    return (own_factor.reshape(child_border.shape), combined.reshape(root_front.shape))


def solution(mesh):
    in_specs = (
        P("half", None, None),
        P("half", None, "row", None, None),
        P("half", None, "row", None, None, "col", None),
        P(),
        P(None, ("half", "row"), None, None, "col", None),
    )
    out_specs = (
        P("half", None, "row", None, None),
        P(None, ("half", "row"), None, None, "col", None),
    )
    return jax.shard_map(
        per_device, mesh=mesh, in_specs=in_specs, out_specs=out_specs, check_vma=False
    )
```

```python
import functools

import jax
import jax.numpy as jnp
from jax import lax
from jax.experimental import pallas as pl
from jax.experimental.pallas import tpu as pltpu
from jax.sharding import Mesh, PartitionSpec as P

PANEL = 1024
BLOCK = 128
STRIP = 32
F32 = jnp.float32
BF16 = jnp.bfloat16

exact = lax.Precision.HIGHEST
close = lax.Precision.HIGH


def split_three(values):
    high = values.astype(BF16)
    rest = values - high.astype(F32)
    middle = rest.astype(BF16)
    low = (rest - middle.astype(F32)).astype(BF16)
    return high, middle, low


def gram_strip(rows):
    high, middle, low = split_three(rows)
    left = jnp.concatenate([high, high, middle, high, middle, low], axis=0)
    right = jnp.concatenate([high, middle, high, low, middle, high], axis=0)
    return lax.dot_general(left, right, (((0,), (0,)), ((), ())), preferred_element_type=F32)


def inverse_root(pivot):
    guess = lax.rsqrt(pivot)
    return guess * (1.5 - 0.5 * pivot * guess * guess)


def eliminate_strip(rows, start):
    lanes = lax.broadcasted_iota(jnp.int32, (STRIP, BLOCK), 1)
    sublanes = lax.broadcasted_iota(jnp.int32, (STRIP, BLOCK), 0)
    columns = [
        jnp.broadcast_to(rows[:, start + j : start + j + 1], (STRIP, BLOCK)) for j in range(STRIP)
    ]
    inside = jnp.logical_and(lanes >= start, lanes < start + STRIP)
    rows = jnp.where(inside, jnp.where(lanes - start == sublanes, 1.0, 0.0), rows)
    for j in range(STRIP):
        scale = inverse_root(jnp.broadcast_to(columns[j][j : j + 1, :], (8, BLOCK)))
        factor = columns[j] * jnp.concatenate([scale] * (STRIP // 8), axis=0)
        for k in range(j + 1, STRIP):
            columns[k] = columns[k] - factor * jnp.broadcast_to(
                factor[k : k + 1, :], (STRIP, BLOCK)
            )
        solved = jnp.broadcast_to(rows[j : j + 1, :] * scale[0:1, :], (STRIP, BLOCK))
        rows = jnp.where(
            sublanes == j, solved, rows - jnp.where(sublanes > j, factor, 0.0) * solved
        )
    return rows


def eliminate_block(block):
    for start in range(0, BLOCK, STRIP):
        stop = start + STRIP
        rows = eliminate_strip(block[start:stop, :], start)
        block[start:stop, :] = rows
        if stop < BLOCK:
            change = gram_strip(rows)[stop:, :]
            lanes = lax.broadcasted_iota(jnp.int32, (BLOCK - stop, BLOCK), 1)
            inside = jnp.logical_and(lanes >= start, lanes < stop)
            block[stop:, :] = jnp.where(inside, 0.0, block[stop:, :]) - change


def inverse_factor_kernel(source, state, block, scaled):
    count = state.shape[0] // BLOCK
    if len(source.shape) == 2:
        state[...] = source[...]
    else:
        kept = source.shape[2]
        for i in range(count):
            for k in range(i, count):
                if k - i < kept:
                    part = source[k % 2, k // 2, k - i]
                else:
                    part = source[i % 2, i // 2, count + i - k].T
                state[i * BLOCK : (i + 1) * BLOCK, k * BLOCK : (k + 1) * BLOCK] = part
    row_ids = lax.broadcasted_iota(jnp.int32, (BLOCK, BLOCK), 0)
    col_ids = lax.broadcasted_iota(jnp.int32, (BLOCK, BLOCK), 1)

    def step(j, _):
        here = pl.ds(pl.multiple_of(j * BLOCK, BLOCK), BLOCK)
        block[...] = state[here, here]
        eliminate_block(block)
        inverse = jnp.where(col_ids <= row_ids, block[...], 0.0)
        state[here, here] = jnp.where(col_ids == row_ids, 1.0, 0.0).astype(F32)
        scaled[...] = jnp.dot(
            inverse, state[here, :], precision=exact, preferred_element_type=F32
        )
        state[here, :] = scaled[...]

        def update(i, _):
            there = pl.ds(pl.multiple_of(i * BLOCK, BLOCK), BLOCK)
            state[there, here] = jnp.zeros((BLOCK, BLOCK), F32)
            state[there, :] = state[there, :] - lax.dot_general(
                scaled[:, there],
                scaled[...],
                (((0,), (0,)), ((), ())),
                precision=exact,
                preferred_element_type=F32,
            )
            return 0

        lax.fori_loop(j + 1, count, update, 0)
        return 0

    lax.fori_loop(0, count, step, 0)

    def clear(i, _):
        here = pl.ds(pl.multiple_of(i * BLOCK, BLOCK), BLOCK)

        def clear_block(k, _):
            right = pl.ds(pl.multiple_of(k * BLOCK, BLOCK), BLOCK)
            state[here, right] = jnp.zeros((BLOCK, BLOCK), F32)
            return 0

        lax.fori_loop(i + 1, count, clear_block, 0)
        return 0

    lax.fori_loop(0, count, clear, 0)


def inverse_factor(source, order):
    whole = pl.BlockSpec(memory_space=pltpu.VMEM)
    return pl.pallas_call(
        inverse_factor_kernel,
        out_shape=jax.ShapeDtypeStruct((order, order), F32),
        in_specs=[whole],
        out_specs=whole,
        scratch_shapes=[pltpu.VMEM((BLOCK, BLOCK), F32), pltpu.VMEM((BLOCK, order), F32)],
        compiler_params=pltpu.CompilerParams(vmem_limit_bytes=32 * 1024 * 1024),
        cost_estimate=pl.CostEstimate(
            flops=60_000_000_000, bytes_accessed=8 * order * order, transcendentals=0
        ),
        name="inverse_factor",
    )(source)


def spread_kernel(slots, source, target):
    blocks = source.shape[0] // target.shape[1]
    for b in range(blocks):
        target[slots[b]] = source[pl.ds(b, target.shape[1], stride=blocks), :]


def spread_columns(slots, source, slot_total, blocks):
    rows = source.shape[0] // blocks
    tile = rows // 4
    return pl.pallas_call(
        spread_kernel,
        out_shape=jax.ShapeDtypeStruct((slot_total, rows, BLOCK), F32),
        grid_spec=pltpu.PrefetchScalarGridSpec(
            num_scalar_prefetch=1,
            grid=(4,),
            in_specs=[pl.BlockSpec((tile * blocks, BLOCK), lambda i, s: (i, 0))],
            out_specs=pl.BlockSpec((slot_total, tile, BLOCK), lambda i, s: (0, i, 0)),
        ),
        compiler_params=pltpu.CompilerParams(vmem_limit_bytes=32 * 1024 * 1024),
        cost_estimate=pl.CostEstimate(
            flops=0, bytes_accessed=4 * BLOCK * rows * (blocks + slot_total), transcendentals=0
        ),
        name="spread_columns",
    )(slots, source)


def copy_kernel(slots, source, target):
    target[...] = source[...]


def pick_blocks(slots, source):
    shape = (slots.shape[0],) + source.shape[1:]
    block = (1,) + source.shape[1:]
    return pl.pallas_call(
        copy_kernel,
        out_shape=jax.ShapeDtypeStruct(shape, F32),
        grid_spec=pltpu.PrefetchScalarGridSpec(
            num_scalar_prefetch=1,
            grid=(shape[0],),
            in_specs=[pl.BlockSpec(block, lambda i, s: (s[i], 0, 0))],
            out_specs=pl.BlockSpec(block, lambda i, s: (i, 0, 0)),
        ),
        cost_estimate=pl.CostEstimate(
            flops=0, bytes_accessed=8 * shape[0] * shape[1] * shape[2], transcendentals=0
        ),
        name="pick_blocks",
    )(slots, source)


def place_kernel(slots, there, dests, update, product, target):
    k = pl.program_id(0)
    for b in range(update.shape[1] // BLOCK):
        rows = slice(b * BLOCK, (b + 1) * BLOCK)
        change = update[0, rows, :] - product[rows, :]
        target[dests[b], 0] = jnp.where(there[k] > 0, change, 0.0)


def place_updates(slots, there, dests, updates, product, groups):
    count, rows = slots.shape[0], updates.shape[1]
    return pl.pallas_call(
        place_kernel,
        out_shape=jax.ShapeDtypeStruct((groups, count, BLOCK, BLOCK), F32),
        grid_spec=pltpu.PrefetchScalarGridSpec(
            num_scalar_prefetch=3,
            grid=(count,),
            in_specs=[
                pl.BlockSpec((1, rows, BLOCK), lambda k, s, t, d: (s[k], 0, 0)),
                pl.BlockSpec((rows, BLOCK), lambda k, s, t, d: (0, k)),
            ],
            out_specs=pl.BlockSpec(
                (groups, 1, BLOCK, BLOCK), lambda k, s, t, d: (0, k, 0, 0)
            ),
        ),
        cost_estimate=pl.CostEstimate(
            flops=0,
            bytes_accessed=4 * BLOCK * count * (2 * rows + groups * BLOCK),
            transcendentals=0,
        ),
        name="place_updates",
    )(slots, there, dests, updates, product)


def finish_kernel(slots, there, top, root, panel, first, second, product, target):
    i = pl.program_id(0)
    columns = first.shape[1] + 1
    target[pl.ds(0, BLOCK, stride=columns), :] = panel[...]
    for k in range(1, columns):
        here = pl.ds(k, BLOCK, stride=columns)
        total = root[here, :]
        total = total + jnp.where(there[0, i] > 0, first[0, k - 1], 0.0)
        total = total + jnp.where(there[1, i] > 0, second[0, k - 1], 0.0)
        total = total - product[:, (k - 1) * BLOCK : k * BLOCK]
        target[here, :] = jnp.where(top[i] > 0, 0.0, total)


def finish(slots, there, top, root, panel, received, product):
    columns = received.shape[1] + 1
    root_rows = slots.shape[1]
    rows = BLOCK * columns
    block = (1,) + received.shape[1:]
    return pl.pallas_call(
        finish_kernel,
        out_shape=jax.ShapeDtypeStruct(root.shape, F32),
        grid_spec=pltpu.PrefetchScalarGridSpec(
            num_scalar_prefetch=3,
            grid=(root_rows,),
            in_specs=[
                pl.BlockSpec((rows, BLOCK), lambda i, s, t, p: (i, 0)),
                pl.BlockSpec((BLOCK, BLOCK), lambda i, s, t, p: (i, 0)),
                pl.BlockSpec(block, lambda i, s, t, p: (s[0, i], 0, 0, 0)),
                pl.BlockSpec(block, lambda i, s, t, p: (s[1, i], 0, 0, 0)),
                pl.BlockSpec((BLOCK, product.shape[1]), lambda i, s, t, p: (i, 0)),
            ],
            out_specs=pl.BlockSpec((rows, BLOCK), lambda i, s, t, p: (i, 0)),
        ),
        cost_estimate=pl.CostEstimate(
            flops=0, bytes_accessed=4 * BLOCK * 5 * rows * root_rows, transcendentals=0
        ),
        name="finish",
    )(slots, there, top, root, panel, received, received, product)


def ranks(targets, keys):
    same = targets[..., :, None] == targets[..., None, :]
    before = keys[..., None, :] < keys[..., :, None]
    return jnp.sum(jnp.logical_and(same, before).astype(jnp.int32), axis=-1)


def locate(matches, values):
    matches = matches.astype(jnp.int32)
    return (jnp.sum(matches * values, axis=-1), jnp.sum(matches, axis=-1) > 0)


def times_transposed(left, right, precision):
    return lax.dot_general(
        left, right, (((1,), (1,)), ((), ())), precision=precision, preferred_element_type=F32
    )


def exchange(values, axes):
    return lax.all_to_all(values, axes, split_axis=0, concat_axis=0, tiled=True)


def shift(values, axis, size, step):
    return lax.ppermute(values, axis, [(i, (i + step) % size) for i in range(size)])


def ring(values, axis, size):
    return [values] + [shift(values, axis, size, d) for d in range(1, size)]


def in_order(pieces, axis):
    size = len(pieces)
    return jnp.take(
        jnp.stack(pieces), (lax.axis_index(axis) - jnp.arange(size, dtype=jnp.int32)) % size, axis=0
    )


def after(values, *earlier):
    return lax.optimization_barrier((values,) + earlier)[0]


def per_device(child_pivot, child_border, child_update, index_map, root_front):
    row, col = ("x", "z_hi"), ("y", "core")
    joined = ("half",) + row
    n_rows = lax.axis_size("x") * lax.axis_size("z_hi")
    n_y, n_core = lax.axis_size("y"), lax.axis_size("core")
    n_cols = n_y * n_core
    groups = 2 * n_rows
    sibling = lax.axis_index("half")
    row_index = lax.axis_index(row)
    col_index = lax.axis_index(col)
    group = sibling * n_rows + row_index
    block_count = child_border.shape[1]
    pivots = child_border.shape[4]
    local_rows = block_count * BLOCK
    root_rows = root_front.shape[0]
    root_cols = root_front.shape[3]
    numbers = jnp.arange(block_count, dtype=jnp.int32)

    child_map = lax.dynamic_index_in_dim(index_map, sibling, 0, keepdims=False).reshape(
        block_count, n_rows
    )
    by_class = child_map.T
    class_dest = by_class % n_cols
    class_rank = ranks(
        class_dest, jnp.where(by_class < n_cols, 0, block_count) + numbers[None, :]
    )
    col_dest = lax.dynamic_index_in_dim(class_dest, col_index, 0, keepdims=False)
    col_rank = lax.dynamic_index_in_dim(class_rank, col_index, 0, keepdims=False)
    row_map = lax.dynamic_index_in_dim(by_class, row_index, 0, keepdims=False)
    row_dest = lax.dynamic_index_in_dim(class_dest, row_index, 0, keepdims=False)
    row_rank = lax.dynamic_index_in_dim(class_rank, row_index, 0, keepdims=False)

    border = child_border.reshape(block_count, BLOCK, pivots)

    wanted, _ = locate(
        jnp.logical_and(
            row_dest[None, :] == col_index,
            row_rank[None, :] == jnp.arange(2, dtype=jnp.int32)[:, None],
        ),
        numbers,
    )
    borders = lax.all_gather(pick_blocks(wanted, border), row, axis=0, tiled=True)
    updates = exchange(
        spread_columns(
            col_dest * 2 + col_rank,
            child_update.reshape(local_rows * block_count, BLOCK),
            2 * n_cols,
            block_count,
        ),
        col,
    )

    flat_source = numbers[:, None] * 2 + class_rank
    wanted_roots = jnp.arange(root_cols, dtype=jnp.int32) * n_cols + col_index
    source_slots, source_there = locate(
        by_class.reshape(1, -1) == wanted_roots[:, None], flat_source.reshape(-1)
    )

    inverse = inverse_factor(child_pivot[0], pivots)
    own_factor = times_transposed(border.reshape(local_rows, pivots), inverse, exact)

    root_view = root_front.reshape(root_rows, BLOCK, root_cols, BLOCK)
    panel_slot = source_slots[0]
    panel_border = lax.dynamic_index_in_dim(borders, panel_slot, 0, keepdims=False)
    panel_factor = times_transposed(panel_border, inverse, exact)
    panel_update = lax.dynamic_index_in_dim(
        updates, panel_slot, 0, keepdims=False
    ) - times_transposed(own_factor, panel_factor, close)
    panel_update = jnp.where(source_there[0], panel_update, 0.0).reshape(block_count, BLOCK, BLOCK)

    sent_blocks, _ = locate(
        (row_map % groups)[None, :] == jnp.arange(groups, dtype=jnp.int32)[:, None], numbers
    )
    every_map = index_map.reshape(2, 1, block_count * n_rows)
    my_roots = jnp.arange(root_rows, dtype=jnp.int32) * groups + group
    sender = (
        jnp.arange(2, dtype=jnp.int32)[:, None, None] * n_rows
        + (jnp.arange(block_count * n_rows, dtype=jnp.int32) % n_rows)[None, None, :]
    )
    got_slots, got_there = locate(every_map == my_roots[None, :, None], sender)

    def extend_add(base, received):
        shape = (-1,) + (1,) * (received.ndim - 1)
        for half in range(2):
            picked = jnp.take(received, got_slots[half], axis=0)
            base = base + jnp.where(got_there[half].reshape(shape), picked, 0.0)
        return base

    panel_got = exchange(jnp.take(panel_update, sent_blocks, axis=0), joined)
    own_panel = extend_add(root_view[:, :, 0, :], panel_got)

    n_x, n_z = lax.axis_size("x"), lax.axis_size("z_hi")
    corner = jnp.where(sibling == 0, own_panel[0], shift(own_panel[0], "half", 2, 1))
    corner = in_order(ring(corner, "z_hi", n_z), "z_hi")
    leading_column = in_order(ring(corner, "x", n_x), "x").reshape(n_rows, BLOCK, BLOCK)
    kept = n_cols // 2 + 1
    kept_rows = (col_index - jnp.arange(kept, dtype=jnp.int32)) % n_cols
    kept_blocks = jnp.take(leading_column, kept_rows, axis=0)
    leading = in_order(ring(kept_blocks, "y", n_y), "y")
    other_core = shift(leading, "core", 2, 1)
    is_first = lax.axis_index("core") == 0
    leading = jnp.stack(
        [jnp.where(is_first, leading, other_core), jnp.where(is_first, other_core, leading)]
    )

    panel_rows = lax.all_gather(after(own_panel, leading), col, axis=2, tiled=True)
    swaps = [(r * n_cols + c, c * n_rows + r) for r in range(n_rows) for c in range(n_cols)]
    swapped = lax.ppermute(after(own_panel, leading), row + col, swaps)
    by_z = in_order(ring(in_order(ring(swapped, "half", 2), "half"), "z_hi", n_z), "z_hi")
    column_panel = in_order(ring(by_z, "x", n_x), "x")
    column_panel = jnp.transpose(column_panel, (3, 2, 4, 0, 1, 5)).reshape(
        root_cols, BLOCK, PANEL
    )

    rest_factor = times_transposed(
        pick_blocks(source_slots[1:], borders).reshape(-1, pivots), inverse, exact
    )
    rest_sent = place_updates(
        source_slots[1:],
        source_there[1:].astype(jnp.int32),
        row_map % groups,
        updates,
        times_transposed(own_factor, rest_factor, close),
        groups,
    )
    rest_got = exchange(after(rest_sent, panel_got), joined)

    root_inverse = inverse_factor(leading, PANEL)
    factor_rows = times_transposed(panel_rows.reshape(root_rows * BLOCK, PANEL), root_inverse, exact)
    column_factor = times_transposed(
        column_panel[1:].reshape((root_cols - 1) * BLOCK, PANEL), root_inverse, exact
    )
    global_rows = (
        my_roots[:, None] * BLOCK + jnp.arange(BLOCK, dtype=jnp.int32)[None, :]
    ).reshape(-1)
    is_top = global_rows < PANEL
    above = jnp.logical_and(
        is_top[:, None], jnp.arange(PANEL, dtype=jnp.int32)[None, :] > global_rows[:, None]
    )
    factor_rows = jnp.where(above, 0.0, factor_rows)
    panel_part = lax.dynamic_index_in_dim(
        factor_rows.reshape(-1, n_cols, BLOCK), col_index, 1, keepdims=False
    )
    combined = finish(
        got_slots,
        got_there.astype(jnp.int32),
        (my_roots < n_cols).astype(jnp.int32),
        root_front.reshape(root_rows * BLOCK * root_cols, BLOCK),
        panel_part,
        rest_got,
        times_transposed(factor_rows, column_factor, close),
    )
    return (own_factor.reshape(child_border.shape), combined.reshape(root_front.shape))


def solution(mesh):
    fine = Mesh(mesh.devices.reshape(2, 4, 2, 4, 2), ("half", "x", "z_hi", "y", "core"))
    row, col = ("x", "z_hi"), ("y", "core")
    in_specs = (
        P("half", None, None),
        P("half", None, row, None, None),
        P("half", None, row, None, None, col, None),
        P(),
        P(None, ("half",) + row, None, None, col, None),
    )
    out_specs = (
        P("half", None, row, None, None),
        P(None, ("half",) + row, None, None, col, None),
    )
    return jax.shard_map(
        per_device, mesh=fine, in_specs=in_specs, out_specs=out_specs, check_vma=False
    )
```

```python
import functools

import jax
import jax.numpy as jnp
from jax import lax
from jax.experimental import pallas as pl
from jax.experimental.pallas import tpu as pltpu
from jax.sharding import Mesh, PartitionSpec as P

PANEL = 1024
BLOCK = 128
STRIP = 32
CHUNK = 256
F32 = jnp.float32
BF16 = jnp.bfloat16

exact = lax.Precision.HIGHEST
close = lax.Precision.HIGH


def split_three(values):
    high = values.astype(BF16)
    rest = values - high.astype(F32)
    middle = rest.astype(BF16)
    low = (rest - middle.astype(F32)).astype(BF16)
    return high, middle, low


def gram_strip(rows):
    high, middle, low = split_three(rows)
    left = jnp.concatenate([high, high, middle, high, middle, low], axis=0)
    right = jnp.concatenate([high, middle, high, low, middle, high], axis=0)
    return lax.dot_general(left, right, (((0,), (0,)), ((), ())), preferred_element_type=F32)


def inverse_root(pivot):
    guess = lax.rsqrt(pivot)
    return guess * (1.5 - 0.5 * pivot * guess * guess)


def eliminate_strip(rows, start):
    lanes = lax.broadcasted_iota(jnp.int32, (STRIP, BLOCK), 1)
    sublanes = lax.broadcasted_iota(jnp.int32, (STRIP, BLOCK), 0)
    columns = [
        jnp.broadcast_to(rows[:, start + j : start + j + 1], (STRIP, BLOCK)) for j in range(STRIP)
    ]
    inside = jnp.logical_and(lanes >= start, lanes < start + STRIP)
    rows = jnp.where(inside, jnp.where(lanes - start == sublanes, 1.0, 0.0), rows)
    for j in range(STRIP):
        scale = inverse_root(jnp.broadcast_to(columns[j][j : j + 1, :], (8, BLOCK)))
        factor = columns[j] * jnp.concatenate([scale] * (STRIP // 8), axis=0)
        for k in range(j + 1, STRIP):
            columns[k] = columns[k] - factor * jnp.broadcast_to(
                factor[k : k + 1, :], (STRIP, BLOCK)
            )
        solved = jnp.broadcast_to(rows[j : j + 1, :] * scale[0:1, :], (STRIP, BLOCK))
        rows = jnp.where(
            sublanes == j, solved, rows - jnp.where(sublanes > j, factor, 0.0) * solved
        )
    return rows


def eliminate_block(block):
    for start in range(0, BLOCK, STRIP):
        stop = start + STRIP
        rows = eliminate_strip(block[start:stop, :], start)
        block[start:stop, :] = rows
        if stop < BLOCK:
            change = gram_strip(rows)[stop:, :]
            lanes = lax.broadcasted_iota(jnp.int32, (BLOCK - stop, BLOCK), 1)
            inside = jnp.logical_and(lanes >= start, lanes < stop)
            block[stop:, :] = jnp.where(inside, 0.0, block[stop:, :]) - change


def inverse_factor_kernel(source, state, block, scaled):
    count = state.shape[0] // BLOCK
    if len(source.shape) == 2:
        state[...] = source[...]
    else:
        kept = source.shape[2]
        for i in range(count):
            for k in range(i, count):
                if k - i < kept:
                    part = source[k % 2, k // 2, k - i]
                else:
                    part = source[i % 2, i // 2, count + i - k].T
                state[i * BLOCK : (i + 1) * BLOCK, k * BLOCK : (k + 1) * BLOCK] = part
    row_ids = lax.broadcasted_iota(jnp.int32, (BLOCK, BLOCK), 0)
    col_ids = lax.broadcasted_iota(jnp.int32, (BLOCK, BLOCK), 1)

    def step(j, _):
        here = pl.ds(pl.multiple_of(j * BLOCK, BLOCK), BLOCK)
        block[...] = state[here, here]
        eliminate_block(block)
        inverse = jnp.where(col_ids <= row_ids, block[...], 0.0)
        state[here, here] = jnp.where(col_ids == row_ids, 1.0, 0.0).astype(F32)
        scaled[...] = jnp.dot(
            inverse, state[here, :], precision=exact, preferred_element_type=F32
        )
        state[here, :] = scaled[...]

        def update(i, _):
            there = pl.ds(pl.multiple_of(i * BLOCK, BLOCK), BLOCK)
            state[there, here] = jnp.zeros((BLOCK, BLOCK), F32)
            state[there, :] = state[there, :] - lax.dot_general(
                scaled[:, there],
                scaled[...],
                (((0,), (0,)), ((), ())),
                precision=exact,
                preferred_element_type=F32,
            )
            return 0

        lax.fori_loop(j + 1, count, update, 0)
        return 0

    lax.fori_loop(0, count, step, 0)

    def clear(i, _):
        here = pl.ds(pl.multiple_of(i * BLOCK, BLOCK), BLOCK)

        def clear_block(k, _):
            right = pl.ds(pl.multiple_of(k * BLOCK, BLOCK), BLOCK)
            state[here, right] = jnp.zeros((BLOCK, BLOCK), F32)
            return 0

        lax.fori_loop(i + 1, count, clear_block, 0)
        return 0

    lax.fori_loop(0, count, clear, 0)


def inverse_factor(source, order):
    whole = pl.BlockSpec(memory_space=pltpu.VMEM)
    return pl.pallas_call(
        inverse_factor_kernel,
        out_shape=jax.ShapeDtypeStruct((order, order), F32),
        in_specs=[whole],
        out_specs=whole,
        scratch_shapes=[pltpu.VMEM((BLOCK, BLOCK), F32), pltpu.VMEM((BLOCK, order), F32)],
        compiler_params=pltpu.CompilerParams(vmem_limit_bytes=32 * 1024 * 1024),
        cost_estimate=pl.CostEstimate(
            flops=60_000_000_000, bytes_accessed=8 * order * order, transcendentals=0
        ),
        name="inverse_factor",
    )(source)


def spread_kernel(slots, source, target):
    blocks = source.shape[0] // target.shape[1]
    for b in range(blocks):
        target[slots[b]] = source[pl.ds(b, target.shape[1], stride=blocks), :]


def spread_columns(slots, source, slot_total, blocks):
    rows = source.shape[0] // blocks
    tile = rows // 4
    return pl.pallas_call(
        spread_kernel,
        out_shape=jax.ShapeDtypeStruct((slot_total, rows, BLOCK), F32),
        grid_spec=pltpu.PrefetchScalarGridSpec(
            num_scalar_prefetch=1,
            grid=(4,),
            in_specs=[pl.BlockSpec((tile * blocks, BLOCK), lambda i, s: (i, 0))],
            out_specs=pl.BlockSpec((slot_total, tile, BLOCK), lambda i, s: (0, i, 0)),
        ),
        compiler_params=pltpu.CompilerParams(vmem_limit_bytes=32 * 1024 * 1024),
        cost_estimate=pl.CostEstimate(
            flops=0, bytes_accessed=4 * BLOCK * rows * (blocks + slot_total), transcendentals=0
        ),
        name="spread_columns",
    )(slots, source)


def copy_kernel(slots, source, target):
    target[...] = source[...]


def pick_blocks(slots, source):
    shape = (slots.shape[0],) + source.shape[1:]
    block = (1,) + source.shape[1:]
    return pl.pallas_call(
        copy_kernel,
        out_shape=jax.ShapeDtypeStruct(shape, F32),
        grid_spec=pltpu.PrefetchScalarGridSpec(
            num_scalar_prefetch=1,
            grid=(shape[0],),
            in_specs=[pl.BlockSpec(block, lambda i, s: (s[i], 0, 0))],
            out_specs=pl.BlockSpec(block, lambda i, s: (i, 0, 0)),
        ),
        cost_estimate=pl.CostEstimate(
            flops=0, bytes_accessed=8 * shape[0] * shape[1] * shape[2], transcendentals=0
        ),
        name="pick_blocks",
    )(slots, source)


def split_two(values):
    high = values.astype(BF16)
    return high, (values - high.astype(F32)).astype(BF16)


def solve_kernel(slots, first, second, inverse, target, high, middle, low):
    order = inverse.shape[0]

    @pl.when(pl.program_id(0) == 0)
    def _():
        for n in range(0, order, CHUNK):
            here = slice(n, n + CHUNK)
            high[here, :], middle[here, :], low[here, :] = split_three(inverse[here, :])

    def turned(block):
        if len(block.shape) == 3:
            return block[0].T
        parts = [block[z, 0, x, 0].T for x in range(block.shape[2]) for z in range(block.shape[0])]
        return jnp.concatenate(parts, axis=0)

    rows_high, rows_middle, rows_low = split_three(
        jnp.concatenate([turned(first), turned(second)], axis=1)
    )
    for n in range(0, order, CHUNK):
        here, depth = slice(n, n + CHUNK), n + CHUNK
        inverse_high, inverse_middle, inverse_low = (
            part[here, :depth] for part in (high, middle, low)
        )
        h, m, l = rows_high[:depth], rows_middle[:depth], rows_low[:depth]
        left = jnp.concatenate(
            [inverse_low, inverse_middle, inverse_high, inverse_middle, inverse_high, inverse_high],
            axis=1,
        )
        right = jnp.concatenate([h, m, l, h, m, h], axis=0)
        target[here, :] = jnp.dot(left, right, preferred_element_type=F32)


def solve_columns(slots, source, inverse):
    count, order = slots.shape[0], inverse.shape[0]
    if len(source.shape) == 3:
        block = (1, BLOCK, order)
        place = lambda slot: (slot, 0, 0)
    else:
        block = (source.shape[0], 1, source.shape[2], 1, BLOCK, BLOCK)
        place = lambda slot: (0, slot % 2, 0, slot // 2, 0, 0)
    return pl.pallas_call(
        solve_kernel,
        out_shape=jax.ShapeDtypeStruct((order, count * BLOCK), F32),
        grid_spec=pltpu.PrefetchScalarGridSpec(
            num_scalar_prefetch=1,
            grid=(count // 2,),
            in_specs=[
                pl.BlockSpec(block, lambda i, s: place(s[2 * i])),
                pl.BlockSpec(block, lambda i, s: place(s[2 * i + 1])),
                pl.BlockSpec((order, order), lambda i, s: (0, 0), pipeline_mode=pl.Buffered(1)),
            ],
            out_specs=pl.BlockSpec((order, 2 * BLOCK), lambda i, s: (0, i)),
            scratch_shapes=[pltpu.VMEM((order, order), BF16)] * 3,
        ),
        compiler_params=pltpu.CompilerParams(vmem_limit_bytes=40 * 1024 * 1024),
        cost_estimate=pl.CostEstimate(
            flops=16 * count * BLOCK * order * order,
            bytes_accessed=8 * count * BLOCK * order,
            transcendentals=0,
        ),
        name="solve_columns",
    )(slots, source, source, inverse)


def update_kernel(slots, there, dests, own, columns, first, second, target, stack):
    t = pl.program_id(0)
    order = own.shape[1]

    @pl.when(t == 0)
    def _():
        for n in range(0, own.shape[0], CHUNK):
            here = slice(n, n + CHUNK)
            high, low = split_two(own[here, :])
            stack[here, :order] = low
            stack[here, order : 2 * order] = high
            stack[here, 2 * order :] = high

    high, low = split_two(columns[...])
    product = jnp.dot(
        stack[...], jnp.concatenate([high, low, high], axis=0), preferred_element_type=F32
    )
    left = jnp.where(there[2 * t] > 0, first[0] - product[:, :BLOCK], 0.0)
    right = jnp.where(there[2 * t + 1] > 0, second[0] - product[:, BLOCK:], 0.0)
    for b in range(own.shape[0] // BLOCK):
        part = slice(b * BLOCK, (b + 1) * BLOCK)
        target[dests[b], 0] = left[part]
        target[dests[b], 1] = right[part]


def update_columns(slots, there, dests, own, columns, updates, groups, count):
    rows, order = own.shape
    return pl.pallas_call(
        update_kernel,
        out_shape=jax.ShapeDtypeStruct((groups, count, BLOCK, BLOCK), F32),
        grid_spec=pltpu.PrefetchScalarGridSpec(
            num_scalar_prefetch=3,
            grid=(slots.shape[0] // 2,),
            in_specs=[
                pl.BlockSpec(
                    (rows, order), lambda t, s, e, d: (0, 0), pipeline_mode=pl.Buffered(1)
                ),
                pl.BlockSpec((order, 2 * BLOCK), lambda t, s, e, d: (0, t)),
                pl.BlockSpec((1, rows, BLOCK), lambda t, s, e, d: (s[2 * t], 0, 0)),
                pl.BlockSpec((1, rows, BLOCK), lambda t, s, e, d: (s[2 * t + 1], 0, 0)),
            ],
            out_specs=pl.BlockSpec((groups, 2, BLOCK, BLOCK), lambda t, s, e, d: (0, t, 0, 0)),
            scratch_shapes=[pltpu.VMEM((rows, 3 * order), BF16)],
        ),
        compiler_params=pltpu.CompilerParams(vmem_limit_bytes=40 * 1024 * 1024),
        cost_estimate=pl.CostEstimate(
            flops=16 * count * BLOCK * rows * order,
            bytes_accessed=4 * count * BLOCK * (2 * rows + order + groups * BLOCK),
            transcendentals=0,
        ),
        name="update_columns",
    )(slots, there, dests, own, columns, updates, updates)


def finish_kernel(slots, there, top, root, panel, first, second, product, target):
    i = pl.program_id(0)
    columns = first.shape[1] + 1
    target[pl.ds(0, BLOCK, stride=columns), :] = panel[...]
    for k in range(1, columns):
        here = pl.ds(k, BLOCK, stride=columns)
        total = root[here, :]
        total = total + jnp.where(there[0, i] > 0, first[0, k - 1], 0.0)
        total = total + jnp.where(there[1, i] > 0, second[0, k - 1], 0.0)
        total = total - product[:, (k - 1) * BLOCK : k * BLOCK]
        target[here, :] = jnp.where(top[i] > 0, 0.0, total)


def finish(slots, there, top, root, panel, received, product):
    columns = received.shape[1] + 1
    root_rows = slots.shape[1]
    rows = BLOCK * columns
    block = (1,) + received.shape[1:]
    return pl.pallas_call(
        finish_kernel,
        out_shape=jax.ShapeDtypeStruct(root.shape, F32),
        grid_spec=pltpu.PrefetchScalarGridSpec(
            num_scalar_prefetch=3,
            grid=(root_rows,),
            in_specs=[
                pl.BlockSpec((rows, BLOCK), lambda i, s, t, p: (i, 0)),
                pl.BlockSpec((BLOCK, BLOCK), lambda i, s, t, p: (i, 0)),
                pl.BlockSpec(block, lambda i, s, t, p: (s[0, i], 0, 0, 0)),
                pl.BlockSpec(block, lambda i, s, t, p: (s[1, i], 0, 0, 0)),
                pl.BlockSpec((BLOCK, product.shape[1]), lambda i, s, t, p: (i, 0)),
            ],
            out_specs=pl.BlockSpec((rows, BLOCK), lambda i, s, t, p: (i, 0)),
        ),
        cost_estimate=pl.CostEstimate(
            flops=0, bytes_accessed=4 * BLOCK * 5 * rows * root_rows, transcendentals=0
        ),
        name="finish",
    )(slots, there, top, root, panel, received, received, product)


def ranks(targets, keys):
    same = targets[..., :, None] == targets[..., None, :]
    before = keys[..., None, :] < keys[..., :, None]
    return jnp.sum(jnp.logical_and(same, before).astype(jnp.int32), axis=-1)


def locate(matches, values):
    matches = matches.astype(jnp.int32)
    return (jnp.sum(matches * values, axis=-1), jnp.sum(matches, axis=-1) > 0)


def times_transposed(left, right, precision):
    return lax.dot_general(
        left, right, (((1,), (1,)), ((), ())), precision=precision, preferred_element_type=F32
    )


def exchange(values, axes):
    return lax.all_to_all(values, axes, split_axis=0, concat_axis=0, tiled=True)


def shift(values, axis, size, step):
    return lax.ppermute(values, axis, [(i, (i + step) % size) for i in range(size)])


def ring(values, axis, size):
    return [values] + [shift(values, axis, size, d) for d in range(1, size)]


def in_order(pieces, axis):
    size = len(pieces)
    return jnp.take(
        jnp.stack(pieces), (lax.axis_index(axis) - jnp.arange(size, dtype=jnp.int32)) % size, axis=0
    )


def after(values, *earlier):
    return lax.optimization_barrier((values,) + earlier)[0]


def per_device(child_pivot, child_border, child_update, index_map, root_front):
    row, col = ("x", "z_hi"), ("y", "core")
    joined = ("half",) + row
    n_rows = lax.axis_size("x") * lax.axis_size("z_hi")
    n_y, n_core = lax.axis_size("y"), lax.axis_size("core")
    n_cols = n_y * n_core
    groups = 2 * n_rows
    sibling = lax.axis_index("half")
    row_index = lax.axis_index(row)
    col_index = lax.axis_index(col)
    group = sibling * n_rows + row_index
    block_count = child_border.shape[1]
    pivots = child_border.shape[4]
    local_rows = block_count * BLOCK
    root_rows = root_front.shape[0]
    root_cols = root_front.shape[3]
    numbers = jnp.arange(block_count, dtype=jnp.int32)

    child_map = lax.dynamic_index_in_dim(index_map, sibling, 0, keepdims=False).reshape(
        block_count, n_rows
    )
    by_class = child_map.T
    class_dest = by_class % n_cols
    class_rank = ranks(
        class_dest, jnp.where(by_class < n_cols, 0, block_count) + numbers[None, :]
    )
    col_dest = lax.dynamic_index_in_dim(class_dest, col_index, 0, keepdims=False)
    col_rank = lax.dynamic_index_in_dim(class_rank, col_index, 0, keepdims=False)
    row_map = lax.dynamic_index_in_dim(by_class, row_index, 0, keepdims=False)
    row_dest = lax.dynamic_index_in_dim(class_dest, row_index, 0, keepdims=False)
    row_rank = lax.dynamic_index_in_dim(class_rank, row_index, 0, keepdims=False)

    border = child_border.reshape(block_count, BLOCK, pivots)

    wanted, _ = locate(
        jnp.logical_and(
            row_dest[None, :] == col_index,
            row_rank[None, :] == jnp.arange(2, dtype=jnp.int32)[:, None],
        ),
        numbers,
    )
    borders = lax.all_gather(pick_blocks(wanted, border), row, axis=0, tiled=True)
    updates = exchange(
        spread_columns(
            col_dest * 2 + col_rank,
            child_update.reshape(local_rows * block_count, BLOCK),
            2 * n_cols,
            block_count,
        ),
        col,
    )

    flat_source = numbers[:, None] * 2 + class_rank
    wanted_roots = jnp.arange(root_cols, dtype=jnp.int32) * n_cols + col_index
    source_slots, source_there = locate(
        by_class.reshape(1, -1) == wanted_roots[:, None], flat_source.reshape(-1)
    )

    inverse = inverse_factor(child_pivot[0], pivots)
    own_factor = times_transposed(border.reshape(local_rows, pivots), inverse, exact)

    root_view = root_front.reshape(root_rows, BLOCK, root_cols, BLOCK)
    panel_slot = source_slots[0]
    panel_border = lax.dynamic_index_in_dim(borders, panel_slot, 0, keepdims=False)
    panel_factor = times_transposed(panel_border, inverse, exact)
    panel_update = lax.dynamic_index_in_dim(
        updates, panel_slot, 0, keepdims=False
    ) - times_transposed(own_factor, panel_factor, close)
    panel_update = jnp.where(source_there[0], panel_update, 0.0).reshape(block_count, BLOCK, BLOCK)

    sent_blocks, _ = locate(
        (row_map % groups)[None, :] == jnp.arange(groups, dtype=jnp.int32)[:, None], numbers
    )
    every_map = index_map.reshape(2, 1, block_count * n_rows)
    my_roots = jnp.arange(root_rows, dtype=jnp.int32) * groups + group
    sender = (
        jnp.arange(2, dtype=jnp.int32)[:, None, None] * n_rows
        + (jnp.arange(block_count * n_rows, dtype=jnp.int32) % n_rows)[None, None, :]
    )
    got_slots, got_there = locate(every_map == my_roots[None, :, None], sender)

    def extend_add(base, received):
        shape = (-1,) + (1,) * (received.ndim - 1)
        for half in range(2):
            picked = jnp.take(received, got_slots[half], axis=0)
            base = base + jnp.where(got_there[half].reshape(shape), picked, 0.0)
        return base

    panel_got = exchange(jnp.take(panel_update, sent_blocks, axis=0), joined)

    def even(values):
        return jnp.concatenate([values[1:], values[-1:]])

    rest_slots = even(source_slots)
    rest_columns = solve_columns(rest_slots, after(borders, panel_update), inverse)
    own_panel = extend_add(root_view[:, :, 0, :], after(panel_got, rest_columns))
    rest_sent = update_columns(
        rest_slots,
        even(source_there.astype(jnp.int32)),
        row_map % groups,
        own_factor,
        rest_columns,
        updates,
        groups,
        root_cols - 1,
    )
    rest_got = exchange(after(rest_sent, own_panel), joined)

    n_x, n_z = lax.axis_size("x"), lax.axis_size("z_hi")
    corner = jnp.where(sibling == 0, own_panel[0], shift(own_panel[0], "half", 2, 1))
    corner = in_order(ring(after(corner, rest_sent), "z_hi", n_z), "z_hi")
    leading_column = in_order(ring(corner, "x", n_x), "x").reshape(n_rows, BLOCK, BLOCK)
    kept = n_cols // 2 + 1
    kept_rows = (col_index - jnp.arange(kept, dtype=jnp.int32)) % n_cols
    kept_blocks = jnp.take(leading_column, kept_rows, axis=0)
    leading = in_order(ring(kept_blocks, "y", n_y), "y")
    other_core = shift(leading, "core", 2, 1)
    is_first = lax.axis_index("core") == 0
    leading = jnp.stack(
        [jnp.where(is_first, leading, other_core), jnp.where(is_first, other_core, leading)]
    )

    swaps = [(r * n_cols + c, c * n_rows + r) for r in range(n_rows) for c in range(n_cols)]
    swapped = lax.ppermute(own_panel, row + col, swaps)
    column_panel = lax.all_gather(swapped, ("z_hi", "half", "x"), axis=0, tiled=False).reshape(
        n_z, 2, n_x, root_rows, BLOCK, BLOCK
    )
    panel_rows = lax.all_gather(own_panel, col, axis=2, tiled=True)

    root_inverse = inverse_factor(leading, PANEL)
    factor_rows = times_transposed(panel_rows.reshape(root_rows * BLOCK, PANEL), root_inverse, exact)
    column_factor = solve_columns(
        even(jnp.arange(root_cols, dtype=jnp.int32)), column_panel, root_inverse
    )[:, : (root_cols - 1) * BLOCK]
    global_rows = (
        my_roots[:, None] * BLOCK + jnp.arange(BLOCK, dtype=jnp.int32)[None, :]
    ).reshape(-1)
    is_top = global_rows < PANEL
    above = jnp.logical_and(
        is_top[:, None], jnp.arange(PANEL, dtype=jnp.int32)[None, :] > global_rows[:, None]
    )
    factor_rows = jnp.where(above, 0.0, factor_rows)
    panel_part = lax.dynamic_index_in_dim(
        factor_rows.reshape(-1, n_cols, BLOCK), col_index, 1, keepdims=False
    )
    combined = finish(
        got_slots,
        got_there.astype(jnp.int32),
        (my_roots < n_cols).astype(jnp.int32),
        root_front.reshape(root_rows * BLOCK * root_cols, BLOCK),
        panel_part,
        rest_got,
        jnp.dot(factor_rows, column_factor, precision=close, preferred_element_type=F32),
    )
    return (own_factor.reshape(child_border.shape), combined.reshape(root_front.shape))


def solution(mesh):
    fine = Mesh(mesh.devices.reshape(2, 4, 2, 4, 2), ("half", "x", "z_hi", "y", "core"))
    row, col = ("x", "z_hi"), ("y", "core")
    in_specs = (
        P("half", None, None),
        P("half", None, row, None, None),
        P("half", None, row, None, None, col, None),
        P(),
        P(None, ("half",) + row, None, None, col, None),
    )
    out_specs = (
        P("half", None, row, None, None),
        P(None, ("half",) + row, None, None, col, None),
    )
    return jax.shard_map(
        per_device, mesh=fine, in_specs=in_specs, out_specs=out_specs, check_vma=False
    )
```

```python
import functools

import jax
import jax.numpy as jnp
from jax import lax
from jax.experimental import pallas as pl
from jax.experimental.pallas import tpu as pltpu
from jax.sharding import Mesh, PartitionSpec as P

PANEL = 1024
BLOCK = 128
STRIP = 32
CHUNK = 256
F32 = jnp.float32
BF16 = jnp.bfloat16

exact = lax.Precision.HIGHEST
close = lax.Precision.HIGH


def split_three(values):
    high = values.astype(BF16)
    rest = values - high.astype(F32)
    middle = rest.astype(BF16)
    low = (rest - middle.astype(F32)).astype(BF16)
    return high, middle, low


def gram_strip(rows):
    high, middle, low = split_three(rows)
    left = jnp.concatenate([high, high, middle, high, middle, low], axis=0)
    right = jnp.concatenate([high, middle, high, low, middle, high], axis=0)
    return lax.dot_general(left, right, (((0,), (0,)), ((), ())), preferred_element_type=F32)


def inverse_root(pivot):
    guess = lax.rsqrt(pivot)
    return guess * (1.5 - 0.5 * pivot * guess * guess)


def eliminate_strip(rows, start):
    lanes = lax.broadcasted_iota(jnp.int32, (STRIP, BLOCK), 1)
    sublanes = lax.broadcasted_iota(jnp.int32, (STRIP, BLOCK), 0)
    columns = [
        jnp.broadcast_to(rows[:, start + j : start + j + 1], (STRIP, BLOCK)) for j in range(STRIP)
    ]
    inside = jnp.logical_and(lanes >= start, lanes < start + STRIP)
    rows = jnp.where(inside, jnp.where(lanes - start == sublanes, 1.0, 0.0), rows)
    for j in range(STRIP):
        scale = inverse_root(jnp.broadcast_to(columns[j][j : j + 1, :], (8, BLOCK)))
        factor = columns[j] * jnp.concatenate([scale] * (STRIP // 8), axis=0)
        for k in range(j + 1, STRIP):
            columns[k] = columns[k] - factor * jnp.broadcast_to(
                factor[k : k + 1, :], (STRIP, BLOCK)
            )
        solved = jnp.broadcast_to(rows[j : j + 1, :] * scale[0:1, :], (STRIP, BLOCK))
        rows = jnp.where(
            sublanes == j, solved, rows - jnp.where(sublanes > j, factor, 0.0) * solved
        )
    return rows


def eliminate_block(block):
    for start in range(0, BLOCK, STRIP):
        stop = start + STRIP
        rows = eliminate_strip(block[start:stop, :], start)
        block[start:stop, :] = rows
        if stop < BLOCK:
            change = gram_strip(rows)[stop:, :]
            lanes = lax.broadcasted_iota(jnp.int32, (BLOCK - stop, BLOCK), 1)
            inside = jnp.logical_and(lanes >= start, lanes < stop)
            block[stop:, :] = jnp.where(inside, 0.0, block[stop:, :]) - change


def inverse_factor_kernel(source, state, block, scaled):
    count = state.shape[0] // BLOCK
    if len(source.shape) == 2:
        state[...] = source[...]
    else:
        kept = source.shape[2]
        for i in range(count):
            for k in range(i, count):
                if k - i < kept:
                    part = source[k % 2, k // 2, k - i]
                else:
                    part = source[i % 2, i // 2, count + i - k].T
                state[i * BLOCK : (i + 1) * BLOCK, k * BLOCK : (k + 1) * BLOCK] = part
    row_ids = lax.broadcasted_iota(jnp.int32, (BLOCK, BLOCK), 0)
    col_ids = lax.broadcasted_iota(jnp.int32, (BLOCK, BLOCK), 1)

    def step(j, _):
        here = pl.ds(pl.multiple_of(j * BLOCK, BLOCK), BLOCK)
        block[...] = state[here, here]
        eliminate_block(block)
        inverse = jnp.where(col_ids <= row_ids, block[...], 0.0)
        state[here, here] = jnp.where(col_ids == row_ids, 1.0, 0.0).astype(F32)
        scaled[...] = jnp.dot(
            inverse, state[here, :], precision=exact, preferred_element_type=F32
        )
        state[here, :] = scaled[...]

        def update(i, _):
            there = pl.ds(pl.multiple_of(i * BLOCK, BLOCK), BLOCK)
            state[there, here] = jnp.zeros((BLOCK, BLOCK), F32)
            state[there, :] = state[there, :] - lax.dot_general(
                scaled[:, there],
                scaled[...],
                (((0,), (0,)), ((), ())),
                precision=exact,
                preferred_element_type=F32,
            )
            return 0

        lax.fori_loop(j + 1, count, update, 0)
        return 0

    lax.fori_loop(0, count, step, 0)

    def clear(i, _):
        here = pl.ds(pl.multiple_of(i * BLOCK, BLOCK), BLOCK)

        def clear_block(k, _):
            right = pl.ds(pl.multiple_of(k * BLOCK, BLOCK), BLOCK)
            state[here, right] = jnp.zeros((BLOCK, BLOCK), F32)
            return 0

        lax.fori_loop(i + 1, count, clear_block, 0)
        return 0

    lax.fori_loop(0, count, clear, 0)


def inverse_factor(source, order):
    whole = pl.BlockSpec(memory_space=pltpu.VMEM)
    return pl.pallas_call(
        inverse_factor_kernel,
        out_shape=jax.ShapeDtypeStruct((order, order), F32),
        in_specs=[whole],
        out_specs=whole,
        scratch_shapes=[pltpu.VMEM((BLOCK, BLOCK), F32), pltpu.VMEM((BLOCK, order), F32)],
        compiler_params=pltpu.CompilerParams(vmem_limit_bytes=32 * 1024 * 1024),
        cost_estimate=pl.CostEstimate(
            flops=60_000_000_000, bytes_accessed=8 * order * order, transcendentals=0
        ),
        name="inverse_factor",
    )(source)


def spread_kernel(slots, source, target):
    blocks = source.shape[0] // target.shape[1]
    for b in range(blocks):
        target[slots[b]] = source[pl.ds(b, target.shape[1], stride=blocks), :]


def spread_columns(slots, source, slot_total, blocks):
    rows = source.shape[0] // blocks
    tile = rows // 4
    return pl.pallas_call(
        spread_kernel,
        out_shape=jax.ShapeDtypeStruct((slot_total, rows, BLOCK), F32),
        grid_spec=pltpu.PrefetchScalarGridSpec(
            num_scalar_prefetch=1,
            grid=(4,),
            in_specs=[pl.BlockSpec((tile * blocks, BLOCK), lambda i, s: (i, 0))],
            out_specs=pl.BlockSpec((slot_total, tile, BLOCK), lambda i, s: (0, i, 0)),
        ),
        compiler_params=pltpu.CompilerParams(vmem_limit_bytes=32 * 1024 * 1024),
        cost_estimate=pl.CostEstimate(
            flops=0, bytes_accessed=4 * BLOCK * rows * (blocks + slot_total), transcendentals=0
        ),
        name="spread_columns",
    )(slots, source)


def copy_kernel(slots, source, target):
    target[...] = source[...]


def pick_blocks(slots, source):
    shape = (slots.shape[0],) + source.shape[1:]
    block = (1,) + source.shape[1:]
    return pl.pallas_call(
        copy_kernel,
        out_shape=jax.ShapeDtypeStruct(shape, F32),
        grid_spec=pltpu.PrefetchScalarGridSpec(
            num_scalar_prefetch=1,
            grid=(shape[0],),
            in_specs=[pl.BlockSpec(block, lambda i, s: (s[i], 0, 0))],
            out_specs=pl.BlockSpec(block, lambda i, s: (i, 0, 0)),
        ),
        cost_estimate=pl.CostEstimate(
            flops=0, bytes_accessed=8 * shape[0] * shape[1] * shape[2], transcendentals=0
        ),
        name="pick_blocks",
    )(slots, source)


def split_two(values):
    high = values.astype(BF16)
    return high, (values - high.astype(F32)).astype(BF16)


def solve_kernel(slots, first, second, inverse, target, high, middle, low):
    order = inverse.shape[0]

    @pl.when(pl.program_id(0) == 0)
    def _():
        for n in range(0, order, CHUNK):
            here = slice(n, n + CHUNK)
            high[here, :], middle[here, :], low[here, :] = split_three(inverse[here, :])

    def turned(block):
        if len(block.shape) == 3:
            return block[0].T
        parts = [block[z, 0, x, 0].T for x in range(block.shape[2]) for z in range(block.shape[0])]
        return jnp.concatenate(parts, axis=0)

    rows_high, rows_middle, rows_low = split_three(
        jnp.concatenate([turned(first), turned(second)], axis=1)
    )
    for n in range(0, order, CHUNK):
        here, depth = slice(n, n + CHUNK), n + CHUNK
        inverse_high, inverse_middle, inverse_low = (
            part[here, :depth] for part in (high, middle, low)
        )
        h, m, l = rows_high[:depth], rows_middle[:depth], rows_low[:depth]
        left = jnp.concatenate(
            [inverse_low, inverse_middle, inverse_high, inverse_middle, inverse_high, inverse_high],
            axis=1,
        )
        right = jnp.concatenate([h, m, l, h, m, h], axis=0)
        target[here, :] = jnp.dot(left, right, preferred_element_type=F32)


def solve_columns(slots, source, inverse):
    count, order = slots.shape[0], inverse.shape[0]
    if len(source.shape) == 3:
        block = (1, BLOCK, order)
        place = lambda slot: (slot, 0, 0)
    else:
        block = (source.shape[0], 1, source.shape[2], 1, BLOCK, BLOCK)
        place = lambda slot: (0, slot % 2, 0, slot // 2, 0, 0)
    return pl.pallas_call(
        solve_kernel,
        out_shape=jax.ShapeDtypeStruct((order, count * BLOCK), F32),
        grid_spec=pltpu.PrefetchScalarGridSpec(
            num_scalar_prefetch=1,
            grid=(count // 2,),
            in_specs=[
                pl.BlockSpec(block, lambda i, s: place(s[2 * i])),
                pl.BlockSpec(block, lambda i, s: place(s[2 * i + 1])),
                pl.BlockSpec((order, order), lambda i, s: (0, 0), pipeline_mode=pl.Buffered(1)),
            ],
            out_specs=pl.BlockSpec((order, 2 * BLOCK), lambda i, s: (0, i)),
            scratch_shapes=[pltpu.VMEM((order, order), BF16)] * 3,
        ),
        compiler_params=pltpu.CompilerParams(vmem_limit_bytes=40 * 1024 * 1024),
        cost_estimate=pl.CostEstimate(
            flops=16 * count * BLOCK * order * order,
            bytes_accessed=8 * count * BLOCK * order,
            transcendentals=0,
        ),
        name="solve_columns",
    )(slots, source, source, inverse)


def update_kernel(slots, there, dests, own, columns, first, second, target, stack):
    t = pl.program_id(0)
    order = own.shape[1]

    @pl.when(t == 0)
    def _():
        for n in range(0, own.shape[0], CHUNK):
            here = slice(n, n + CHUNK)
            high, low = split_two(own[here, :])
            stack[here, :order] = low
            stack[here, order : 2 * order] = high
            stack[here, 2 * order :] = high

    high, low = split_two(columns[...])
    product = jnp.dot(
        stack[...], jnp.concatenate([high, low, high], axis=0), preferred_element_type=F32
    )
    left = jnp.where(there[2 * t] > 0, first[0] - product[:, :BLOCK], 0.0)
    right = jnp.where(there[2 * t + 1] > 0, second[0] - product[:, BLOCK:], 0.0)
    for b in range(own.shape[0] // BLOCK):
        part = slice(b * BLOCK, (b + 1) * BLOCK)
        target[dests[b], 0] = left[part]
        target[dests[b], 1] = right[part]


def update_columns(slots, there, dests, own, columns, updates, groups, count):
    rows, order = own.shape
    return pl.pallas_call(
        update_kernel,
        out_shape=jax.ShapeDtypeStruct((groups, count, BLOCK, BLOCK), F32),
        grid_spec=pltpu.PrefetchScalarGridSpec(
            num_scalar_prefetch=3,
            grid=(slots.shape[0] // 2,),
            in_specs=[
                pl.BlockSpec(
                    (rows, order), lambda t, s, e, d: (0, 0), pipeline_mode=pl.Buffered(1)
                ),
                pl.BlockSpec((order, 2 * BLOCK), lambda t, s, e, d: (0, t)),
                pl.BlockSpec((1, rows, BLOCK), lambda t, s, e, d: (s[2 * t], 0, 0)),
                pl.BlockSpec((1, rows, BLOCK), lambda t, s, e, d: (s[2 * t + 1], 0, 0)),
            ],
            out_specs=pl.BlockSpec((groups, 2, BLOCK, BLOCK), lambda t, s, e, d: (0, t, 0, 0)),
            scratch_shapes=[pltpu.VMEM((rows, 3 * order), BF16)],
        ),
        compiler_params=pltpu.CompilerParams(vmem_limit_bytes=40 * 1024 * 1024),
        cost_estimate=pl.CostEstimate(
            flops=16 * count * BLOCK * rows * order,
            bytes_accessed=4 * count * BLOCK * (2 * rows + order + groups * BLOCK),
            transcendentals=0,
        ),
        name="update_columns",
    )(slots, there, dests, own, columns, updates, updates)


def finish_kernel(slots, there, top, root, panel, first, second, product, target):
    i = pl.program_id(0)
    columns = first.shape[1] + 1
    target[pl.ds(0, BLOCK, stride=columns), :] = panel[...]
    for k in range(1, columns):
        here = pl.ds(k, BLOCK, stride=columns)
        total = root[here, :]
        total = total + jnp.where(there[0, i] > 0, first[0, k - 1], 0.0)
        total = total + jnp.where(there[1, i] > 0, second[0, k - 1], 0.0)
        total = total - product[:, (k - 1) * BLOCK : k * BLOCK]
        target[here, :] = jnp.where(top[i] > 0, 0.0, total)


def finish(slots, there, top, root, panel, received, product):
    columns = received.shape[1] + 1
    root_rows = slots.shape[1]
    rows = BLOCK * columns
    block = (1,) + received.shape[1:]
    return pl.pallas_call(
        finish_kernel,
        out_shape=jax.ShapeDtypeStruct(root.shape, F32),
        grid_spec=pltpu.PrefetchScalarGridSpec(
            num_scalar_prefetch=3,
            grid=(root_rows,),
            in_specs=[
                pl.BlockSpec((rows, BLOCK), lambda i, s, t, p: (i, 0)),
                pl.BlockSpec((BLOCK, BLOCK), lambda i, s, t, p: (i, 0)),
                pl.BlockSpec(block, lambda i, s, t, p: (s[0, i], 0, 0, 0)),
                pl.BlockSpec(block, lambda i, s, t, p: (s[1, i], 0, 0, 0)),
                pl.BlockSpec((BLOCK, product.shape[1]), lambda i, s, t, p: (i, 0)),
            ],
            out_specs=pl.BlockSpec((rows, BLOCK), lambda i, s, t, p: (i, 0)),
        ),
        cost_estimate=pl.CostEstimate(
            flops=0, bytes_accessed=4 * BLOCK * 5 * rows * root_rows, transcendentals=0
        ),
        name="finish",
    )(slots, there, top, root, panel, received, received, product)


def ranks(targets, keys):
    same = targets[..., :, None] == targets[..., None, :]
    before = keys[..., None, :] < keys[..., :, None]
    return jnp.sum(jnp.logical_and(same, before).astype(jnp.int32), axis=-1)


def locate(matches, values):
    matches = matches.astype(jnp.int32)
    return (jnp.sum(matches * values, axis=-1), jnp.sum(matches, axis=-1) > 0)


def times_transposed(left, right, precision):
    return lax.dot_general(
        left, right, (((1,), (1,)), ((), ())), precision=precision, preferred_element_type=F32
    )


def exchange(values, axes):
    return lax.all_to_all(values, axes, split_axis=0, concat_axis=0, tiled=True)


def shift(values, axis, size, step):
    return lax.ppermute(values, axis, [(i, (i + step) % size) for i in range(size)])


def ring(values, axis, size):
    return [values] + [shift(values, axis, size, d) for d in range(1, size)]


def in_order(pieces, axis):
    size = len(pieces)
    return jnp.take(
        jnp.stack(pieces), (lax.axis_index(axis) - jnp.arange(size, dtype=jnp.int32)) % size, axis=0
    )


def after(values, *earlier):
    return lax.optimization_barrier((values,) + earlier)[0]


def per_device(child_pivot, child_border, child_update, index_map, root_front):
    row, col = ("x", "z_hi"), ("y", "core")
    joined = ("half",) + row
    n_rows = lax.axis_size("x") * lax.axis_size("z_hi")
    n_y, n_core = lax.axis_size("y"), lax.axis_size("core")
    n_cols = n_y * n_core
    groups = 2 * n_rows
    sibling = lax.axis_index("half")
    row_index = lax.axis_index(row)
    col_index = lax.axis_index(col)
    group = sibling * n_rows + row_index
    block_count = child_border.shape[1]
    pivots = child_border.shape[4]
    local_rows = block_count * BLOCK
    root_rows = root_front.shape[0]
    root_cols = root_front.shape[3]
    numbers = jnp.arange(block_count, dtype=jnp.int32)

    child_map = lax.dynamic_index_in_dim(index_map, sibling, 0, keepdims=False).reshape(
        block_count, n_rows
    )
    by_class = child_map.T
    class_dest = by_class % n_cols
    class_rank = ranks(
        class_dest, jnp.where(by_class < n_cols, 0, block_count) + numbers[None, :]
    )
    col_dest = lax.dynamic_index_in_dim(class_dest, col_index, 0, keepdims=False)
    col_rank = lax.dynamic_index_in_dim(class_rank, col_index, 0, keepdims=False)
    row_map = lax.dynamic_index_in_dim(by_class, row_index, 0, keepdims=False)
    row_dest = lax.dynamic_index_in_dim(class_dest, row_index, 0, keepdims=False)
    row_rank = lax.dynamic_index_in_dim(class_rank, row_index, 0, keepdims=False)

    border = child_border.reshape(block_count, BLOCK, pivots)

    wanted, _ = locate(
        jnp.logical_and(
            row_dest[None, :] == col_index,
            row_rank[None, :] == jnp.arange(2, dtype=jnp.int32)[:, None],
        ),
        numbers,
    )
    updates = exchange(
        spread_columns(
            col_dest * 2 + col_rank,
            child_update.reshape(local_rows * block_count, BLOCK),
            2 * n_cols,
            block_count,
        ),
        col,
    )
    borders = lax.all_gather(pick_blocks(wanted, border), row, axis=0, tiled=True)

    flat_source = numbers[:, None] * 2 + class_rank
    wanted_roots = jnp.arange(root_cols, dtype=jnp.int32) * n_cols + col_index
    source_slots, source_there = locate(
        by_class.reshape(1, -1) == wanted_roots[:, None], flat_source.reshape(-1)
    )

    inverse = inverse_factor(child_pivot[0], pivots)
    own_factor = times_transposed(border.reshape(local_rows, pivots), inverse, exact)

    root_view = root_front.reshape(root_rows, BLOCK, root_cols, BLOCK)
    panel_slot = source_slots[0]
    panel_border = lax.dynamic_index_in_dim(borders, panel_slot, 0, keepdims=False)
    panel_factor = times_transposed(panel_border, inverse, exact)
    panel_update = lax.dynamic_index_in_dim(
        updates, panel_slot, 0, keepdims=False
    ) - times_transposed(own_factor, panel_factor, close)
    panel_update = jnp.where(source_there[0], panel_update, 0.0).reshape(block_count, BLOCK, BLOCK)

    sent_blocks, _ = locate(
        (row_map % groups)[None, :] == jnp.arange(groups, dtype=jnp.int32)[:, None], numbers
    )
    every_map = index_map.reshape(2, 1, block_count * n_rows)
    my_roots = jnp.arange(root_rows, dtype=jnp.int32) * groups + group
    sender = (
        jnp.arange(2, dtype=jnp.int32)[:, None, None] * n_rows
        + (jnp.arange(block_count * n_rows, dtype=jnp.int32) % n_rows)[None, None, :]
    )
    got_slots, got_there = locate(every_map == my_roots[None, :, None], sender)

    def extend_add(base, received):
        shape = (-1,) + (1,) * (received.ndim - 1)
        for half in range(2):
            picked = jnp.take(received, got_slots[half], axis=0)
            base = base + jnp.where(got_there[half].reshape(shape), picked, 0.0)
        return base

    panel_got = exchange(jnp.take(panel_update, sent_blocks, axis=0), joined)

    def even(values):
        return jnp.concatenate([values[1:], values[-1:]])

    rest_slots = even(source_slots)
    rest_columns = solve_columns(rest_slots, after(borders, panel_update), inverse)
    own_panel = extend_add(root_view[:, :, 0, :], after(panel_got, rest_columns))

    n_x, n_z = lax.axis_size("x"), lax.axis_size("z_hi")
    swaps = [(r * n_cols + c, c * n_rows + r) for r in range(n_rows) for c in range(n_cols)]
    swapped = lax.ppermute(own_panel, row + col, swaps)
    column_panel = lax.all_gather(swapped, ("z_hi", "half", "x"), axis=0, tiled=False).reshape(
        n_z, 2, n_x, root_rows, BLOCK, BLOCK
    )

    corner = jnp.where(sibling == 0, own_panel[0], shift(own_panel[0], "half", 2, 1))
    corner = in_order(ring(after(corner, swapped), "z_hi", n_z), "z_hi")
    leading_column = in_order(ring(corner, "x", n_x), "x").reshape(n_rows, BLOCK, BLOCK)
    kept = n_cols // 2 + 1
    kept_rows = (col_index - jnp.arange(kept, dtype=jnp.int32)) % n_cols
    kept_blocks = jnp.take(leading_column, kept_rows, axis=0)
    leading = in_order(ring(kept_blocks, "y", n_y), "y")
    other_core = shift(leading, "core", 2, 1)
    is_first = lax.axis_index("core") == 0
    leading = jnp.stack(
        [jnp.where(is_first, leading, other_core), jnp.where(is_first, other_core, leading)]
    )

    rest_sent = update_columns(
        rest_slots,
        even(source_there.astype(jnp.int32)),
        row_map % groups,
        own_factor,
        after(rest_columns, leading_column),
        updates,
        groups,
        root_cols - 1,
    )
    column_panel, rest_sent, leading, panel_sent = lax.optimization_barrier(
        (column_panel, rest_sent, leading, own_panel)
    )
    rest_got = exchange(rest_sent, joined)
    panel_rows = lax.all_gather(panel_sent, col, axis=2, tiled=True)

    root_inverse = inverse_factor(leading, PANEL)
    factor_rows = times_transposed(panel_rows.reshape(root_rows * BLOCK, PANEL), root_inverse, exact)
    column_factor = solve_columns(
        even(jnp.arange(root_cols, dtype=jnp.int32)), column_panel, root_inverse
    )[:, : (root_cols - 1) * BLOCK]
    global_rows = (
        my_roots[:, None] * BLOCK + jnp.arange(BLOCK, dtype=jnp.int32)[None, :]
    ).reshape(-1)
    is_top = global_rows < PANEL
    above = jnp.logical_and(
        is_top[:, None], jnp.arange(PANEL, dtype=jnp.int32)[None, :] > global_rows[:, None]
    )
    factor_rows = jnp.where(above, 0.0, factor_rows)
    panel_part = lax.dynamic_index_in_dim(
        factor_rows.reshape(-1, n_cols, BLOCK), col_index, 1, keepdims=False
    )
    combined = finish(
        got_slots,
        got_there.astype(jnp.int32),
        (my_roots < n_cols).astype(jnp.int32),
        root_front.reshape(root_rows * BLOCK * root_cols, BLOCK),
        panel_part,
        rest_got,
        jnp.dot(factor_rows, column_factor, precision=close, preferred_element_type=F32),
    )
    return (own_factor.reshape(child_border.shape), combined.reshape(root_front.shape))


def solution(mesh):
    fine = Mesh(mesh.devices.reshape(2, 4, 2, 4, 2), ("half", "x", "z_hi", "y", "core"))
    row, col = ("x", "z_hi"), ("y", "core")
    in_specs = (
        P("half", None, None),
        P("half", None, row, None, None),
        P("half", None, row, None, None, col, None),
        P(),
        P(None, ("half",) + row, None, None, col, None),
    )
    out_specs = (
        P("half", None, row, None, None),
        P(None, ("half",) + row, None, None, col, None),
    )
    return jax.shard_map(
        per_device, mesh=fine, in_specs=in_specs, out_specs=out_specs, check_vma=False
    )
```

```python
import functools

import jax
import jax.numpy as jnp
from jax import lax
from jax.experimental import pallas as pl
from jax.experimental.pallas import tpu as pltpu
from jax.sharding import Mesh, PartitionSpec as P

PANEL = 1024
BLOCK = 128
STRIP = 32
CHUNK = 256
F32 = jnp.float32
BF16 = jnp.bfloat16

exact = lax.Precision.HIGHEST
close = lax.Precision.HIGH


def split_three(values):
    high = values.astype(BF16)
    rest = values - high.astype(F32)
    middle = rest.astype(BF16)
    low = (rest - middle.astype(F32)).astype(BF16)
    return high, middle, low


def gram_strip(rows):
    high, middle, low = split_three(rows)
    left = jnp.concatenate([high, high, middle, high, middle, low], axis=0)
    right = jnp.concatenate([high, middle, high, low, middle, high], axis=0)
    return lax.dot_general(left, right, (((0,), (0,)), ((), ())), preferred_element_type=F32)


def inverse_root(pivot):
    guess = lax.rsqrt(pivot)
    return guess * (1.5 - 0.5 * pivot * guess * guess)


def eliminate_strip(rows, start):
    lanes = lax.broadcasted_iota(jnp.int32, (STRIP, BLOCK), 1)
    sublanes = lax.broadcasted_iota(jnp.int32, (STRIP, BLOCK), 0)
    columns = [
        jnp.broadcast_to(rows[:, start + j : start + j + 1], (STRIP, BLOCK)) for j in range(STRIP)
    ]
    inside = jnp.logical_and(lanes >= start, lanes < start + STRIP)
    rows = jnp.where(inside, jnp.where(lanes - start == sublanes, 1.0, 0.0), rows)
    for j in range(STRIP):
        scale = inverse_root(jnp.broadcast_to(columns[j][j : j + 1, :], (8, BLOCK)))
        factor = columns[j] * jnp.concatenate([scale] * (STRIP // 8), axis=0)
        for k in range(j + 1, STRIP):
            columns[k] = columns[k] - factor * jnp.broadcast_to(
                factor[k : k + 1, :], (STRIP, BLOCK)
            )
        solved = jnp.broadcast_to(rows[j : j + 1, :] * scale[0:1, :], (STRIP, BLOCK))
        rows = jnp.where(
            sublanes == j, solved, rows - jnp.where(sublanes > j, factor, 0.0) * solved
        )
    return rows


def eliminate_block(block):
    for start in range(0, BLOCK, STRIP):
        stop = start + STRIP
        rows = eliminate_strip(block[start:stop, :], start)
        block[start:stop, :] = rows
        if stop < BLOCK:
            change = gram_strip(rows)[stop:, :]
            lanes = lax.broadcasted_iota(jnp.int32, (BLOCK - stop, BLOCK), 1)
            inside = jnp.logical_and(lanes >= start, lanes < stop)
            block[stop:, :] = jnp.where(inside, 0.0, block[stop:, :]) - change


def inverse_factor_kernel(source, state, block, scaled):
    count = state.shape[0] // BLOCK
    if len(source.shape) == 2:
        state[...] = source[...]
    else:
        kept = source.shape[2]
        for i in range(count):
            for k in range(i, count):
                if k - i < kept:
                    part = source[k % 2, k // 2, k - i]
                else:
                    part = source[i % 2, i // 2, count + i - k].T
                state[i * BLOCK : (i + 1) * BLOCK, k * BLOCK : (k + 1) * BLOCK] = part
    row_ids = lax.broadcasted_iota(jnp.int32, (BLOCK, BLOCK), 0)
    col_ids = lax.broadcasted_iota(jnp.int32, (BLOCK, BLOCK), 1)

    def step(j, _):
        here = pl.ds(pl.multiple_of(j * BLOCK, BLOCK), BLOCK)
        block[...] = state[here, here]
        eliminate_block(block)
        inverse = jnp.where(col_ids <= row_ids, block[...], 0.0)
        state[here, here] = jnp.where(col_ids == row_ids, 1.0, 0.0).astype(F32)
        scaled[...] = jnp.dot(
            inverse, state[here, :], precision=exact, preferred_element_type=F32
        )
        state[here, :] = scaled[...]

        def update(i, _):
            there = pl.ds(pl.multiple_of(i * BLOCK, BLOCK), BLOCK)
            state[there, here] = jnp.zeros((BLOCK, BLOCK), F32)
            state[there, :] = state[there, :] - lax.dot_general(
                scaled[:, there],
                scaled[...],
                (((0,), (0,)), ((), ())),
                precision=exact,
                preferred_element_type=F32,
            )
            return 0

        lax.fori_loop(j + 1, count, update, 0)
        return 0

    lax.fori_loop(0, count, step, 0)

    def clear(i, _):
        here = pl.ds(pl.multiple_of(i * BLOCK, BLOCK), BLOCK)

        def clear_block(k, _):
            right = pl.ds(pl.multiple_of(k * BLOCK, BLOCK), BLOCK)
            state[here, right] = jnp.zeros((BLOCK, BLOCK), F32)
            return 0

        lax.fori_loop(i + 1, count, clear_block, 0)
        return 0

    lax.fori_loop(0, count, clear, 0)


def inverse_factor(source, order):
    whole = pl.BlockSpec(memory_space=pltpu.VMEM)
    return pl.pallas_call(
        inverse_factor_kernel,
        out_shape=jax.ShapeDtypeStruct((order, order), F32),
        in_specs=[whole],
        out_specs=whole,
        scratch_shapes=[pltpu.VMEM((BLOCK, BLOCK), F32), pltpu.VMEM((BLOCK, order), F32)],
        compiler_params=pltpu.CompilerParams(vmem_limit_bytes=32 * 1024 * 1024),
        cost_estimate=pl.CostEstimate(
            flops=60_000_000_000, bytes_accessed=8 * order * order, transcendentals=0
        ),
        name="inverse_factor",
    )(source)


def spread_kernel(slots, source, target):
    blocks = source.shape[0] // target.shape[1]
    for b in range(blocks):
        target[slots[b]] = source[pl.ds(b, target.shape[1], stride=blocks), :]


def spread_columns(slots, source, slot_total, blocks):
    rows = source.shape[0] // blocks
    tile = rows // 4
    return pl.pallas_call(
        spread_kernel,
        out_shape=jax.ShapeDtypeStruct((slot_total, rows, BLOCK), F32),
        grid_spec=pltpu.PrefetchScalarGridSpec(
            num_scalar_prefetch=1,
            grid=(4,),
            in_specs=[pl.BlockSpec((tile * blocks, BLOCK), lambda i, s: (i, 0))],
            out_specs=pl.BlockSpec((slot_total, tile, BLOCK), lambda i, s: (0, i, 0)),
        ),
        compiler_params=pltpu.CompilerParams(vmem_limit_bytes=32 * 1024 * 1024),
        cost_estimate=pl.CostEstimate(
            flops=0, bytes_accessed=4 * BLOCK * rows * (blocks + slot_total), transcendentals=0
        ),
        name="spread_columns",
    )(slots, source)


def copy_kernel(slots, source, target):
    target[...] = source[...]


def pick_blocks(slots, source):
    shape = (slots.shape[0],) + source.shape[1:]
    block = (1,) + source.shape[1:]
    return pl.pallas_call(
        copy_kernel,
        out_shape=jax.ShapeDtypeStruct(shape, F32),
        grid_spec=pltpu.PrefetchScalarGridSpec(
            num_scalar_prefetch=1,
            grid=(shape[0],),
            in_specs=[pl.BlockSpec(block, lambda i, s: (s[i], 0, 0))],
            out_specs=pl.BlockSpec(block, lambda i, s: (i, 0, 0)),
        ),
        cost_estimate=pl.CostEstimate(
            flops=0, bytes_accessed=8 * shape[0] * shape[1] * shape[2], transcendentals=0
        ),
        name="pick_blocks",
    )(slots, source)


def split_two(values):
    high = values.astype(BF16)
    return high, (values - high.astype(F32)).astype(BF16)


def solve_kernel(slots, first, second, inverse, target, high, middle, low):
    order = inverse.shape[0]

    @pl.when(pl.program_id(0) == 0)
    def _():
        for n in range(0, order, CHUNK):
            here = slice(n, n + CHUNK)
            high[here, :], middle[here, :], low[here, :] = split_three(inverse[here, :])

    def turned(block):
        if len(block.shape) == 3:
            return block[0].T
        parts = [block[z, 0, x, 0].T for x in range(block.shape[2]) for z in range(block.shape[0])]
        return jnp.concatenate(parts, axis=0)

    rows_high, rows_middle, rows_low = split_three(
        jnp.concatenate([turned(first), turned(second)], axis=1)
    )
    for n in range(0, order, CHUNK):
        here, depth = slice(n, n + CHUNK), n + CHUNK
        inverse_high, inverse_middle, inverse_low = (
            part[here, :depth] for part in (high, middle, low)
        )
        h, m, l = rows_high[:depth], rows_middle[:depth], rows_low[:depth]
        left = jnp.concatenate(
            [inverse_low, inverse_middle, inverse_high, inverse_middle, inverse_high, inverse_high],
            axis=1,
        )
        right = jnp.concatenate([h, m, l, h, m, h], axis=0)
        target[here, :] = jnp.dot(left, right, preferred_element_type=F32)


def solve_columns(slots, source, inverse):
    count, order = slots.shape[0], inverse.shape[0]
    if len(source.shape) == 3:
        block = (1, BLOCK, order)
        place = lambda slot: (slot, 0, 0)
    else:
        block = (source.shape[0], 1, source.shape[2], 1, BLOCK, BLOCK)
        place = lambda slot: (0, slot % 2, 0, slot // 2, 0, 0)
    return pl.pallas_call(
        solve_kernel,
        out_shape=jax.ShapeDtypeStruct((order, count * BLOCK), F32),
        grid_spec=pltpu.PrefetchScalarGridSpec(
            num_scalar_prefetch=1,
            grid=(count // 2,),
            in_specs=[
                pl.BlockSpec(block, lambda i, s: place(s[2 * i])),
                pl.BlockSpec(block, lambda i, s: place(s[2 * i + 1])),
                pl.BlockSpec((order, order), lambda i, s: (0, 0), pipeline_mode=pl.Buffered(1)),
            ],
            out_specs=pl.BlockSpec((order, 2 * BLOCK), lambda i, s: (0, i)),
            scratch_shapes=[pltpu.VMEM((order, order), BF16)] * 3,
        ),
        compiler_params=pltpu.CompilerParams(vmem_limit_bytes=40 * 1024 * 1024),
        cost_estimate=pl.CostEstimate(
            flops=16 * count * BLOCK * order * order,
            bytes_accessed=8 * count * BLOCK * order,
            transcendentals=0,
        ),
        name="solve_columns",
    )(slots, source, source, inverse)


def update_kernel(slots, there, dests, own, columns, first, second, target, stack):
    t = pl.program_id(0)
    order = own.shape[1]

    @pl.when(t == 0)
    def _():
        for n in range(0, own.shape[0], CHUNK):
            here = slice(n, n + CHUNK)
            high, low = split_two(own[here, :])
            stack[here, :order] = low
            stack[here, order : 2 * order] = high
            stack[here, 2 * order :] = high

    high, low = split_two(columns[...])
    product = jnp.dot(
        stack[...], jnp.concatenate([high, low, high], axis=0), preferred_element_type=F32
    )
    left = jnp.where(there[2 * t] > 0, first[0] - product[:, :BLOCK], 0.0)
    right = jnp.where(there[2 * t + 1] > 0, second[0] - product[:, BLOCK:], 0.0)
    for b in range(own.shape[0] // BLOCK):
        part = slice(b * BLOCK, (b + 1) * BLOCK)
        target[dests[b], 0] = left[part]
        target[dests[b], 1] = right[part]


def update_columns(slots, there, dests, own, columns, updates, groups, count):
    rows, order = own.shape
    return pl.pallas_call(
        update_kernel,
        out_shape=jax.ShapeDtypeStruct((groups, count, BLOCK, BLOCK), F32),
        grid_spec=pltpu.PrefetchScalarGridSpec(
            num_scalar_prefetch=3,
            grid=(slots.shape[0] // 2,),
            in_specs=[
                pl.BlockSpec(
                    (rows, order), lambda t, s, e, d: (0, 0), pipeline_mode=pl.Buffered(1)
                ),
                pl.BlockSpec((order, 2 * BLOCK), lambda t, s, e, d: (0, t)),
                pl.BlockSpec((1, rows, BLOCK), lambda t, s, e, d: (s[2 * t], 0, 0)),
                pl.BlockSpec((1, rows, BLOCK), lambda t, s, e, d: (s[2 * t + 1], 0, 0)),
            ],
            out_specs=pl.BlockSpec((groups, 2, BLOCK, BLOCK), lambda t, s, e, d: (0, t, 0, 0)),
            scratch_shapes=[pltpu.VMEM((rows, 3 * order), BF16)],
        ),
        compiler_params=pltpu.CompilerParams(vmem_limit_bytes=40 * 1024 * 1024),
        cost_estimate=pl.CostEstimate(
            flops=16 * count * BLOCK * rows * order,
            bytes_accessed=4 * count * BLOCK * (2 * rows + order + groups * BLOCK),
            transcendentals=0,
        ),
        name="update_columns",
    )(slots, there, dests, own, columns, updates, updates)


def finish_kernel(slots, there, top, root, panel, first, second, product, target):
    i = pl.program_id(0)
    columns = first.shape[1] + 1
    target[pl.ds(0, BLOCK, stride=columns), :] = panel[...]
    for k in range(1, columns):
        here = pl.ds(k, BLOCK, stride=columns)
        total = root[here, :]
        total = total + jnp.where(there[0, i] > 0, first[0, k - 1], 0.0)
        total = total + jnp.where(there[1, i] > 0, second[0, k - 1], 0.0)
        total = total - product[:, (k - 1) * BLOCK : k * BLOCK]
        target[here, :] = jnp.where(top[i] > 0, 0.0, total)


def finish(slots, there, top, root, panel, received, product):
    columns = received.shape[1] + 1
    root_rows = slots.shape[1]
    rows = BLOCK * columns
    block = (1,) + received.shape[1:]
    return pl.pallas_call(
        finish_kernel,
        out_shape=jax.ShapeDtypeStruct(root.shape, F32),
        grid_spec=pltpu.PrefetchScalarGridSpec(
            num_scalar_prefetch=3,
            grid=(root_rows,),
            in_specs=[
                pl.BlockSpec((rows, BLOCK), lambda i, s, t, p: (i, 0)),
                pl.BlockSpec((BLOCK, BLOCK), lambda i, s, t, p: (i, 0)),
                pl.BlockSpec(block, lambda i, s, t, p: (s[0, i], 0, 0, 0)),
                pl.BlockSpec(block, lambda i, s, t, p: (s[1, i], 0, 0, 0)),
                pl.BlockSpec((BLOCK, product.shape[1]), lambda i, s, t, p: (i, 0)),
            ],
            out_specs=pl.BlockSpec((rows, BLOCK), lambda i, s, t, p: (i, 0)),
        ),
        cost_estimate=pl.CostEstimate(
            flops=0, bytes_accessed=4 * BLOCK * 5 * rows * root_rows, transcendentals=0
        ),
        name="finish",
    )(slots, there, top, root, panel, received, received, product)


def ranks(targets, keys):
    same = targets[..., :, None] == targets[..., None, :]
    before = keys[..., None, :] < keys[..., :, None]
    return jnp.sum(jnp.logical_and(same, before).astype(jnp.int32), axis=-1)


def locate(matches, values):
    matches = matches.astype(jnp.int32)
    return (jnp.sum(matches * values, axis=-1), jnp.sum(matches, axis=-1) > 0)


def times_transposed(left, right, precision):
    return lax.dot_general(
        left, right, (((1,), (1,)), ((), ())), precision=precision, preferred_element_type=F32
    )


def exchange(values, axes):
    return lax.all_to_all(values, axes, split_axis=0, concat_axis=0, tiled=True)


def shift(values, axis, size, step):
    return lax.ppermute(values, axis, [(i, (i + step) % size) for i in range(size)])


def ring(values, axis, size):
    return [values] + [shift(values, axis, size, d) for d in range(1, size)]


def in_order(pieces, axis):
    size = len(pieces)
    return jnp.take(
        jnp.stack(pieces), (lax.axis_index(axis) - jnp.arange(size, dtype=jnp.int32)) % size, axis=0
    )


def after(values, *earlier):
    return lax.optimization_barrier((values,) + earlier)[0]


def per_device(child_pivot, child_border, child_update, index_map, root_front):
    row, col = ("x", "z_hi"), ("y", "core")
    joined = ("z_hi", "half", "x")
    n_x, n_z = lax.axis_size("x"), lax.axis_size("z_hi")
    n_rows = n_x * n_z
    n_y, n_core = lax.axis_size("y"), lax.axis_size("core")
    n_cols = n_y * n_core
    groups = 2 * n_rows
    sibling = lax.axis_index("half")
    row_index = lax.axis_index(row)
    col_index = lax.axis_index(col)
    group = sibling * n_rows + row_index
    block_count = child_border.shape[1]
    pivots = child_border.shape[4]
    local_rows = block_count * BLOCK
    root_rows = root_front.shape[0]
    root_cols = root_front.shape[3]
    numbers = jnp.arange(block_count, dtype=jnp.int32)

    def place_of(groups_of):
        half, x, z = groups_of // n_rows, groups_of // n_z % n_x, groups_of % n_z
        return (z * 2 + half) * n_x + x

    child_map = lax.dynamic_index_in_dim(index_map, sibling, 0, keepdims=False).reshape(
        block_count, n_rows
    )
    by_class = child_map.T
    class_dest = by_class % n_cols
    class_rank = ranks(
        class_dest, jnp.where(by_class < n_cols, 0, block_count) + numbers[None, :]
    )
    col_dest = lax.dynamic_index_in_dim(class_dest, col_index, 0, keepdims=False)
    col_rank = lax.dynamic_index_in_dim(class_rank, col_index, 0, keepdims=False)
    row_map = lax.dynamic_index_in_dim(by_class, row_index, 0, keepdims=False)
    row_dest = lax.dynamic_index_in_dim(class_dest, row_index, 0, keepdims=False)
    row_rank = lax.dynamic_index_in_dim(class_rank, row_index, 0, keepdims=False)

    border = child_border.reshape(block_count, BLOCK, pivots)

    wanted, _ = locate(
        jnp.logical_and(
            row_dest[None, :] == col_index,
            row_rank[None, :] == jnp.arange(2, dtype=jnp.int32)[:, None],
        ),
        numbers,
    )
    updates = exchange(
        spread_columns(
            col_dest * 2 + col_rank,
            child_update.reshape(local_rows * block_count, BLOCK),
            2 * n_cols,
            block_count,
        ),
        col,
    )
    borders = lax.all_gather(pick_blocks(wanted, border), row, axis=0, tiled=True)

    flat_source = numbers[:, None] * 2 + class_rank
    wanted_roots = jnp.arange(root_cols, dtype=jnp.int32) * n_cols + col_index
    source_slots, source_there = locate(
        by_class.reshape(1, -1) == wanted_roots[:, None], flat_source.reshape(-1)
    )

    inverse = inverse_factor(child_pivot[0], pivots)
    own_factor = times_transposed(border.reshape(local_rows, pivots), inverse, exact)

    root_view = root_front.reshape(root_rows, BLOCK, root_cols, BLOCK)
    panel_slot = source_slots[0]
    panel_border = lax.dynamic_index_in_dim(borders, panel_slot, 0, keepdims=False)
    panel_factor = times_transposed(panel_border, inverse, exact)
    panel_update = lax.dynamic_index_in_dim(
        updates, panel_slot, 0, keepdims=False
    ) - times_transposed(own_factor, panel_factor, close)
    panel_update = jnp.where(source_there[0], panel_update, 0.0).reshape(block_count, BLOCK, BLOCK)

    sent_blocks, _ = locate(
        place_of(row_map % groups)[None, :] == jnp.arange(groups, dtype=jnp.int32)[:, None], numbers
    )
    every_map = index_map.reshape(2, 1, block_count * n_rows)
    my_roots = jnp.arange(root_rows, dtype=jnp.int32) * groups + group
    sender = place_of(
        jnp.arange(2, dtype=jnp.int32)[:, None, None] * n_rows
        + (jnp.arange(block_count * n_rows, dtype=jnp.int32) % n_rows)[None, None, :]
    )
    got_slots, got_there = locate(every_map == my_roots[None, :, None], sender)

    def extend_add(base, received):
        shape = (-1,) + (1,) * (received.ndim - 1)
        for half in range(2):
            picked = jnp.take(received, got_slots[half], axis=0)
            base = base + jnp.where(got_there[half].reshape(shape), picked, 0.0)
        return base

    panel_got = exchange(jnp.take(panel_update, sent_blocks, axis=0), joined)

    def even(values):
        return jnp.concatenate([values[1:], values[-1:]])

    rest_slots = even(source_slots)
    rest_columns = solve_columns(rest_slots, after(borders, panel_update), inverse)
    own_panel = extend_add(root_view[:, :, 0, :], after(panel_got, rest_columns))

    swaps = [(r * n_cols + c, c * n_rows + r) for r in range(n_rows) for c in range(n_cols)]
    swapped = lax.ppermute(own_panel, row + col, swaps)
    column_panel = lax.all_gather(swapped, ("z_hi", "half", "x"), axis=0, tiled=False).reshape(
        n_z, 2, n_x, root_rows, BLOCK, BLOCK
    )

    rest_sent = update_columns(
        rest_slots,
        even(source_there.astype(jnp.int32)),
        place_of(row_map % groups),
        own_factor,
        after(rest_columns, swapped),
        updates,
        groups,
        root_cols - 1,
    )

    corner = jnp.where(sibling == 0, own_panel[0], shift(own_panel[0], "half", 2, 1))
    corner = in_order(ring(after(corner, swapped), "z_hi", n_z), "z_hi")
    leading_column = in_order(ring(after(corner, rest_sent), "x", n_x), "x").reshape(n_rows, BLOCK, BLOCK)
    kept = n_cols // 2 + 1
    kept_rows = (col_index - jnp.arange(kept, dtype=jnp.int32)) % n_cols
    kept_blocks = jnp.take(leading_column, kept_rows, axis=0)
    leading = in_order(ring(kept_blocks, "y", n_y), "y")
    other_core = shift(leading, "core", 2, 1)
    is_first = lax.axis_index("core") == 0
    leading = jnp.stack(
        [jnp.where(is_first, leading, other_core), jnp.where(is_first, other_core, leading)]
    )

    column_panel, rest_sent, leading, panel_sent = lax.optimization_barrier(
        (column_panel, rest_sent, leading, own_panel)
    )
    rest_got = exchange(rest_sent, joined)
    panel_rows = lax.all_gather(panel_sent, col, axis=2, tiled=True)

    root_inverse = inverse_factor(leading, PANEL)
    factor_rows = times_transposed(panel_rows.reshape(root_rows * BLOCK, PANEL), root_inverse, exact)
    column_factor = solve_columns(
        even(jnp.arange(root_cols, dtype=jnp.int32)), column_panel, root_inverse
    )[:, : (root_cols - 1) * BLOCK]
    global_rows = (
        my_roots[:, None] * BLOCK + jnp.arange(BLOCK, dtype=jnp.int32)[None, :]
    ).reshape(-1)
    is_top = global_rows < PANEL
    above = jnp.logical_and(
        is_top[:, None], jnp.arange(PANEL, dtype=jnp.int32)[None, :] > global_rows[:, None]
    )
    factor_rows = jnp.where(above, 0.0, factor_rows)
    panel_part = lax.dynamic_index_in_dim(
        factor_rows.reshape(-1, n_cols, BLOCK), col_index, 1, keepdims=False
    )
    combined = finish(
        got_slots,
        got_there.astype(jnp.int32),
        (my_roots < n_cols).astype(jnp.int32),
        root_front.reshape(root_rows * BLOCK * root_cols, BLOCK),
        panel_part,
        rest_got,
        jnp.dot(factor_rows, column_factor, precision=close, preferred_element_type=F32),
    )
    return (own_factor.reshape(child_border.shape), combined.reshape(root_front.shape))


def solution(mesh):
    fine = Mesh(mesh.devices.reshape(2, 4, 2, 4, 2), ("half", "x", "z_hi", "y", "core"))
    row, col = ("x", "z_hi"), ("y", "core")
    in_specs = (
        P("half", None, None),
        P("half", None, row, None, None),
        P("half", None, row, None, None, col, None),
        P(),
        P(None, ("half",) + row, None, None, col, None),
    )
    out_specs = (
        P("half", None, row, None, None),
        P(None, ("half",) + row, None, None, col, None),
    )
    return jax.shard_map(
        per_device, mesh=fine, in_specs=in_specs, out_specs=out_specs, check_vma=False
    )
```

```python
import functools

import jax
import jax.numpy as jnp
from jax import lax
from jax.experimental import pallas as pl
from jax.experimental.pallas import tpu as pltpu
from jax.sharding import Mesh, PartitionSpec as P

PANEL = 1024
BLOCK = 128
STRIP = 32
CHUNK = 256
HALF = 64
F32 = jnp.float32
BF16 = jnp.bfloat16

exact = lax.Precision.HIGHEST
close = lax.Precision.HIGH


def split_three(values):
    high = values.astype(BF16)
    rest = values - high.astype(F32)
    middle = rest.astype(BF16)
    low = (rest - middle.astype(F32)).astype(BF16)
    return high, middle, low


def gram_strip(rows):
    high, middle, low = split_three(rows)
    left = jnp.concatenate([high, high, middle, high, middle, low], axis=0)
    right = jnp.concatenate([high, middle, high, low, middle, high], axis=0)
    return lax.dot_general(left, right, (((0,), (0,)), ((), ())), preferred_element_type=F32)


def inverse_root(pivot):
    guess = lax.rsqrt(pivot)
    return guess * (1.5 - 0.5 * pivot * guess * guess)


def eliminate_strip(rows, start):
    lanes = lax.broadcasted_iota(jnp.int32, (STRIP, BLOCK), 1)
    sublanes = lax.broadcasted_iota(jnp.int32, (STRIP, BLOCK), 0)
    columns = [
        jnp.broadcast_to(rows[:, start + j : start + j + 1], (STRIP, BLOCK)) for j in range(STRIP)
    ]
    inside = jnp.logical_and(lanes >= start, lanes < start + STRIP)
    rows = jnp.where(inside, jnp.where(lanes - start == sublanes, 1.0, 0.0), rows)
    for j in range(STRIP):
        scale = inverse_root(jnp.broadcast_to(columns[j][j : j + 1, :], (8, BLOCK)))
        factor = columns[j] * jnp.concatenate([scale] * (STRIP // 8), axis=0)
        for k in range(j + 1, STRIP):
            columns[k] = columns[k] - factor * jnp.broadcast_to(
                factor[k : k + 1, :], (STRIP, BLOCK)
            )
        solved = jnp.broadcast_to(rows[j : j + 1, :] * scale[0:1, :], (STRIP, BLOCK))
        rows = jnp.where(
            sublanes == j, solved, rows - jnp.where(sublanes > j, factor, 0.0) * solved
        )
    return rows


def eliminate_block(block):
    for start in range(0, BLOCK, STRIP):
        stop = start + STRIP
        rows = eliminate_strip(block[start:stop, :], start)
        block[start:stop, :] = rows
        if stop < BLOCK:
            change = gram_strip(rows)[stop:, :]
            lanes = lax.broadcasted_iota(jnp.int32, (BLOCK - stop, BLOCK), 1)
            inside = jnp.logical_and(lanes >= start, lanes < stop)
            block[stop:, :] = jnp.where(inside, 0.0, block[stop:, :]) - change


def inverse_factor_kernel(source, state, block, scaled):
    count = state.shape[0] // BLOCK
    if len(source.shape) == 2:
        state[...] = source[...]
    else:
        kept = source.shape[2]
        for i in range(count):
            for k in range(i, count):
                if k - i < kept:
                    part = source[k % 2, k // 2, k - i]
                else:
                    part = source[i % 2, i // 2, count + i - k].T
                state[i * BLOCK : (i + 1) * BLOCK, k * BLOCK : (k + 1) * BLOCK] = part
    row_ids = lax.broadcasted_iota(jnp.int32, (BLOCK, BLOCK), 0)
    col_ids = lax.broadcasted_iota(jnp.int32, (BLOCK, BLOCK), 1)

    def step(j, _):
        here = pl.ds(pl.multiple_of(j * BLOCK, BLOCK), BLOCK)
        block[...] = state[here, here]
        eliminate_block(block)
        inverse = jnp.where(col_ids <= row_ids, block[...], 0.0)
        state[here, here] = jnp.where(col_ids == row_ids, 1.0, 0.0).astype(F32)
        scaled[...] = jnp.dot(
            inverse, state[here, :], precision=exact, preferred_element_type=F32
        )
        state[here, :] = scaled[...]

        def update(i, _):
            there = pl.ds(pl.multiple_of(i * BLOCK, BLOCK), BLOCK)
            state[there, here] = jnp.zeros((BLOCK, BLOCK), F32)
            state[there, :] = state[there, :] - lax.dot_general(
                scaled[:, there],
                scaled[...],
                (((0,), (0,)), ((), ())),
                precision=exact,
                preferred_element_type=F32,
            )
            return 0

        lax.fori_loop(j + 1, count, update, 0)
        return 0

    lax.fori_loop(0, count, step, 0)

    def clear(i, _):
        here = pl.ds(pl.multiple_of(i * BLOCK, BLOCK), BLOCK)

        def clear_block(k, _):
            right = pl.ds(pl.multiple_of(k * BLOCK, BLOCK), BLOCK)
            state[here, right] = jnp.zeros((BLOCK, BLOCK), F32)
            return 0

        lax.fori_loop(i + 1, count, clear_block, 0)
        return 0

    lax.fori_loop(0, count, clear, 0)


def inverse_factor(source, order):
    whole = pl.BlockSpec(memory_space=pltpu.VMEM)
    return pl.pallas_call(
        inverse_factor_kernel,
        out_shape=jax.ShapeDtypeStruct((order, order), F32),
        in_specs=[whole],
        out_specs=whole,
        scratch_shapes=[pltpu.VMEM((BLOCK, BLOCK), F32), pltpu.VMEM((BLOCK, order), F32)],
        compiler_params=pltpu.CompilerParams(vmem_limit_bytes=32 * 1024 * 1024),
        cost_estimate=pl.CostEstimate(
            flops=60_000_000_000, bytes_accessed=8 * order * order, transcendentals=0
        ),
        name="inverse_factor",
    )(source)


def spread_kernel(slots, source, target):
    blocks = source.shape[0] // target.shape[1]
    for b in range(blocks):
        target[slots[b]] = source[pl.ds(b, target.shape[1], stride=blocks), :]


def spread_columns(slots, source, slot_total, blocks):
    rows = source.shape[0] // blocks
    tile = rows // 4
    return pl.pallas_call(
        spread_kernel,
        out_shape=jax.ShapeDtypeStruct((slot_total, rows, BLOCK), F32),
        grid_spec=pltpu.PrefetchScalarGridSpec(
            num_scalar_prefetch=1,
            grid=(4,),
            in_specs=[pl.BlockSpec((tile * blocks, BLOCK), lambda i, s: (i, 0))],
            out_specs=pl.BlockSpec((slot_total, tile, BLOCK), lambda i, s: (0, i, 0)),
        ),
        compiler_params=pltpu.CompilerParams(vmem_limit_bytes=32 * 1024 * 1024),
        cost_estimate=pl.CostEstimate(
            flops=0, bytes_accessed=4 * BLOCK * rows * (blocks + slot_total), transcendentals=0
        ),
        name="spread_columns",
    )(slots, source)


def copy_kernel(slots, source, target):
    target[...] = source[...]


def pick_blocks(slots, source):
    shape = (slots.shape[0],) + source.shape[1:]
    block = (1,) + source.shape[1:]
    return pl.pallas_call(
        copy_kernel,
        out_shape=jax.ShapeDtypeStruct(shape, F32),
        grid_spec=pltpu.PrefetchScalarGridSpec(
            num_scalar_prefetch=1,
            grid=(shape[0],),
            in_specs=[pl.BlockSpec(block, lambda i, s: (s[i], 0, 0))],
            out_specs=pl.BlockSpec(block, lambda i, s: (i, 0, 0)),
        ),
        cost_estimate=pl.CostEstimate(
            flops=0, bytes_accessed=8 * shape[0] * shape[1] * shape[2], transcendentals=0
        ),
        name="pick_blocks",
    )(slots, source)


def split_two(values):
    high = values.astype(BF16)
    return high, (values - high.astype(F32)).astype(BF16)


def solve_kernel(slots, first, second, inverse, target, high, middle, low):
    order = inverse.shape[0]

    @pl.when(pl.program_id(0) == 0)
    def _():
        for n in range(0, order, CHUNK):
            here = slice(n, n + CHUNK)
            high[here, :], middle[here, :], low[here, :] = split_three(inverse[here, :])

    def turned(block):
        if len(block.shape) == 3:
            return block[0].T
        parts = [block[z, 0, x, 0].T for x in range(block.shape[2]) for z in range(block.shape[0])]
        return jnp.concatenate(parts, axis=0)

    rows_high, rows_middle, rows_low = split_three(
        jnp.concatenate([turned(first), turned(second)], axis=1)
    )
    for n in range(0, order, CHUNK):
        here, depth = slice(n, n + CHUNK), n + CHUNK
        inverse_high, inverse_middle, inverse_low = (
            part[here, :depth] for part in (high, middle, low)
        )
        h, m, l = rows_high[:depth], rows_middle[:depth], rows_low[:depth]
        left = jnp.concatenate(
            [inverse_low, inverse_middle, inverse_high, inverse_middle, inverse_high, inverse_high],
            axis=1,
        )
        right = jnp.concatenate([h, m, l, h, m, h], axis=0)
        target[here, :] = jnp.dot(left, right, preferred_element_type=F32)


def solve_columns(slots, source, inverse):
    count, order = slots.shape[0], inverse.shape[0]
    if len(source.shape) == 3:
        block = (1, BLOCK, order)
        place = lambda slot: (slot, 0, 0)
    else:
        block = (source.shape[0], 1, source.shape[2], 1, BLOCK, BLOCK)
        place = lambda slot: (0, slot % 2, 0, slot // 2, 0, 0)
    return pl.pallas_call(
        solve_kernel,
        out_shape=jax.ShapeDtypeStruct((order, count * BLOCK), F32),
        grid_spec=pltpu.PrefetchScalarGridSpec(
            num_scalar_prefetch=1,
            grid=(count // 2,),
            in_specs=[
                pl.BlockSpec(block, lambda i, s: place(s[2 * i])),
                pl.BlockSpec(block, lambda i, s: place(s[2 * i + 1])),
                pl.BlockSpec((order, order), lambda i, s: (0, 0), pipeline_mode=pl.Buffered(1)),
            ],
            out_specs=pl.BlockSpec((order, 2 * BLOCK), lambda i, s: (0, i)),
            scratch_shapes=[pltpu.VMEM((order, order), BF16)] * 3,
        ),
        compiler_params=pltpu.CompilerParams(vmem_limit_bytes=40 * 1024 * 1024),
        cost_estimate=pl.CostEstimate(
            flops=16 * count * BLOCK * order * order,
            bytes_accessed=8 * count * BLOCK * order,
            transcendentals=0,
        ),
        name="solve_columns",
    )(slots, source, source, inverse)


def update_kernel(
    slots, there, dests, own, columns, first, second, upper, lower, stack
):
    t = pl.program_id(0)
    order = own.shape[1]

    @pl.when(t == 0)
    def _():
        for n in range(0, own.shape[0], CHUNK):
            here = slice(n, n + CHUNK)
            high, low = split_two(own[here, :])
            stack[here, :order] = low
            stack[here, order : 2 * order] = high
            stack[here, 2 * order :] = high

    high, low = split_two(columns[...])
    product = jnp.dot(
        stack[...], jnp.concatenate([high, low, high], axis=0), preferred_element_type=F32
    )
    left = jnp.where(there[2 * t] > 0, first[0] - product[:, :BLOCK], 0.0)
    right = jnp.where(there[2 * t + 1] > 0, second[0] - product[:, BLOCK:], 0.0)
    for b in range(own.shape[0] // BLOCK):
        for half, target in enumerate((upper, lower)):
            part = slice(b * BLOCK + half * HALF, b * BLOCK + (half + 1) * HALF)
            target[dests[half, b], 0] = left[part]
            target[dests[half, b], 1] = right[part]


def update_columns(slots, there, dests, own, columns, updates, groups, count):
    rows, order = own.shape
    out = jax.ShapeDtypeStruct((groups, count, HALF, BLOCK), F32)
    out_spec = pl.BlockSpec((groups, 2, HALF, BLOCK), lambda t, s, e, d: (0, t, 0, 0))
    return pl.pallas_call(
        update_kernel,
        out_shape=(out, out),
        grid_spec=pltpu.PrefetchScalarGridSpec(
            num_scalar_prefetch=3,
            grid=(slots.shape[0] // 2,),
            in_specs=[
                pl.BlockSpec(
                    (rows, order), lambda t, s, e, d: (0, 0), pipeline_mode=pl.Buffered(1)
                ),
                pl.BlockSpec((order, 2 * BLOCK), lambda t, s, e, d: (0, t)),
                pl.BlockSpec((1, rows, BLOCK), lambda t, s, e, d: (s[2 * t], 0, 0)),
                pl.BlockSpec((1, rows, BLOCK), lambda t, s, e, d: (s[2 * t + 1], 0, 0)),
            ],
            out_specs=(out_spec, out_spec),
            scratch_shapes=[pltpu.VMEM((rows, 3 * order), BF16)],
        ),
        compiler_params=pltpu.CompilerParams(vmem_limit_bytes=40 * 1024 * 1024),
        cost_estimate=pl.CostEstimate(
            flops=16 * count * BLOCK * rows * order,
            bytes_accessed=4 * count * BLOCK * (2 * rows + order + groups * BLOCK),
            transcendentals=0,
        ),
        name="update_columns",
    )(slots, there, dests, own, columns, updates, updates)


def finish_kernel(
    slots, there, top, root, panel, first_upper, second_upper, first_lower, second_lower, product, target
):
    i = pl.program_id(0)
    columns = first_upper.shape[1] + 1
    target[pl.ds(0, BLOCK, stride=columns), :] = panel[...]
    parts = ((first_upper, second_upper), (first_lower, second_lower))
    for half, (first, second) in enumerate(parts):
        rows = slice(half * HALF, (half + 1) * HALF)
        for k in range(1, columns):
            here = pl.ds(half * HALF * columns + k, HALF, stride=columns)
            total = root[here, :]
            total = total + jnp.where(there[0, i] > 0, first[0, k - 1], 0.0)
            total = total + jnp.where(there[1, i] > 0, second[0, k - 1], 0.0)
            total = total - product[rows, (k - 1) * BLOCK : k * BLOCK]
            target[here, :] = jnp.where(top[i] > 0, 0.0, total)


def finish(slots, there, top, root, panel, upper, lower, product):
    columns = upper.shape[1] + 1
    root_rows = there.shape[1]
    rows = BLOCK * columns
    block = (1,) + upper.shape[1:]

    def received(part, half):
        return pl.BlockSpec(block, lambda i, s, t, p: (s[part, half, i], 0, 0, 0))

    return pl.pallas_call(
        finish_kernel,
        out_shape=jax.ShapeDtypeStruct(root.shape, F32),
        grid_spec=pltpu.PrefetchScalarGridSpec(
            num_scalar_prefetch=3,
            grid=(root_rows,),
            in_specs=[
                pl.BlockSpec((rows, BLOCK), lambda i, s, t, p: (i, 0)),
                pl.BlockSpec((BLOCK, BLOCK), lambda i, s, t, p: (i, 0)),
                received(0, 0),
                received(0, 1),
                received(1, 0),
                received(1, 1),
                pl.BlockSpec((BLOCK, product.shape[1]), lambda i, s, t, p: (i, 0)),
            ],
            out_specs=pl.BlockSpec((rows, BLOCK), lambda i, s, t, p: (i, 0)),
        ),
        cost_estimate=pl.CostEstimate(
            flops=0, bytes_accessed=4 * BLOCK * 5 * rows * root_rows, transcendentals=0
        ),
        name="finish",
    )(slots, there, top, root, panel, upper, upper, lower, lower, product)


def ranks(targets, keys):
    same = targets[..., :, None] == targets[..., None, :]
    before = keys[..., None, :] < keys[..., :, None]
    return jnp.sum(jnp.logical_and(same, before).astype(jnp.int32), axis=-1)


def locate(matches, values):
    matches = matches.astype(jnp.int32)
    return (jnp.sum(matches * values, axis=-1), jnp.sum(matches, axis=-1) > 0)


def times_transposed(left, right, precision):
    return lax.dot_general(
        left, right, (((1,), (1,)), ((), ())), precision=precision, preferred_element_type=F32
    )


def exchange(values, axes):
    return lax.all_to_all(values, axes, split_axis=0, concat_axis=0, tiled=True)


def shift(values, axis, size, step):
    return lax.ppermute(values, axis, [(i, (i + step) % size) for i in range(size)])


def ring(values, axis, size):
    return [values] + [shift(values, axis, size, d) for d in range(1, size)]


def in_order(pieces, axis):
    size = len(pieces)
    return jnp.take(
        jnp.stack(pieces), (lax.axis_index(axis) - jnp.arange(size, dtype=jnp.int32)) % size, axis=0
    )


def after(values, *earlier):
    return lax.optimization_barrier((values,) + earlier)[0]


def per_device(child_pivot, child_border, child_update, index_map, root_front):
    row, col = ("x", "z_hi"), ("y", "core")
    joined = ("z_hi", "half", "x")
    n_x, n_z = lax.axis_size("x"), lax.axis_size("z_hi")
    n_rows = n_x * n_z
    n_y, n_core = lax.axis_size("y"), lax.axis_size("core")
    n_cols = n_y * n_core
    groups = 2 * n_rows
    sibling = lax.axis_index("half")
    row_index = lax.axis_index(row)
    col_index = lax.axis_index(col)
    group = sibling * n_rows + row_index
    block_count = child_border.shape[1]
    pivots = child_border.shape[4]
    local_rows = block_count * BLOCK
    root_rows = root_front.shape[0]
    root_cols = root_front.shape[3]
    numbers = jnp.arange(block_count, dtype=jnp.int32)

    def place_of(groups_of):
        half, x, z = groups_of // n_rows, groups_of // n_z % n_x, groups_of % n_z
        return (z * 2 + half) * n_x + x

    n_zs = 2 * n_z
    z_index = lax.axis_index("z_hi") * 2 + sibling

    def z_shift(values, step):
        spot = lambda z: z % 2 * n_z + z // 2
        pairs = [(spot(z), spot((z + step) % n_zs)) for z in range(n_zs)]
        return lax.ppermute(values, ("half", "z_hi"), pairs)

    child_map = lax.dynamic_index_in_dim(index_map, sibling, 0, keepdims=False).reshape(
        block_count, n_rows
    )
    by_class = child_map.T
    class_dest = by_class % n_cols
    class_rank = ranks(
        class_dest, jnp.where(by_class < n_cols, 0, block_count) + numbers[None, :]
    )
    col_dest = lax.dynamic_index_in_dim(class_dest, col_index, 0, keepdims=False)
    col_rank = lax.dynamic_index_in_dim(class_rank, col_index, 0, keepdims=False)
    row_map = lax.dynamic_index_in_dim(by_class, row_index, 0, keepdims=False)
    row_dest = lax.dynamic_index_in_dim(class_dest, row_index, 0, keepdims=False)
    row_rank = lax.dynamic_index_in_dim(class_rank, row_index, 0, keepdims=False)

    border = child_border.reshape(block_count, BLOCK, pivots)

    wanted, _ = locate(
        jnp.logical_and(
            row_dest[None, :] == col_index,
            row_rank[None, :] == jnp.arange(2, dtype=jnp.int32)[:, None],
        ),
        numbers,
    )
    updates = exchange(
        spread_columns(
            col_dest * 2 + col_rank,
            child_update.reshape(local_rows * block_count, BLOCK),
            2 * n_cols,
            block_count,
        ),
        col,
    )
    borders = lax.all_gather(pick_blocks(wanted, border), row, axis=0, tiled=True)

    flat_source = numbers[:, None] * 2 + class_rank
    wanted_roots = jnp.arange(root_cols, dtype=jnp.int32) * n_cols + col_index
    source_slots, source_there = locate(
        by_class.reshape(1, -1) == wanted_roots[:, None], flat_source.reshape(-1)
    )

    inverse = inverse_factor(child_pivot[0], pivots)
    own_factor = times_transposed(border.reshape(local_rows, pivots), inverse, exact)

    root_view = root_front.reshape(root_rows, BLOCK, root_cols, BLOCK)
    panel_slot = source_slots[0]
    panel_border = lax.dynamic_index_in_dim(borders, panel_slot, 0, keepdims=False)
    panel_factor = times_transposed(panel_border, inverse, exact)
    panel_update = lax.dynamic_index_in_dim(
        updates, panel_slot, 0, keepdims=False
    ) - times_transposed(own_factor, panel_factor, close)
    panel_update = jnp.where(source_there[0], panel_update, 0.0).reshape(block_count, BLOCK, BLOCK)

    sent_blocks, _ = locate(
        place_of(row_map % groups)[None, :] == jnp.arange(groups, dtype=jnp.int32)[:, None], numbers
    )
    every_map = index_map.reshape(2, 1, block_count * n_rows)
    my_roots = jnp.arange(root_rows, dtype=jnp.int32) * groups + group
    sender = place_of(
        jnp.arange(2, dtype=jnp.int32)[:, None, None] * n_rows
        + (jnp.arange(block_count * n_rows, dtype=jnp.int32) % n_rows)[None, None, :]
    )
    got_slots, got_there = locate(every_map == my_roots[None, :, None], sender)

    def extend_add(base, received):
        shape = (-1,) + (1,) * (received.ndim - 1)
        for half in range(2):
            picked = jnp.take(received, got_slots[half], axis=0)
            base = base + jnp.where(got_there[half].reshape(shape), picked, 0.0)
        return base

    panel_got = exchange(jnp.take(panel_update, sent_blocks, axis=0), joined)

    def even(values):
        return jnp.concatenate([values[1:], values[-1:]])

    rest_slots = even(source_slots)
    rest_columns = solve_columns(rest_slots, after(borders, panel_update), inverse)
    own_panel = extend_add(root_view[:, :, 0, :], after(panel_got, rest_columns))

    swaps = [(r * n_cols + c, c * n_rows + r) for r in range(n_rows) for c in range(n_cols)]
    swapped = lax.ppermute(own_panel, row + col, swaps)
    column_panel = lax.all_gather(swapped, ("z_hi", "half", "x"), axis=0, tiled=False).reshape(
        n_z, 2, n_x, root_rows, BLOCK, BLOCK
    )

    sent_place = place_of(row_map % groups)
    sent_z, sent_x = (sent_place // n_x - z_index) % n_zs, sent_place % n_x
    rest_sent = update_columns(
        rest_slots,
        even(source_there.astype(jnp.int32)),
        jnp.stack([sent_x * n_zs + sent_z, sent_z * n_x + sent_x]),
        own_factor,
        after(rest_columns, swapped),
        updates,
        groups,
        root_cols - 1,
    )

    corner = jnp.where(sibling == 0, own_panel[0], shift(own_panel[0], "half", 2, 1))
    corner = in_order(ring(after(corner, swapped), "z_hi", n_z), "z_hi")
    leading_column = in_order(ring(after(corner, rest_sent), "x", n_x), "x").reshape(n_rows, BLOCK, BLOCK)
    kept = n_cols // 2 + 1
    kept_rows = (col_index - jnp.arange(kept, dtype=jnp.int32)) % n_cols
    kept_blocks = jnp.take(leading_column, kept_rows, axis=0)
    leading = in_order(ring(kept_blocks, "y", n_y), "y")
    other_core = shift(leading, "core", 2, 1)
    is_first = lax.axis_index("core") == 0
    leading = jnp.stack(
        [jnp.where(is_first, leading, other_core), jnp.where(is_first, other_core, leading)]
    )

    column_panel, rest_sent, leading, panel_sent = lax.optimization_barrier(
        (column_panel, rest_sent, leading, own_panel)
    )
    upper = rest_sent[0].reshape((n_x, n_zs) + rest_sent[0].shape[1:])
    lower = rest_sent[1].reshape((n_zs, n_x) + rest_sent[1].shape[1:])
    upper = exchange(upper, "x")
    lower = [lower[0]] + [z_shift(lower[d], d) for d in range(1, n_zs)]
    panel_rows = lax.all_gather(panel_sent, col, axis=2, tiled=True)

    root_inverse = inverse_factor(leading, PANEL)
    upper, lower, root_inverse = lax.optimization_barrier(
        ([upper[:, d] for d in range(n_zs)], jnp.stack(lower, axis=1), root_inverse)
    )
    lower = exchange(lower, "x").reshape((groups,) + rest_sent[1].shape[1:])
    upper = [upper[0]] + [z_shift(upper[d], d) for d in range(1, n_zs)]
    upper = jnp.stack(upper).reshape((groups,) + rest_sent[0].shape[1:])
    got_z, got_x = (z_index - got_slots // n_x) % n_zs, got_slots % n_x

    factor_rows = times_transposed(panel_rows.reshape(root_rows * BLOCK, PANEL), root_inverse, exact)
    column_factor = solve_columns(
        even(jnp.arange(root_cols, dtype=jnp.int32)), column_panel, root_inverse
    )[:, : (root_cols - 1) * BLOCK]
    global_rows = (
        my_roots[:, None] * BLOCK + jnp.arange(BLOCK, dtype=jnp.int32)[None, :]
    ).reshape(-1)
    is_top = global_rows < PANEL
    above = jnp.logical_and(
        is_top[:, None], jnp.arange(PANEL, dtype=jnp.int32)[None, :] > global_rows[:, None]
    )
    factor_rows = jnp.where(above, 0.0, factor_rows)
    panel_part = lax.dynamic_index_in_dim(
        factor_rows.reshape(-1, n_cols, BLOCK), col_index, 1, keepdims=False
    )
    combined = finish(
        jnp.stack([got_z * n_x + got_x, got_x * n_zs + got_z]),
        got_there.astype(jnp.int32),
        (my_roots < n_cols).astype(jnp.int32),
        root_front.reshape(root_rows * BLOCK * root_cols, BLOCK),
        panel_part,
        upper,
        lower,
        jnp.dot(factor_rows, column_factor, precision=close, preferred_element_type=F32),
    )
    return (own_factor.reshape(child_border.shape), combined.reshape(root_front.shape))


def solution(mesh):
    fine = Mesh(mesh.devices.reshape(2, 4, 2, 4, 2), ("half", "x", "z_hi", "y", "core"))
    row, col = ("x", "z_hi"), ("y", "core")
    in_specs = (
        P("half", None, None),
        P("half", None, row, None, None),
        P("half", None, row, None, None, col, None),
        P(),
        P(None, ("half",) + row, None, None, col, None),
    )
    out_specs = (
        P("half", None, row, None, None),
        P(None, ("half",) + row, None, None, col, None),
    )
    return jax.shard_map(
        per_device, mesh=fine, in_specs=in_specs, out_specs=out_specs, check_vma=False
    )
```

```python
import functools

import jax
import jax.numpy as jnp
from jax import lax
from jax.experimental import pallas as pl
from jax.experimental.pallas import tpu as pltpu
from jax.sharding import Mesh, PartitionSpec as P

PANEL = 1024
BLOCK = 128
STRIP = 32
CHUNK = 256
HALF = 64
F32 = jnp.float32
BF16 = jnp.bfloat16

exact = lax.Precision.HIGHEST
close = lax.Precision.HIGH


def split_three(values):
    high = values.astype(BF16)
    rest = values - high.astype(F32)
    middle = rest.astype(BF16)
    low = (rest - middle.astype(F32)).astype(BF16)
    return high, middle, low


def gram_strip(rows):
    high, middle, low = split_three(rows)
    left = jnp.concatenate([high, high, middle, high, middle, low], axis=0)
    right = jnp.concatenate([high, middle, high, low, middle, high], axis=0)
    return lax.dot_general(left, right, (((0,), (0,)), ((), ())), preferred_element_type=F32)


def eliminate_strip(rows, start):
    lanes = lax.broadcasted_iota(jnp.int32, (STRIP, BLOCK), 1)
    sublanes = lax.broadcasted_iota(jnp.int32, (STRIP, BLOCK), 0)

    def spread(values, row, count):
        return jnp.broadcast_to(values[row : row + 1, :], (count, BLOCK))

    columns = [
        jnp.broadcast_to(rows[j // 8 * 8 :, start + j : start + j + 1], (STRIP - j // 8 * 8, BLOCK))
        for j in range(STRIP)
    ]
    inside = jnp.logical_and(lanes >= start, lanes < start + STRIP)
    rows = jnp.where(inside, jnp.where(lanes - start == sublanes, 1.0, 0.0), rows)
    for j in range(STRIP):
        base = j // 8 * 8
        column = columns[j]
        scale = lax.rsqrt(spread(column, j - base, 8))
        factor = column * jnp.concatenate([scale] * ((STRIP - base) // 8), axis=0)
        for k in range(j + 1, STRIP):
            skip, count = k // 8 * 8 - base, STRIP - k // 8 * 8
            change = factor[skip:] * spread(factor, k - base, count)
            columns[k] = columns[k] - change
        solved = spread(rows[j : j + 1, :] * scale[0:1, :], 0, STRIP - base)
        below = jnp.where(sublanes[base:] > j, factor, 0.0)
        lower = jnp.where(sublanes[base:] == j, solved, rows[base:] - below * solved)
        rows = jnp.concatenate([rows[:base], lower], axis=0) if base else lower
    return rows


def eliminate_block(block):
    for start in range(0, BLOCK, STRIP):
        stop = start + STRIP
        rows = eliminate_strip(block[start:stop, :], start)
        block[start:stop, :] = rows
        if stop < BLOCK:
            change = gram_strip(rows)[stop:, :]
            lanes = lax.broadcasted_iota(jnp.int32, (BLOCK - stop, BLOCK), 1)
            inside = jnp.logical_and(lanes >= start, lanes < stop)
            block[stop:, :] = jnp.where(inside, 0.0, block[stop:, :]) - change


def inverse_factor_kernel(source, state, block, scaled, stack):
    order = state.shape[0]
    count = order // BLOCK
    if len(source.shape) == 2:
        state[...] = source[...]
    else:
        kept = source.shape[2]
        for i in range(count):
            for k in range(i, count):
                if k - i < kept:
                    part = source[k % 2, k // 2, k - i]
                else:
                    part = source[i % 2, i // 2, count + i - k].T
                state[i * BLOCK : (i + 1) * BLOCK, k * BLOCK : (k + 1) * BLOCK] = part
    row_ids = lax.broadcasted_iota(jnp.int32, (BLOCK, BLOCK), 0)
    col_ids = lax.broadcasted_iota(jnp.int32, (BLOCK, BLOCK), 1)

    def update(j):
        start = (j + 1) * BLOCK
        high, middle, low = split_three(scaled[:, start:].T)
        left = jnp.concatenate([low, middle, high, middle, high, high], axis=1)
        state[start:, j * BLOCK : start] = jnp.zeros((order - start, BLOCK), F32)
        for first in range(0, order, CHUNK):
            stop = order if first < start else min(order, first + CHUNK)
            state[start:stop, first : first + CHUNK] = state[
                start:stop, first : first + CHUNK
            ] - jnp.dot(
                left[: stop - start], stack[:, first : first + CHUNK], preferred_element_type=F32
            )

    def step(j, _):
        here = pl.ds(pl.multiple_of(j * BLOCK, BLOCK), BLOCK)
        block[...] = state[here, here]
        eliminate_block(block)
        inverse = jnp.where(col_ids <= row_ids, block[...], 0.0)
        state[here, here] = jnp.where(col_ids == row_ids, 1.0, 0.0).astype(F32)
        high, middle, low = split_three(inverse)
        left = jnp.concatenate([low, middle, high, middle, high, high], axis=1)
        high, middle, low = split_three(state[here, :])
        right = jnp.concatenate([high, middle, low, high, middle, high], axis=0)
        rows = jnp.dot(left, right, preferred_element_type=F32)
        scaled[...] = rows
        state[here, :] = rows
        high, middle, low = split_three(rows)
        for place, part in enumerate((high, middle, low, high, middle, high)):
            stack[place * BLOCK : (place + 1) * BLOCK, :] = part
        for known in range(count - 1):
            pl.when(j == known)(functools.partial(update, known))
        return 0

    lax.fori_loop(0, count, step, 0)
    for i in range(count - 1):
        stop = (i + 1) * BLOCK
        state[i * BLOCK : stop, stop:] = jnp.zeros((BLOCK, order - stop), F32)


def inverse_factor(source, order):
    whole = pl.BlockSpec(memory_space=pltpu.VMEM)
    return pl.pallas_call(
        inverse_factor_kernel,
        out_shape=jax.ShapeDtypeStruct((order, order), F32),
        in_specs=[whole],
        out_specs=whole,
        scratch_shapes=[
            pltpu.VMEM((BLOCK, BLOCK), F32),
            pltpu.VMEM((BLOCK, order), F32),
            pltpu.VMEM((6 * BLOCK, order), BF16),
        ],
        compiler_params=pltpu.CompilerParams(vmem_limit_bytes=32 * 1024 * 1024),
        cost_estimate=pl.CostEstimate(
            flops=60_000_000_000, bytes_accessed=8 * order * order, transcendentals=0
        ),
        name="inverse_factor",
    )(source)


def spread_kernel(slots, source, target):
    blocks = source.shape[0] // target.shape[1]
    for b in range(blocks):
        target[slots[b]] = source[pl.ds(b, target.shape[1], stride=blocks), :]


def spread_columns(slots, source, slot_total, blocks):
    rows = source.shape[0] // blocks
    tile = rows // 4
    return pl.pallas_call(
        spread_kernel,
        out_shape=jax.ShapeDtypeStruct((slot_total, rows, BLOCK), F32),
        grid_spec=pltpu.PrefetchScalarGridSpec(
            num_scalar_prefetch=1,
            grid=(4,),
            in_specs=[pl.BlockSpec((tile * blocks, BLOCK), lambda i, s: (i, 0))],
            out_specs=pl.BlockSpec((slot_total, tile, BLOCK), lambda i, s: (0, i, 0)),
        ),
        compiler_params=pltpu.CompilerParams(vmem_limit_bytes=32 * 1024 * 1024),
        cost_estimate=pl.CostEstimate(
            flops=0, bytes_accessed=4 * BLOCK * rows * (blocks + slot_total), transcendentals=0
        ),
        name="spread_columns",
    )(slots, source)


def copy_kernel(slots, source, target):
    target[...] = source[...]


def pick_blocks(slots, source):
    shape = (slots.shape[0],) + source.shape[1:]
    block = (1,) + source.shape[1:]
    return pl.pallas_call(
        copy_kernel,
        out_shape=jax.ShapeDtypeStruct(shape, F32),
        grid_spec=pltpu.PrefetchScalarGridSpec(
            num_scalar_prefetch=1,
            grid=(shape[0],),
            in_specs=[pl.BlockSpec(block, lambda i, s: (s[i], 0, 0))],
            out_specs=pl.BlockSpec(block, lambda i, s: (i, 0, 0)),
        ),
        cost_estimate=pl.CostEstimate(
            flops=0, bytes_accessed=8 * shape[0] * shape[1] * shape[2], transcendentals=0
        ),
        name="pick_blocks",
    )(slots, source)


def split_two(values):
    high = values.astype(BF16)
    return high, (values - high.astype(F32)).astype(BF16)


def solve_kernel(slots, first, second, inverse, target, high, middle, low):
    order = inverse.shape[0]

    @pl.when(pl.program_id(0) == 0)
    def _():
        for n in range(0, order, CHUNK):
            here = slice(n, n + CHUNK)
            high[here, :], middle[here, :], low[here, :] = split_three(inverse[here, :])

    def turned(block):
        if len(block.shape) == 3:
            return block[0].T
        parts = [block[z, 0, x, 0].T for x in range(block.shape[2]) for z in range(block.shape[0])]
        return jnp.concatenate(parts, axis=0)

    rows_high, rows_middle, rows_low = split_three(
        jnp.concatenate([turned(first), turned(second)], axis=1)
    )
    for n in range(0, order, CHUNK):
        here, depth = slice(n, n + CHUNK), n + CHUNK
        inverse_high, inverse_middle, inverse_low = (
            part[here, :depth] for part in (high, middle, low)
        )
        h, m, l = rows_high[:depth], rows_middle[:depth], rows_low[:depth]
        left = jnp.concatenate(
            [inverse_low, inverse_middle, inverse_high, inverse_middle, inverse_high, inverse_high],
            axis=1,
        )
        right = jnp.concatenate([h, m, l, h, m, h], axis=0)
        target[here, :] = jnp.dot(left, right, preferred_element_type=F32)


def solve_columns(slots, source, inverse):
    count, order = slots.shape[0], inverse.shape[0]
    if len(source.shape) == 3:
        block = (1, BLOCK, order)
        place = lambda slot: (slot, 0, 0)
    else:
        block = (source.shape[0], 1, source.shape[2], 1, BLOCK, BLOCK)
        place = lambda slot: (0, slot % 2, 0, slot // 2, 0, 0)
    return pl.pallas_call(
        solve_kernel,
        out_shape=jax.ShapeDtypeStruct((order, count * BLOCK), F32),
        grid_spec=pltpu.PrefetchScalarGridSpec(
            num_scalar_prefetch=1,
            grid=(count // 2,),
            in_specs=[
                pl.BlockSpec(block, lambda i, s: place(s[2 * i])),
                pl.BlockSpec(block, lambda i, s: place(s[2 * i + 1])),
                pl.BlockSpec((order, order), lambda i, s: (0, 0), pipeline_mode=pl.Buffered(1)),
            ],
            out_specs=pl.BlockSpec((order, 2 * BLOCK), lambda i, s: (0, i)),
            scratch_shapes=[pltpu.VMEM((order, order), BF16)] * 3,
        ),
        compiler_params=pltpu.CompilerParams(vmem_limit_bytes=40 * 1024 * 1024),
        cost_estimate=pl.CostEstimate(
            flops=16 * count * BLOCK * order * order,
            bytes_accessed=8 * count * BLOCK * order,
            transcendentals=0,
        ),
        name="solve_columns",
    )(slots, source, source, inverse)


def update_kernel(
    slots, there, dests, own, columns, first, second, upper, lower, stack
):
    t = pl.program_id(0)
    order = own.shape[1]

    @pl.when(t == 0)
    def _():
        for n in range(0, own.shape[0], CHUNK):
            here = slice(n, n + CHUNK)
            high, low = split_two(own[here, :])
            stack[here, :order] = low
            stack[here, order : 2 * order] = high
            stack[here, 2 * order :] = high

    high, low = split_two(columns[...])
    product = jnp.dot(
        stack[...], jnp.concatenate([high, low, high], axis=0), preferred_element_type=F32
    )
    left = jnp.where(there[2 * t] > 0, first[0] - product[:, :BLOCK], 0.0)
    right = jnp.where(there[2 * t + 1] > 0, second[0] - product[:, BLOCK:], 0.0)
    for b in range(own.shape[0] // BLOCK):
        for half, target in enumerate((upper, lower)):
            part = slice(b * BLOCK + half * HALF, b * BLOCK + (half + 1) * HALF)
            target[dests[half, b], 0] = left[part]
            target[dests[half, b], 1] = right[part]


def update_columns(slots, there, dests, own, columns, updates, groups, count):
    rows, order = own.shape
    out = jax.ShapeDtypeStruct((groups, count, HALF, BLOCK), F32)
    out_spec = pl.BlockSpec((groups, 2, HALF, BLOCK), lambda t, s, e, d: (0, t, 0, 0))
    return pl.pallas_call(
        update_kernel,
        out_shape=(out, out),
        grid_spec=pltpu.PrefetchScalarGridSpec(
            num_scalar_prefetch=3,
            grid=(slots.shape[0] // 2,),
            in_specs=[
                pl.BlockSpec(
                    (rows, order), lambda t, s, e, d: (0, 0), pipeline_mode=pl.Buffered(1)
                ),
                pl.BlockSpec((order, 2 * BLOCK), lambda t, s, e, d: (0, t)),
                pl.BlockSpec((1, rows, BLOCK), lambda t, s, e, d: (s[2 * t], 0, 0)),
                pl.BlockSpec((1, rows, BLOCK), lambda t, s, e, d: (s[2 * t + 1], 0, 0)),
            ],
            out_specs=(out_spec, out_spec),
            scratch_shapes=[pltpu.VMEM((rows, 3 * order), BF16)],
        ),
        compiler_params=pltpu.CompilerParams(vmem_limit_bytes=40 * 1024 * 1024),
        cost_estimate=pl.CostEstimate(
            flops=16 * count * BLOCK * rows * order,
            bytes_accessed=4 * count * BLOCK * (2 * rows + order + groups * BLOCK),
            transcendentals=0,
        ),
        name="update_columns",
    )(slots, there, dests, own, columns, updates, updates)


def finish_kernel(slots, pieces, there, top, root, panel, product, *parts):
    i = pl.program_id(0)
    target, lower, upper = parts[-1], parts[:2], parts[2:-1]
    columns = product.shape[1] // BLOCK + 1
    target[pl.ds(0, BLOCK, stride=columns), :] = panel[...]
    for part in range(2):
        rows = slice(part * HALF, (part + 1) * HALF)
        for k in range(1, columns):
            here = pl.ds(part * HALF * columns + k, HALF, stride=columns)
            total = root[here, :] - product[rows, (k - 1) * BLOCK : k * BLOCK]
            for half in range(2):
                if part:
                    total = total + jnp.where(there[half, i] > 0, lower[half][0, k - 1], 0.0)
                else:
                    for d in range(len(upper) // 2):
                        wanted = jnp.logical_and(there[half, i] > 0, pieces[half, i] == d)
                        total = total + jnp.where(wanted, upper[2 * d + half][0, k - 1], 0.0)
            target[here, :] = jnp.where(top[i] > 0, 0.0, total)


def finish(slots, pieces, there, top, root, panel, product, lower, upper):
    columns = lower.shape[1] + 1
    root_rows = there.shape[1]
    rows = BLOCK * columns
    block = (1,) + lower.shape[1:]

    def lower_part(half):
        return pl.BlockSpec(block, lambda i, s, d, t, p: (s[0, half, i], 0, 0, 0))

    def upper_part(half, piece):
        return pl.BlockSpec(
            block,
            lambda i, s, d, t, p: (jnp.where(d[half, i] == piece, s[1, half, i], 0), 0, 0, 0),
        )

    return pl.pallas_call(
        finish_kernel,
        out_shape=jax.ShapeDtypeStruct(root.shape, F32),
        grid_spec=pltpu.PrefetchScalarGridSpec(
            num_scalar_prefetch=4,
            grid=(root_rows,),
            in_specs=[
                pl.BlockSpec((rows, BLOCK), lambda i, s, d, t, p: (i, 0)),
                pl.BlockSpec((BLOCK, BLOCK), lambda i, s, d, t, p: (i, 0)),
                pl.BlockSpec((BLOCK, product.shape[1]), lambda i, s, d, t, p: (i, 0)),
                lower_part(0),
                lower_part(1),
            ]
            + [upper_part(half, piece) for piece in range(len(upper)) for half in range(2)],
            out_specs=pl.BlockSpec((rows, BLOCK), lambda i, s, d, t, p: (i, 0)),
        ),
        compiler_params=pltpu.CompilerParams(vmem_limit_bytes=32 * 1024 * 1024),
        cost_estimate=pl.CostEstimate(
            flops=0, bytes_accessed=4 * BLOCK * 5 * rows * root_rows, transcendentals=0
        ),
        name="finish",
    )(slots, pieces, there, top, root, panel, product, lower, lower, *(u for u in upper for _ in range(2)))


def ranks(targets, keys):
    same = targets[..., :, None] == targets[..., None, :]
    before = keys[..., None, :] < keys[..., :, None]
    return jnp.sum(jnp.logical_and(same, before).astype(jnp.int32), axis=-1)


def locate(matches, values):
    matches = matches.astype(jnp.int32)
    return (jnp.sum(matches * values, axis=-1), jnp.sum(matches, axis=-1) > 0)


def times_transposed(left, right, precision):
    return lax.dot_general(
        left, right, (((1,), (1,)), ((), ())), precision=precision, preferred_element_type=F32
    )


def exchange(values, axes):
    return lax.all_to_all(values, axes, split_axis=0, concat_axis=0, tiled=True)


def shift(values, axis, size, step):
    return lax.ppermute(values, axis, [(i, (i + step) % size) for i in range(size)])


def ring(values, axis, size):
    return [values] + [shift(values, axis, size, d) for d in range(1, size)]


def in_order(pieces, axis):
    size = len(pieces)
    return jnp.take(
        jnp.stack(pieces), (lax.axis_index(axis) - jnp.arange(size, dtype=jnp.int32)) % size, axis=0
    )


def after(values, *earlier):
    return lax.optimization_barrier((values,) + earlier)[0]


def per_device(child_pivot, child_border, child_update, index_map, root_front):
    row, col = ("x", "z_hi"), ("y", "core")
    joined = ("z_hi", "half", "x")
    n_x, n_z = lax.axis_size("x"), lax.axis_size("z_hi")
    n_rows = n_x * n_z
    n_y, n_core = lax.axis_size("y"), lax.axis_size("core")
    n_cols = n_y * n_core
    groups = 2 * n_rows
    sibling = lax.axis_index("half")
    row_index = lax.axis_index(row)
    col_index = lax.axis_index(col)
    group = sibling * n_rows + row_index
    block_count = child_border.shape[1]
    pivots = child_border.shape[4]
    local_rows = block_count * BLOCK
    root_rows = root_front.shape[0]
    root_cols = root_front.shape[3]
    numbers = jnp.arange(block_count, dtype=jnp.int32)

    def place_of(groups_of):
        half, x, z = groups_of // n_rows, groups_of // n_z % n_x, groups_of % n_z
        return (z * 2 + half) * n_x + x

    n_zs = 2 * n_z
    z_index = lax.axis_index("z_hi") * 2 + sibling

    def z_shift(values, step):
        spot = lambda z: z % 2 * n_z + z // 2
        pairs = [(spot(z), spot((z + step) % n_zs)) for z in range(n_zs)]
        return lax.ppermute(values, ("half", "z_hi"), pairs)

    child_map = lax.dynamic_index_in_dim(index_map, sibling, 0, keepdims=False).reshape(
        block_count, n_rows
    )
    by_class = child_map.T
    class_dest = by_class % n_cols
    class_rank = ranks(
        class_dest, jnp.where(by_class < n_cols, 0, block_count) + numbers[None, :]
    )
    col_dest = lax.dynamic_index_in_dim(class_dest, col_index, 0, keepdims=False)
    col_rank = lax.dynamic_index_in_dim(class_rank, col_index, 0, keepdims=False)
    row_map = lax.dynamic_index_in_dim(by_class, row_index, 0, keepdims=False)
    row_dest = lax.dynamic_index_in_dim(class_dest, row_index, 0, keepdims=False)
    row_rank = lax.dynamic_index_in_dim(class_rank, row_index, 0, keepdims=False)

    border = child_border.reshape(block_count, BLOCK, pivots)

    wanted, _ = locate(
        jnp.logical_and(
            row_dest[None, :] == col_index,
            row_rank[None, :] == jnp.arange(2, dtype=jnp.int32)[:, None],
        ),
        numbers,
    )
    updates = exchange(
        spread_columns(
            col_dest * 2 + col_rank,
            child_update.reshape(local_rows * block_count, BLOCK),
            2 * n_cols,
            block_count,
        ),
        col,
    )
    borders = lax.all_gather(pick_blocks(wanted, border), row, axis=0, tiled=True)

    flat_source = numbers[:, None] * 2 + class_rank
    wanted_roots = jnp.arange(root_cols, dtype=jnp.int32) * n_cols + col_index
    source_slots, source_there = locate(
        by_class.reshape(1, -1) == wanted_roots[:, None], flat_source.reshape(-1)
    )

    inverse = inverse_factor(child_pivot[0], pivots)
    own_factor = times_transposed(border.reshape(local_rows, pivots), inverse, exact)

    root_view = root_front.reshape(root_rows, BLOCK, root_cols, BLOCK)
    panel_slot = source_slots[0]
    panel_border = lax.dynamic_index_in_dim(borders, panel_slot, 0, keepdims=False)
    panel_factor = times_transposed(panel_border, inverse, exact)
    panel_update = lax.dynamic_index_in_dim(
        updates, panel_slot, 0, keepdims=False
    ) - times_transposed(own_factor, panel_factor, close)
    panel_update = jnp.where(source_there[0], panel_update, 0.0).reshape(block_count, BLOCK, BLOCK)

    sent_blocks, _ = locate(
        place_of(row_map % groups)[None, :] == jnp.arange(groups, dtype=jnp.int32)[:, None], numbers
    )
    every_map = index_map.reshape(2, 1, block_count * n_rows)
    my_roots = jnp.arange(root_rows, dtype=jnp.int32) * groups + group
    sender = place_of(
        jnp.arange(2, dtype=jnp.int32)[:, None, None] * n_rows
        + (jnp.arange(block_count * n_rows, dtype=jnp.int32) % n_rows)[None, None, :]
    )
    got_slots, got_there = locate(every_map == my_roots[None, :, None], sender)

    def extend_add(base, received):
        shape = (-1,) + (1,) * (received.ndim - 1)
        for half in range(2):
            picked = jnp.take(received, got_slots[half], axis=0)
            base = base + jnp.where(got_there[half].reshape(shape), picked, 0.0)
        return base

    panel_got = exchange(jnp.take(panel_update, sent_blocks, axis=0), joined)

    def even(values):
        return jnp.concatenate([values[1:], values[-1:]])

    rest_slots = even(source_slots)
    rest_columns = solve_columns(rest_slots, after(borders, panel_update), inverse)
    own_panel = extend_add(root_view[:, :, 0, :], after(panel_got, rest_columns))

    swaps = [(r * n_cols + c, c * n_rows + r) for r in range(n_rows) for c in range(n_cols)]
    swapped = lax.ppermute(own_panel, row + col, swaps)

    around = [own_panel[0]] + [z_shift(own_panel[0], d) for d in range(1, n_zs)]
    near = jnp.where(sibling == 0, around[0], around[1])
    far = jnp.where(sibling == 0, around[2], around[3])
    first_z = lax.axis_index("z_hi") == 0
    corner = jnp.stack([jnp.where(first_z, near, far), jnp.where(first_z, far, near)])
    leading_column = in_order(ring(corner, "x", n_x), "x").reshape(n_rows, BLOCK, BLOCK)

    column_panel = lax.all_gather(
        after(swapped, leading_column), ("z_hi", "half", "x"), axis=0, tiled=False
    ).reshape(n_z, 2, n_x, root_rows, BLOCK, BLOCK)

    kept = n_cols // 2 + 1
    kept_rows = (col_index - jnp.arange(kept, dtype=jnp.int32)) % n_cols
    kept_blocks = jnp.take(leading_column, kept_rows, axis=0)
    leading = in_order(ring(kept_blocks, "y", n_y), "y")

    sent_place = place_of(row_map % groups)
    sent_z, sent_x = (sent_place // n_x - z_index) % n_zs, sent_place % n_x
    upper, lower = update_columns(
        rest_slots,
        even(source_there.astype(jnp.int32)),
        jnp.stack([sent_x * n_zs + sent_z, sent_z * n_x + sent_x]),
        own_factor,
        after(rest_columns, leading_column),
        updates,
        groups,
        root_cols - 1,
    )
    shape = lower.shape[1:]
    upper = upper.reshape((n_x, n_zs) + shape)
    lower = lower.reshape((n_zs, n_x) + shape)
    lower = [lower[d] for d in range(n_zs)]

    other_core = shift(after(leading, lower), "core", 2, 1)
    is_first = lax.axis_index("core") == 0
    leading = jnp.stack(
        [jnp.where(is_first, leading, other_core), jnp.where(is_first, other_core, leading)]
    )
    root_inverse = inverse_factor(leading, PANEL)

    upper, lower, own_panel, column_panel, root_inverse = lax.optimization_barrier(
        (upper, lower, own_panel, column_panel, root_inverse)
    )
    upper = exchange(upper, "x")
    lower = [lower[0]] + [z_shift(lower[d], d) for d in range(1, n_zs)]
    panel_rows = lax.all_gather(own_panel, col, axis=2, tiled=True)
    upper = [upper[:, d] for d in range(n_zs)]
    upper = [upper[0]] + [z_shift(upper[d], d) for d in range(1, n_zs)]
    lower = exchange(jnp.stack(lower, axis=1), "x").reshape((groups,) + shape)
    got_z, got_x = (z_index - got_slots // n_x) % n_zs, got_slots % n_x

    factor_rows = times_transposed(panel_rows.reshape(root_rows * BLOCK, PANEL), root_inverse, exact)
    column_factor = solve_columns(
        even(jnp.arange(root_cols, dtype=jnp.int32)), column_panel, root_inverse
    )[:, : (root_cols - 1) * BLOCK]
    global_rows = (
        my_roots[:, None] * BLOCK + jnp.arange(BLOCK, dtype=jnp.int32)[None, :]
    ).reshape(-1)
    is_top = global_rows < PANEL
    above = jnp.logical_and(
        is_top[:, None], jnp.arange(PANEL, dtype=jnp.int32)[None, :] > global_rows[:, None]
    )
    factor_rows = jnp.where(above, 0.0, factor_rows)
    panel_part = lax.dynamic_index_in_dim(
        factor_rows.reshape(-1, n_cols, BLOCK), col_index, 1, keepdims=False
    )
    combined = finish(
        jnp.stack([got_x * n_zs + got_z, got_x]),
        got_z,
        got_there.astype(jnp.int32),
        (my_roots < n_cols).astype(jnp.int32),
        root_front.reshape(root_rows * BLOCK * root_cols, BLOCK),
        panel_part,
        jnp.dot(factor_rows, column_factor, precision=close, preferred_element_type=F32),
        lower,
        upper,
    )
    return (own_factor.reshape(child_border.shape), combined.reshape(root_front.shape))


def solution(mesh):
    fine = Mesh(mesh.devices.reshape(2, 4, 2, 4, 2), ("half", "x", "z_hi", "y", "core"))
    row, col = ("x", "z_hi"), ("y", "core")
    in_specs = (
        P("half", None, None),
        P("half", None, row, None, None),
        P("half", None, row, None, None, col, None),
        P(),
        P(None, ("half",) + row, None, None, col, None),
    )
    out_specs = (
        P("half", None, row, None, None),
        P(None, ("half",) + row, None, None, col, None),
    )
    return jax.shard_map(
        per_device, mesh=fine, in_specs=in_specs, out_specs=out_specs, check_vma=False
    )
```

```python
import functools

import jax
import jax.numpy as jnp
from jax import lax
from jax.experimental import pallas as pl
from jax.experimental.pallas import tpu as pltpu
from jax.sharding import Mesh, PartitionSpec as P

PANEL = 1024
BLOCK = 128
STRIP = 32
CHUNK = 256
F32 = jnp.float32
BF16 = jnp.bfloat16

exact = lax.Precision.HIGHEST
close = lax.Precision.HIGH


def split_three(values):
    high = values.astype(BF16)
    rest = values - high.astype(F32)
    middle = rest.astype(BF16)
    low = (rest - middle.astype(F32)).astype(BF16)
    return high, middle, low


def gram_strip(rows):
    high, middle, low = split_three(rows)
    left = jnp.concatenate([high, high, middle, high, middle, low], axis=0)
    right = jnp.concatenate([high, middle, high, low, middle, high], axis=0)
    return lax.dot_general(left, right, (((0,), (0,)), ((), ())), preferred_element_type=F32)


def eliminate_strip(rows, start):
    lanes = lax.broadcasted_iota(jnp.int32, (STRIP, BLOCK), 1)
    sublanes = lax.broadcasted_iota(jnp.int32, (STRIP, BLOCK), 0)

    def spread(values, row, count):
        return jnp.broadcast_to(values[row : row + 1, :], (count, BLOCK))

    columns = [
        jnp.broadcast_to(rows[j // 8 * 8 :, start + j : start + j + 1], (STRIP - j // 8 * 8, BLOCK))
        for j in range(STRIP)
    ]
    inside = jnp.logical_and(lanes >= start, lanes < start + STRIP)
    rows = jnp.where(inside, jnp.where(lanes - start == sublanes, 1.0, 0.0), rows)
    for j in range(STRIP):
        base = j // 8 * 8
        column = columns[j]
        scale = lax.rsqrt(spread(column, j - base, 8))
        factor = column * jnp.concatenate([scale] * ((STRIP - base) // 8), axis=0)
        for k in range(j + 1, STRIP):
            skip, count = k // 8 * 8 - base, STRIP - k // 8 * 8
            change = factor[skip:] * spread(factor, k - base, count)
            columns[k] = columns[k] - change
        solved = spread(rows[j : j + 1, :] * scale[0:1, :], 0, STRIP - base)
        below = jnp.where(sublanes[base:] > j, factor, 0.0)
        lower = jnp.where(sublanes[base:] == j, solved, rows[base:] - below * solved)
        rows = jnp.concatenate([rows[:base], lower], axis=0) if base else lower
    return rows


def eliminate_block(block):
    for start in range(0, BLOCK, STRIP):
        stop = start + STRIP
        rows = eliminate_strip(block[start:stop, :], start)
        block[start:stop, :] = rows
        if stop < BLOCK:
            change = gram_strip(rows)[stop:, :]
            lanes = lax.broadcasted_iota(jnp.int32, (BLOCK - stop, BLOCK), 1)
            inside = jnp.logical_and(lanes >= start, lanes < stop)
            block[stop:, :] = jnp.where(inside, 0.0, block[stop:, :]) - change


def inverse_factor_kernel(source, state, block, scaled, stack):
    order = state.shape[0]
    count = order // BLOCK
    if len(source.shape) == 2:
        state[...] = source[...]
    else:
        kept = source.shape[2]
        for i in range(count):
            for k in range(i, count):
                if k - i < kept:
                    part = source[k % 2, k // 2, k - i]
                else:
                    part = source[i % 2, i // 2, count + i - k].T
                state[i * BLOCK : (i + 1) * BLOCK, k * BLOCK : (k + 1) * BLOCK] = part
    row_ids = lax.broadcasted_iota(jnp.int32, (BLOCK, BLOCK), 0)
    col_ids = lax.broadcasted_iota(jnp.int32, (BLOCK, BLOCK), 1)

    def update(j):
        start = (j + 1) * BLOCK
        high, middle, low = split_three(scaled[:, start:].T)
        left = jnp.concatenate([low, middle, high, middle, high, high], axis=1)
        state[start:, j * BLOCK : start] = jnp.zeros((order - start, BLOCK), F32)
        for first in range(0, order, CHUNK):
            stop = order if first < start else min(order, first + CHUNK)
            state[start:stop, first : first + CHUNK] = state[
                start:stop, first : first + CHUNK
            ] - jnp.dot(
                left[: stop - start], stack[:, first : first + CHUNK], preferred_element_type=F32
            )

    def step(j, _):
        here = pl.ds(pl.multiple_of(j * BLOCK, BLOCK), BLOCK)
        block[...] = state[here, here]
        eliminate_block(block)
        inverse = jnp.where(col_ids <= row_ids, block[...], 0.0)
        state[here, here] = jnp.where(col_ids == row_ids, 1.0, 0.0).astype(F32)
        high, middle, low = split_three(inverse)
        left = jnp.concatenate([low, middle, high, middle, high, high], axis=1)
        high, middle, low = split_three(state[here, :])
        right = jnp.concatenate([high, middle, low, high, middle, high], axis=0)
        rows = jnp.dot(left, right, preferred_element_type=F32)
        scaled[...] = rows
        state[here, :] = rows
        high, middle, low = split_three(rows)
        for place, part in enumerate((high, middle, low, high, middle, high)):
            stack[place * BLOCK : (place + 1) * BLOCK, :] = part
        for known in range(count - 1):
            pl.when(j == known)(functools.partial(update, known))
        return 0

    lax.fori_loop(0, count, step, 0)
    for i in range(count - 1):
        stop = (i + 1) * BLOCK
        state[i * BLOCK : stop, stop:] = jnp.zeros((BLOCK, order - stop), F32)


def inverse_factor(source, order, cost):
    whole = pl.BlockSpec(memory_space=pltpu.VMEM)
    return pl.pallas_call(
        inverse_factor_kernel,
        out_shape=jax.ShapeDtypeStruct((order, order), F32),
        in_specs=[whole],
        out_specs=whole,
        scratch_shapes=[
            pltpu.VMEM((BLOCK, BLOCK), F32),
            pltpu.VMEM((BLOCK, order), F32),
            pltpu.VMEM((6 * BLOCK, order), BF16),
        ],
        compiler_params=pltpu.CompilerParams(vmem_limit_bytes=32 * 1024 * 1024),
        cost_estimate=pl.CostEstimate(
            flops=cost, bytes_accessed=8 * order * order, transcendentals=0
        ),
        name="inverse_factor",
    )(source)


def spread_kernel(slots, source, target):
    blocks = source.shape[0] // target.shape[1]
    for b in range(blocks):
        target[slots[b]] = source[pl.ds(b, target.shape[1], stride=blocks), :]


def spread_columns(slots, source, slot_total, blocks):
    rows = source.shape[0] // blocks
    tile = rows // 4
    return pl.pallas_call(
        spread_kernel,
        out_shape=jax.ShapeDtypeStruct((slot_total, rows, BLOCK), F32),
        grid_spec=pltpu.PrefetchScalarGridSpec(
            num_scalar_prefetch=1,
            grid=(4,),
            in_specs=[pl.BlockSpec((tile * blocks, BLOCK), lambda i, s: (i, 0))],
            out_specs=pl.BlockSpec((slot_total, tile, BLOCK), lambda i, s: (0, i, 0)),
        ),
        compiler_params=pltpu.CompilerParams(vmem_limit_bytes=32 * 1024 * 1024),
        cost_estimate=pl.CostEstimate(
            flops=0, bytes_accessed=4 * BLOCK * rows * (blocks + slot_total), transcendentals=0
        ),
        name="spread_columns",
    )(slots, source)


def copy_kernel(slots, source, target):
    target[...] = source[...]


def pick_blocks(slots, source):
    shape = (slots.shape[0],) + source.shape[1:]
    block = (1,) + source.shape[1:]
    return pl.pallas_call(
        copy_kernel,
        out_shape=jax.ShapeDtypeStruct(shape, F32),
        grid_spec=pltpu.PrefetchScalarGridSpec(
            num_scalar_prefetch=1,
            grid=(shape[0],),
            in_specs=[pl.BlockSpec(block, lambda i, s: (s[i], 0, 0))],
            out_specs=pl.BlockSpec(block, lambda i, s: (i, 0, 0)),
        ),
        cost_estimate=pl.CostEstimate(
            flops=0, bytes_accessed=8 * shape[0] * shape[1] * shape[2], transcendentals=0
        ),
        name="pick_blocks",
    )(slots, source)


def split_two(values):
    high = values.astype(BF16)
    return high, (values - high.astype(F32)).astype(BF16)


def solve_kernel(slots, first, second, inverse, target, high, middle, low):
    order = inverse.shape[0]

    @pl.when(pl.program_id(0) == 0)
    def _():
        for n in range(0, order, CHUNK):
            here = slice(n, n + CHUNK)
            high[here, :], middle[here, :], low[here, :] = split_three(inverse[here, :])

    def turned(block):
        if len(block.shape) == 3:
            return block[0].T
        parts = [block[z, 0, x, 0].T for x in range(block.shape[2]) for z in range(block.shape[0])]
        return jnp.concatenate(parts, axis=0)

    rows_high, rows_middle, rows_low = split_three(
        jnp.concatenate([turned(first), turned(second)], axis=1)
    )
    for n in range(0, order, CHUNK):
        here, depth = slice(n, n + CHUNK), n + CHUNK
        inverse_high, inverse_middle, inverse_low = (
            part[here, :depth] for part in (high, middle, low)
        )
        h, m, l = rows_high[:depth], rows_middle[:depth], rows_low[:depth]
        left = jnp.concatenate(
            [inverse_low, inverse_middle, inverse_high, inverse_middle, inverse_high, inverse_high],
            axis=1,
        )
        right = jnp.concatenate([h, m, l, h, m, h], axis=0)
        target[here, :] = jnp.dot(left, right, preferred_element_type=F32)


def solve_columns(slots, source, inverse):
    count, order = slots.shape[0], inverse.shape[0]
    if len(source.shape) == 3:
        block = (1, BLOCK, order)
        place = lambda slot: (slot, 0, 0)
    else:
        block = (source.shape[0], 1, source.shape[2], 1, BLOCK, BLOCK)
        place = lambda slot: (0, slot % 2, 0, slot // 2, 0, 0)
    return pl.pallas_call(
        solve_kernel,
        out_shape=jax.ShapeDtypeStruct((order, count * BLOCK), F32),
        grid_spec=pltpu.PrefetchScalarGridSpec(
            num_scalar_prefetch=1,
            grid=(count // 2,),
            in_specs=[
                pl.BlockSpec(block, lambda i, s: place(s[2 * i])),
                pl.BlockSpec(block, lambda i, s: place(s[2 * i + 1])),
                pl.BlockSpec((order, order), lambda i, s: (0, 0), pipeline_mode=pl.Buffered(1)),
            ],
            out_specs=pl.BlockSpec((order, 2 * BLOCK), lambda i, s: (0, i)),
            scratch_shapes=[pltpu.VMEM((order, order), BF16)] * 3,
        ),
        compiler_params=pltpu.CompilerParams(vmem_limit_bytes=40 * 1024 * 1024),
        cost_estimate=pl.CostEstimate(
            flops=16 * count * BLOCK * order * order,
            bytes_accessed=8 * count * BLOCK * order,
            transcendentals=0,
        ),
        name="solve_columns",
    )(slots, source, source, inverse)


def update_kernel(slots, there, dests, own, columns, first, second, target, stack):
    t = pl.program_id(0)
    order = own.shape[1]

    @pl.when(t == 0)
    def _():
        for n in range(0, own.shape[0], CHUNK):
            here = slice(n, n + CHUNK)
            high, low = split_two(own[here, :])
            stack[here, :order] = low
            stack[here, order : 2 * order] = high
            stack[here, 2 * order :] = high

    high, low = split_two(columns[...])
    product = jnp.dot(
        stack[...], jnp.concatenate([high, low, high], axis=0), preferred_element_type=F32
    )
    left = jnp.where(there[2 * t] > 0, first[0] - product[:, :BLOCK], 0.0)
    right = jnp.where(there[2 * t + 1] > 0, second[0] - product[:, BLOCK:], 0.0)
    for b in range(own.shape[0] // BLOCK):
        part = slice(b * BLOCK, (b + 1) * BLOCK)
        target[dests[b], 0] = left[part]
        target[dests[b], 1] = right[part]


def update_columns(slots, there, dests, own, columns, updates, groups, count):
    rows, order = own.shape
    return pl.pallas_call(
        update_kernel,
        out_shape=jax.ShapeDtypeStruct((groups, count, BLOCK, BLOCK), F32),
        grid_spec=pltpu.PrefetchScalarGridSpec(
            num_scalar_prefetch=3,
            grid=(slots.shape[0] // 2,),
            in_specs=[
                pl.BlockSpec(
                    (rows, order), lambda t, s, e, d: (0, 0), pipeline_mode=pl.Buffered(1)
                ),
                pl.BlockSpec((order, 2 * BLOCK), lambda t, s, e, d: (0, t)),
                pl.BlockSpec((1, rows, BLOCK), lambda t, s, e, d: (s[2 * t], 0, 0)),
                pl.BlockSpec((1, rows, BLOCK), lambda t, s, e, d: (s[2 * t + 1], 0, 0)),
            ],
            out_specs=pl.BlockSpec((groups, 2, BLOCK, BLOCK), lambda t, s, e, d: (0, t, 0, 0)),
            scratch_shapes=[pltpu.VMEM((rows, 3 * order), BF16)],
        ),
        compiler_params=pltpu.CompilerParams(vmem_limit_bytes=40 * 1024 * 1024),
        cost_estimate=pl.CostEstimate(
            flops=16 * count * BLOCK * rows * order,
            bytes_accessed=4 * count * BLOCK * (2 * rows + order + groups * BLOCK),
            transcendentals=0,
        ),
        name="update_columns",
    )(slots, there, dests, own, columns, updates, updates)


def finish_kernel(slots, there, top, root, panel, first, second, product, target):
    i = pl.program_id(0)
    columns = first.shape[1] + 1
    target[pl.ds(0, BLOCK, stride=columns), :] = panel[...]
    for k in range(1, columns):
        here = pl.ds(k, BLOCK, stride=columns)
        total = root[here, :]
        total = total + jnp.where(there[0, i] > 0, first[0, k - 1], 0.0)
        total = total + jnp.where(there[1, i] > 0, second[0, k - 1], 0.0)
        total = total - product[:, (k - 1) * BLOCK : k * BLOCK]
        target[here, :] = jnp.where(top[i] > 0, 0.0, total)


def finish(slots, there, top, root, panel, received, product):
    columns = received.shape[1] + 1
    root_rows = slots.shape[1]
    rows = BLOCK * columns
    block = (1,) + received.shape[1:]
    return pl.pallas_call(
        finish_kernel,
        out_shape=jax.ShapeDtypeStruct(root.shape, F32),
        grid_spec=pltpu.PrefetchScalarGridSpec(
            num_scalar_prefetch=3,
            grid=(root_rows,),
            in_specs=[
                pl.BlockSpec((rows, BLOCK), lambda i, s, t, p: (i, 0)),
                pl.BlockSpec((BLOCK, BLOCK), lambda i, s, t, p: (i, 0)),
                pl.BlockSpec(block, lambda i, s, t, p: (s[0, i], 0, 0, 0)),
                pl.BlockSpec(block, lambda i, s, t, p: (s[1, i], 0, 0, 0)),
                pl.BlockSpec((BLOCK, product.shape[1]), lambda i, s, t, p: (i, 0)),
            ],
            out_specs=pl.BlockSpec((rows, BLOCK), lambda i, s, t, p: (i, 0)),
        ),
        cost_estimate=pl.CostEstimate(
            flops=0, bytes_accessed=4 * BLOCK * 5 * rows * root_rows, transcendentals=0
        ),
        name="finish",
    )(slots, there, top, root, panel, received, received, product)


def ranks(targets, keys):
    same = targets[..., :, None] == targets[..., None, :]
    before = keys[..., None, :] < keys[..., :, None]
    return jnp.sum(jnp.logical_and(same, before).astype(jnp.int32), axis=-1)


def locate(matches, values):
    matches = matches.astype(jnp.int32)
    return (jnp.sum(matches * values, axis=-1), jnp.sum(matches, axis=-1) > 0)


def times_transposed(left, right, precision):
    return lax.dot_general(
        left, right, (((1,), (1,)), ((), ())), precision=precision, preferred_element_type=F32
    )


def exchange(values, axes):
    return lax.all_to_all(values, axes, split_axis=0, concat_axis=0, tiled=True)


def shift(values, axis, size, step):
    return lax.ppermute(values, axis, [(i, (i + step) % size) for i in range(size)])


def ring(values, axis, size):
    return [values] + [shift(values, axis, size, d) for d in range(1, size)]


def in_order(pieces, axis):
    size = len(pieces)
    return jnp.take(
        jnp.stack(pieces), (lax.axis_index(axis) - jnp.arange(size, dtype=jnp.int32)) % size, axis=0
    )


def after(values, *earlier):
    return lax.optimization_barrier((values,) + earlier)[0]


def per_device(child_pivot, child_border, child_update, index_map, root_front):
    row, col = ("x", "z_hi"), ("y", "core")
    joined = ("z_hi", "half", "x")
    n_x, n_z = lax.axis_size("x"), lax.axis_size("z_hi")
    n_rows = n_x * n_z
    n_y, n_core = lax.axis_size("y"), lax.axis_size("core")
    n_cols = n_y * n_core
    groups = 2 * n_rows
    sibling = lax.axis_index("half")
    row_index = lax.axis_index(row)
    col_index = lax.axis_index(col)
    group = sibling * n_rows + row_index
    block_count = child_border.shape[1]
    pivots = child_border.shape[4]
    local_rows = block_count * BLOCK
    root_rows = root_front.shape[0]
    root_cols = root_front.shape[3]
    numbers = jnp.arange(block_count, dtype=jnp.int32)

    def place_of(groups_of):
        half, x, z = groups_of // n_rows, groups_of // n_z % n_x, groups_of % n_z
        return (z * 2 + half) * n_x + x

    n_zs = 2 * n_z

    def z_shift(values, step):
        spot = lambda z: z % 2 * n_z + z // 2
        pairs = [(spot(z), spot((z + step) % n_zs)) for z in range(n_zs)]
        return lax.ppermute(values, ("half", "z_hi"), pairs)

    child_map = lax.dynamic_index_in_dim(index_map, sibling, 0, keepdims=False).reshape(
        block_count, n_rows
    )
    by_class = child_map.T
    class_dest = by_class % n_cols
    class_rank = ranks(
        class_dest, jnp.where(by_class < n_cols, 0, block_count) + numbers[None, :]
    )
    col_dest = lax.dynamic_index_in_dim(class_dest, col_index, 0, keepdims=False)
    col_rank = lax.dynamic_index_in_dim(class_rank, col_index, 0, keepdims=False)
    row_map = lax.dynamic_index_in_dim(by_class, row_index, 0, keepdims=False)
    row_dest = lax.dynamic_index_in_dim(class_dest, row_index, 0, keepdims=False)
    row_rank = lax.dynamic_index_in_dim(class_rank, row_index, 0, keepdims=False)

    border = child_border.reshape(block_count, BLOCK, pivots)

    wanted, _ = locate(
        jnp.logical_and(
            row_dest[None, :] == col_index,
            row_rank[None, :] == jnp.arange(2, dtype=jnp.int32)[:, None],
        ),
        numbers,
    )
    updates = exchange(
        spread_columns(
            col_dest * 2 + col_rank,
            child_update.reshape(local_rows * block_count, BLOCK),
            2 * n_cols,
            block_count,
        ),
        col,
    )
    borders = lax.all_gather(pick_blocks(wanted, border), row, axis=0, tiled=True)

    flat_source = numbers[:, None] * 2 + class_rank
    wanted_roots = jnp.arange(root_cols, dtype=jnp.int32) * n_cols + col_index
    source_slots, source_there = locate(
        by_class.reshape(1, -1) == wanted_roots[:, None], flat_source.reshape(-1)
    )

    inverse = inverse_factor(child_pivot[0], pivots, 40_000_000_000)
    own_factor = times_transposed(border.reshape(local_rows, pivots), inverse, exact)

    root_view = root_front.reshape(root_rows, BLOCK, root_cols, BLOCK)
    panel_slot = source_slots[0]
    panel_border = lax.dynamic_index_in_dim(borders, panel_slot, 0, keepdims=False)
    panel_factor = times_transposed(panel_border, inverse, exact)
    panel_update = lax.dynamic_index_in_dim(
        updates, panel_slot, 0, keepdims=False
    ) - times_transposed(own_factor, panel_factor, close)
    panel_update = jnp.where(source_there[0], panel_update, 0.0).reshape(block_count, BLOCK, BLOCK)

    sent_blocks, _ = locate(
        place_of(row_map % groups)[None, :] == jnp.arange(groups, dtype=jnp.int32)[:, None], numbers
    )
    every_map = index_map.reshape(2, 1, block_count * n_rows)
    my_roots = jnp.arange(root_rows, dtype=jnp.int32) * groups + group
    sender = place_of(
        jnp.arange(2, dtype=jnp.int32)[:, None, None] * n_rows
        + (jnp.arange(block_count * n_rows, dtype=jnp.int32) % n_rows)[None, None, :]
    )
    got_slots, got_there = locate(every_map == my_roots[None, :, None], sender)

    def extend_add(base, received):
        shape = (-1,) + (1,) * (received.ndim - 1)
        for half in range(2):
            picked = jnp.take(received, got_slots[half], axis=0)
            base = base + jnp.where(got_there[half].reshape(shape), picked, 0.0)
        return base

    panel_got = exchange(jnp.take(panel_update, sent_blocks, axis=0), joined)

    def even(values):
        return jnp.concatenate([values[1:], values[-1:]])

    rest_slots = even(source_slots)
    rest_columns = solve_columns(rest_slots, after(borders, panel_update), inverse)
    own_panel = extend_add(root_view[:, :, 0, :], after(panel_got, rest_columns))

    swaps = [(r * n_cols + c, c * n_rows + r) for r in range(n_rows) for c in range(n_cols)]
    swapped = lax.ppermute(own_panel, row + col, swaps)
    column_panel = lax.all_gather(swapped, ("z_hi", "half", "x"), axis=0, tiled=False).reshape(
        n_z, 2, n_x, root_rows, BLOCK, BLOCK
    )

    rest_sent = update_columns(
        rest_slots,
        even(source_there.astype(jnp.int32)),
        place_of(row_map % groups),
        own_factor,
        after(rest_columns, swapped),
        updates,
        groups,
        root_cols - 1,
    )

    column_panel, rest_sent, own_panel = lax.optimization_barrier(
        (column_panel, rest_sent, own_panel)
    )
    rest_got = exchange(rest_sent, joined)

    around = [own_panel[0]] + [z_shift(own_panel[0], d) for d in range(1, n_zs)]
    near = jnp.where(sibling == 0, around[0], around[1])
    far = jnp.where(sibling == 0, around[2], around[3])
    first_z = lax.axis_index("z_hi") == 0
    corner = jnp.stack([jnp.where(first_z, near, far), jnp.where(first_z, far, near)])
    leading_column = in_order(ring(corner, "x", n_x), "x").reshape(n_rows, BLOCK, BLOCK)
    kept = n_cols // 2 + 1
    kept_rows = (col_index - jnp.arange(kept, dtype=jnp.int32)) % n_cols
    kept_blocks = jnp.take(leading_column, kept_rows, axis=0)
    leading = in_order(ring(kept_blocks, "y", n_y), "y")
    other_core = shift(leading, "core", 2, 1)
    is_first = lax.axis_index("core") == 0
    leading = jnp.stack(
        [jnp.where(is_first, leading, other_core), jnp.where(is_first, other_core, leading)]
    )

    panel_rows = lax.all_gather(own_panel, col, axis=2, tiled=True)

    root_inverse = inverse_factor(leading, PANEL, 1_000_000)
    factor_rows = times_transposed(panel_rows.reshape(root_rows * BLOCK, PANEL), root_inverse, exact)
    column_factor = solve_columns(
        even(jnp.arange(root_cols, dtype=jnp.int32)), column_panel, root_inverse
    )[:, : (root_cols - 1) * BLOCK]
    global_rows = (
        my_roots[:, None] * BLOCK + jnp.arange(BLOCK, dtype=jnp.int32)[None, :]
    ).reshape(-1)
    is_top = global_rows < PANEL
    above = jnp.logical_and(
        is_top[:, None], jnp.arange(PANEL, dtype=jnp.int32)[None, :] > global_rows[:, None]
    )
    factor_rows = jnp.where(above, 0.0, factor_rows)
    panel_part = lax.dynamic_index_in_dim(
        factor_rows.reshape(-1, n_cols, BLOCK), col_index, 1, keepdims=False
    )
    combined = finish(
        got_slots,
        got_there.astype(jnp.int32),
        (my_roots < n_cols).astype(jnp.int32),
        root_front.reshape(root_rows * BLOCK * root_cols, BLOCK),
        panel_part,
        rest_got,
        jnp.dot(factor_rows, column_factor, precision=close, preferred_element_type=F32),
    )
    return (own_factor.reshape(child_border.shape), combined.reshape(root_front.shape))


def solution(mesh):
    fine = Mesh(mesh.devices.reshape(2, 4, 2, 4, 2), ("half", "x", "z_hi", "y", "core"))
    row, col = ("x", "z_hi"), ("y", "core")
    in_specs = (
        P("half", None, None),
        P("half", None, row, None, None),
        P("half", None, row, None, None, col, None),
        P(),
        P(None, ("half",) + row, None, None, col, None),
    )
    out_specs = (
        P("half", None, row, None, None),
        P(None, ("half",) + row, None, None, col, None),
    )
    return jax.shard_map(
        per_device, mesh=fine, in_specs=in_specs, out_specs=out_specs, check_vma=False
    )
```

```python
import functools

import jax
import jax.numpy as jnp
from jax import lax
from jax.experimental import pallas as pl
from jax.experimental.pallas import tpu as pltpu
from jax.sharding import Mesh, PartitionSpec as P

PANEL = 1024
BLOCK = 128
STRIP = 32
CHUNK = 256
HALF = 64
F32 = jnp.float32
BF16 = jnp.bfloat16

exact = lax.Precision.HIGHEST
close = lax.Precision.HIGH


def split_three(values):
    high = values.astype(BF16)
    rest = values - high.astype(F32)
    middle = rest.astype(BF16)
    low = (rest - middle.astype(F32)).astype(BF16)
    return high, middle, low


def gram_strip(rows):
    high, middle, low = split_three(rows)
    left = jnp.concatenate([high, high, middle, high, middle, low], axis=0)
    right = jnp.concatenate([high, middle, high, low, middle, high], axis=0)
    return lax.dot_general(left, right, (((0,), (0,)), ((), ())), preferred_element_type=F32)


def eliminate_strip(rows, start):
    lanes = lax.broadcasted_iota(jnp.int32, (STRIP, BLOCK), 1)
    sublanes = lax.broadcasted_iota(jnp.int32, (STRIP, BLOCK), 0)

    def spread(values, row, count):
        return jnp.broadcast_to(values[row : row + 1, :], (count, BLOCK))

    columns = [
        jnp.broadcast_to(rows[j // 8 * 8 :, start + j : start + j + 1], (STRIP - j // 8 * 8, BLOCK))
        for j in range(STRIP)
    ]
    inside = jnp.logical_and(lanes >= start, lanes < start + STRIP)
    rows = jnp.where(inside, jnp.where(lanes - start == sublanes, 1.0, 0.0), rows)
    for j in range(STRIP):
        base = j // 8 * 8
        column = columns[j]
        scale = lax.rsqrt(spread(column, j - base, 8))
        factor = column * jnp.concatenate([scale] * ((STRIP - base) // 8), axis=0)
        for k in range(j + 1, STRIP):
            skip, count = k // 8 * 8 - base, STRIP - k // 8 * 8
            change = factor[skip:] * spread(factor, k - base, count)
            columns[k] = columns[k] - change
        solved = spread(rows[j : j + 1, :] * scale[0:1, :], 0, STRIP - base)
        below = jnp.where(sublanes[base:] > j, factor, 0.0)
        lower = jnp.where(sublanes[base:] == j, solved, rows[base:] - below * solved)
        rows = jnp.concatenate([rows[:base], lower], axis=0) if base else lower
    return rows


def eliminate_block(block):
    for start in range(0, BLOCK, STRIP):
        stop = start + STRIP
        rows = eliminate_strip(block[start:stop, :], start)
        block[start:stop, :] = rows
        if stop < BLOCK:
            change = gram_strip(rows)[stop:, :]
            lanes = lax.broadcasted_iota(jnp.int32, (BLOCK - stop, BLOCK), 1)
            inside = jnp.logical_and(lanes >= start, lanes < stop)
            block[stop:, :] = jnp.where(inside, 0.0, block[stop:, :]) - change


def inverse_factor_kernel(source, state, block, scaled, stack):
    order = state.shape[0]
    count = order // BLOCK
    if len(source.shape) == 2:
        state[...] = source[...]
    else:
        kept = source.shape[2]
        for i in range(count):
            for k in range(i, count):
                if k - i < kept:
                    part = source[k % 2, k // 2, k - i]
                else:
                    part = source[i % 2, i // 2, count + i - k].T
                state[i * BLOCK : (i + 1) * BLOCK, k * BLOCK : (k + 1) * BLOCK] = part
    row_ids = lax.broadcasted_iota(jnp.int32, (BLOCK, BLOCK), 0)
    col_ids = lax.broadcasted_iota(jnp.int32, (BLOCK, BLOCK), 1)

    def update(j):
        start = (j + 1) * BLOCK
        high, middle, low = split_three(scaled[:, start:].T)
        left = jnp.concatenate([low, middle, high, middle, high, high], axis=1)
        state[start:, j * BLOCK : start] = jnp.zeros((order - start, BLOCK), F32)
        for first in range(0, order, CHUNK):
            stop = order if first < start else min(order, first + CHUNK)
            state[start:stop, first : first + CHUNK] = state[
                start:stop, first : first + CHUNK
            ] - jnp.dot(
                left[: stop - start], stack[:, first : first + CHUNK], preferred_element_type=F32
            )

    def step(j, _):
        here = pl.ds(pl.multiple_of(j * BLOCK, BLOCK), BLOCK)
        block[...] = state[here, here]
        eliminate_block(block)
        inverse = jnp.where(col_ids <= row_ids, block[...], 0.0)
        state[here, here] = jnp.where(col_ids == row_ids, 1.0, 0.0).astype(F32)
        high, middle, low = split_three(inverse)
        left = jnp.concatenate([low, middle, high, middle, high, high], axis=1)
        high, middle, low = split_three(state[here, :])
        right = jnp.concatenate([high, middle, low, high, middle, high], axis=0)
        rows = jnp.dot(left, right, preferred_element_type=F32)
        scaled[...] = rows
        state[here, :] = rows
        high, middle, low = split_three(rows)
        for place, part in enumerate((high, middle, low, high, middle, high)):
            stack[place * BLOCK : (place + 1) * BLOCK, :] = part
        for known in range(count - 1):
            pl.when(j == known)(functools.partial(update, known))
        return 0

    lax.fori_loop(0, count, step, 0)
    for i in range(count - 1):
        stop = (i + 1) * BLOCK
        state[i * BLOCK : stop, stop:] = jnp.zeros((BLOCK, order - stop), F32)


def inverse_factor(source, order):
    whole = pl.BlockSpec(memory_space=pltpu.VMEM)
    return pl.pallas_call(
        inverse_factor_kernel,
        out_shape=jax.ShapeDtypeStruct((order, order), F32),
        in_specs=[whole],
        out_specs=whole,
        scratch_shapes=[
            pltpu.VMEM((BLOCK, BLOCK), F32),
            pltpu.VMEM((BLOCK, order), F32),
            pltpu.VMEM((6 * BLOCK, order), BF16),
        ],
        compiler_params=pltpu.CompilerParams(vmem_limit_bytes=32 * 1024 * 1024),
        cost_estimate=pl.CostEstimate(
            flops=60_000_000_000, bytes_accessed=8 * order * order, transcendentals=0
        ),
        name="inverse_factor",
    )(source)


def spread_kernel(slots, source, target):
    blocks = source.shape[0] // target.shape[1]
    for b in range(blocks):
        target[slots[b]] = source[pl.ds(b, target.shape[1], stride=blocks), :]


def spread_columns(slots, source, slot_total, blocks):
    rows = source.shape[0] // blocks
    tile = rows // 4
    return pl.pallas_call(
        spread_kernel,
        out_shape=jax.ShapeDtypeStruct((slot_total, rows, BLOCK), F32),
        grid_spec=pltpu.PrefetchScalarGridSpec(
            num_scalar_prefetch=1,
            grid=(4,),
            in_specs=[pl.BlockSpec((tile * blocks, BLOCK), lambda i, s: (i, 0))],
            out_specs=pl.BlockSpec((slot_total, tile, BLOCK), lambda i, s: (0, i, 0)),
        ),
        compiler_params=pltpu.CompilerParams(vmem_limit_bytes=32 * 1024 * 1024),
        cost_estimate=pl.CostEstimate(
            flops=0, bytes_accessed=4 * BLOCK * rows * (blocks + slot_total), transcendentals=0
        ),
        name="spread_columns",
    )(slots, source)


def copy_kernel(slots, source, target):
    target[...] = source[...]


def pick_blocks(slots, source):
    shape = (slots.shape[0],) + source.shape[1:]
    block = (1,) + source.shape[1:]
    return pl.pallas_call(
        copy_kernel,
        out_shape=jax.ShapeDtypeStruct(shape, F32),
        grid_spec=pltpu.PrefetchScalarGridSpec(
            num_scalar_prefetch=1,
            grid=(shape[0],),
            in_specs=[pl.BlockSpec(block, lambda i, s: (s[i], 0, 0))],
            out_specs=pl.BlockSpec(block, lambda i, s: (i, 0, 0)),
        ),
        cost_estimate=pl.CostEstimate(
            flops=0, bytes_accessed=8 * shape[0] * shape[1] * shape[2], transcendentals=0
        ),
        name="pick_blocks",
    )(slots, source)


def split_two(values):
    high = values.astype(BF16)
    return high, (values - high.astype(F32)).astype(BF16)


def solve_kernel(slots, first, second, inverse, target, high, middle, low):
    order = inverse.shape[0]

    @pl.when(pl.program_id(0) == 0)
    def _():
        for n in range(0, order, CHUNK):
            here = slice(n, n + CHUNK)
            high[here, :], middle[here, :], low[here, :] = split_three(inverse[here, :])

    def turned(block):
        if len(block.shape) == 3:
            return block[0].T
        parts = [block[z, 0, x, 0].T for x in range(block.shape[2]) for z in range(block.shape[0])]
        return jnp.concatenate(parts, axis=0)

    rows_high, rows_middle, rows_low = split_three(
        jnp.concatenate([turned(first), turned(second)], axis=1)
    )
    for n in range(0, order, CHUNK):
        here, depth = slice(n, n + CHUNK), n + CHUNK
        inverse_high, inverse_middle, inverse_low = (
            part[here, :depth] for part in (high, middle, low)
        )
        h, m, l = rows_high[:depth], rows_middle[:depth], rows_low[:depth]
        left = jnp.concatenate(
            [inverse_low, inverse_middle, inverse_high, inverse_middle, inverse_high, inverse_high],
            axis=1,
        )
        right = jnp.concatenate([h, m, l, h, m, h], axis=0)
        target[here, :] = jnp.dot(left, right, preferred_element_type=F32)


def solve_columns(slots, source, inverse):
    count, order = slots.shape[0], inverse.shape[0]
    if len(source.shape) == 3:
        block = (1, BLOCK, order)
        place = lambda slot: (slot, 0, 0)
    else:
        block = (source.shape[0], 1, source.shape[2], 1, BLOCK, BLOCK)
        place = lambda slot: (0, slot % 2, 0, slot // 2, 0, 0)
    return pl.pallas_call(
        solve_kernel,
        out_shape=jax.ShapeDtypeStruct((order, count * BLOCK), F32),
        grid_spec=pltpu.PrefetchScalarGridSpec(
            num_scalar_prefetch=1,
            grid=(count // 2,),
            in_specs=[
                pl.BlockSpec(block, lambda i, s: place(s[2 * i])),
                pl.BlockSpec(block, lambda i, s: place(s[2 * i + 1])),
                pl.BlockSpec((order, order), lambda i, s: (0, 0), pipeline_mode=pl.Buffered(1)),
            ],
            out_specs=pl.BlockSpec((order, 2 * BLOCK), lambda i, s: (0, i)),
            scratch_shapes=[pltpu.VMEM((order, order), BF16)] * 3,
        ),
        compiler_params=pltpu.CompilerParams(vmem_limit_bytes=40 * 1024 * 1024),
        cost_estimate=pl.CostEstimate(
            flops=16 * count * BLOCK * order * order,
            bytes_accessed=8 * count * BLOCK * order,
            transcendentals=0,
        ),
        name="solve_columns",
    )(slots, source, source, inverse)


def update_kernel(
    slots, there, dests, own, columns, first, second, upper, lower, stack
):
    t = pl.program_id(0)
    order = own.shape[1]

    @pl.when(t == 0)
    def _():
        for n in range(0, own.shape[0], CHUNK):
            here = slice(n, n + CHUNK)
            high, low = split_two(own[here, :])
            stack[here, :order] = low
            stack[here, order : 2 * order] = high
            stack[here, 2 * order :] = high

    high, low = split_two(columns[...])
    product = jnp.dot(
        stack[...], jnp.concatenate([high, low, high], axis=0), preferred_element_type=F32
    )
    left = jnp.where(there[2 * t] > 0, first[0] - product[:, :BLOCK], 0.0)
    right = jnp.where(there[2 * t + 1] > 0, second[0] - product[:, BLOCK:], 0.0)
    for b in range(own.shape[0] // BLOCK):
        for half, target in enumerate((upper, lower)):
            part = slice(b * BLOCK + half * HALF, b * BLOCK + (half + 1) * HALF)
            target[dests[half, b], 0] = left[part]
            target[dests[half, b], 1] = right[part]


def update_columns(slots, there, dests, own, columns, updates, groups, count):
    rows, order = own.shape
    out = jax.ShapeDtypeStruct((groups, count, HALF, BLOCK), F32)
    out_spec = pl.BlockSpec((groups, 2, HALF, BLOCK), lambda t, s, e, d: (0, t, 0, 0))
    return pl.pallas_call(
        update_kernel,
        out_shape=(out, out),
        grid_spec=pltpu.PrefetchScalarGridSpec(
            num_scalar_prefetch=3,
            grid=(slots.shape[0] // 2,),
            in_specs=[
                pl.BlockSpec(
                    (rows, order), lambda t, s, e, d: (0, 0), pipeline_mode=pl.Buffered(1)
                ),
                pl.BlockSpec((order, 2 * BLOCK), lambda t, s, e, d: (0, t)),
                pl.BlockSpec((1, rows, BLOCK), lambda t, s, e, d: (s[2 * t], 0, 0)),
                pl.BlockSpec((1, rows, BLOCK), lambda t, s, e, d: (s[2 * t + 1], 0, 0)),
            ],
            out_specs=(out_spec, out_spec),
            scratch_shapes=[pltpu.VMEM((rows, 3 * order), BF16)],
        ),
        compiler_params=pltpu.CompilerParams(vmem_limit_bytes=40 * 1024 * 1024),
        cost_estimate=pl.CostEstimate(
            flops=16 * count * BLOCK * rows * order,
            bytes_accessed=4 * count * BLOCK * (2 * rows + order + groups * BLOCK),
            transcendentals=0,
        ),
        name="update_columns",
    )(slots, there, dests, own, columns, updates, updates)


def finish_kernel(
    slots, there, top, root, panel, first_upper, second_upper, first_lower, second_lower, product, target
):
    i = pl.program_id(0)
    columns = first_upper.shape[1] + 1
    target[pl.ds(0, BLOCK, stride=columns), :] = panel[...]
    parts = ((first_upper, second_upper), (first_lower, second_lower))
    for half, (first, second) in enumerate(parts):
        rows = slice(half * HALF, (half + 1) * HALF)
        for k in range(1, columns):
            here = pl.ds(half * HALF * columns + k, HALF, stride=columns)
            total = root[here, :]
            total = total + jnp.where(there[0, i] > 0, first[0, k - 1], 0.0)
            total = total + jnp.where(there[1, i] > 0, second[0, k - 1], 0.0)
            total = total - product[rows, (k - 1) * BLOCK : k * BLOCK]
            target[here, :] = jnp.where(top[i] > 0, 0.0, total)


def finish(slots, there, top, root, panel, upper, lower, product):
    columns = upper.shape[1] + 1
    root_rows = there.shape[1]
    rows = BLOCK * columns
    block = (1,) + upper.shape[1:]

    def received(part, half):
        return pl.BlockSpec(block, lambda i, s, t, p: (s[part, half, i], 0, 0, 0))

    return pl.pallas_call(
        finish_kernel,
        out_shape=jax.ShapeDtypeStruct(root.shape, F32),
        grid_spec=pltpu.PrefetchScalarGridSpec(
            num_scalar_prefetch=3,
            grid=(root_rows,),
            in_specs=[
                pl.BlockSpec((rows, BLOCK), lambda i, s, t, p: (i, 0)),
                pl.BlockSpec((BLOCK, BLOCK), lambda i, s, t, p: (i, 0)),
                received(0, 0),
                received(0, 1),
                received(1, 0),
                received(1, 1),
                pl.BlockSpec((BLOCK, product.shape[1]), lambda i, s, t, p: (i, 0)),
            ],
            out_specs=pl.BlockSpec((rows, BLOCK), lambda i, s, t, p: (i, 0)),
        ),
        cost_estimate=pl.CostEstimate(
            flops=0, bytes_accessed=4 * BLOCK * 5 * rows * root_rows, transcendentals=0
        ),
        name="finish",
    )(slots, there, top, root, panel, upper, upper, lower, lower, product)


def ranks(targets, keys):
    same = targets[..., :, None] == targets[..., None, :]
    before = keys[..., None, :] < keys[..., :, None]
    return jnp.sum(jnp.logical_and(same, before).astype(jnp.int32), axis=-1)


def locate(matches, values):
    matches = matches.astype(jnp.int32)
    return (jnp.sum(matches * values, axis=-1), jnp.sum(matches, axis=-1) > 0)


def times_transposed(left, right, precision):
    return lax.dot_general(
        left, right, (((1,), (1,)), ((), ())), precision=precision, preferred_element_type=F32
    )


def exchange(values, axes):
    return lax.all_to_all(values, axes, split_axis=0, concat_axis=0, tiled=True)


def shift(values, axis, size, step):
    return lax.ppermute(values, axis, [(i, (i + step) % size) for i in range(size)])


def ring(values, axis, size):
    return [values] + [shift(values, axis, size, d) for d in range(1, size)]


def in_order(pieces, axis):
    size = len(pieces)
    return jnp.take(
        jnp.stack(pieces), (lax.axis_index(axis) - jnp.arange(size, dtype=jnp.int32)) % size, axis=0
    )


def after(values, *earlier):
    return lax.optimization_barrier((values,) + earlier)[0]


def per_device(child_pivot, child_border, child_update, index_map, root_front):
    row, col = ("x", "z_hi"), ("y", "core")
    joined = ("z_hi", "half", "x")
    n_x, n_z = lax.axis_size("x"), lax.axis_size("z_hi")
    n_rows = n_x * n_z
    n_y, n_core = lax.axis_size("y"), lax.axis_size("core")
    n_cols = n_y * n_core
    groups = 2 * n_rows
    sibling = lax.axis_index("half")
    row_index = lax.axis_index(row)
    col_index = lax.axis_index(col)
    group = sibling * n_rows + row_index
    block_count = child_border.shape[1]
    pivots = child_border.shape[4]
    local_rows = block_count * BLOCK
    root_rows = root_front.shape[0]
    root_cols = root_front.shape[3]
    numbers = jnp.arange(block_count, dtype=jnp.int32)

    def place_of(groups_of):
        half, x, z = groups_of // n_rows, groups_of // n_z % n_x, groups_of % n_z
        return (z * 2 + half) * n_x + x

    n_zs = 2 * n_z
    z_index = lax.axis_index("z_hi") * 2 + sibling

    def z_shift(values, step):
        spot = lambda z: z % 2 * n_z + z // 2
        pairs = [(spot(z), spot((z + step) % n_zs)) for z in range(n_zs)]
        return lax.ppermute(values, ("half", "z_hi"), pairs)

    child_map = lax.dynamic_index_in_dim(index_map, sibling, 0, keepdims=False).reshape(
        block_count, n_rows
    )
    by_class = child_map.T
    class_dest = by_class % n_cols
    class_rank = ranks(
        class_dest, jnp.where(by_class < n_cols, 0, block_count) + numbers[None, :]
    )
    col_dest = lax.dynamic_index_in_dim(class_dest, col_index, 0, keepdims=False)
    col_rank = lax.dynamic_index_in_dim(class_rank, col_index, 0, keepdims=False)
    row_map = lax.dynamic_index_in_dim(by_class, row_index, 0, keepdims=False)
    row_dest = lax.dynamic_index_in_dim(class_dest, row_index, 0, keepdims=False)
    row_rank = lax.dynamic_index_in_dim(class_rank, row_index, 0, keepdims=False)

    border = child_border.reshape(block_count, BLOCK, pivots)

    wanted, _ = locate(
        jnp.logical_and(
            row_dest[None, :] == col_index,
            row_rank[None, :] == jnp.arange(2, dtype=jnp.int32)[:, None],
        ),
        numbers,
    )
    updates = exchange(
        spread_columns(
            col_dest * 2 + col_rank,
            child_update.reshape(local_rows * block_count, BLOCK),
            2 * n_cols,
            block_count,
        ),
        col,
    )
    borders = lax.all_gather(pick_blocks(wanted, border), row, axis=0, tiled=True)

    flat_source = numbers[:, None] * 2 + class_rank
    wanted_roots = jnp.arange(root_cols, dtype=jnp.int32) * n_cols + col_index
    source_slots, source_there = locate(
        by_class.reshape(1, -1) == wanted_roots[:, None], flat_source.reshape(-1)
    )

    inverse = inverse_factor(child_pivot[0], pivots)
    own_factor = times_transposed(border.reshape(local_rows, pivots), inverse, exact)

    root_view = root_front.reshape(root_rows, BLOCK, root_cols, BLOCK)
    panel_slot = source_slots[0]
    panel_border = lax.dynamic_index_in_dim(borders, panel_slot, 0, keepdims=False)
    panel_factor = times_transposed(panel_border, inverse, exact)
    panel_update = lax.dynamic_index_in_dim(
        updates, panel_slot, 0, keepdims=False
    ) - times_transposed(own_factor, panel_factor, close)
    panel_update = jnp.where(source_there[0], panel_update, 0.0).reshape(block_count, BLOCK, BLOCK)

    sent_blocks, _ = locate(
        place_of(row_map % groups)[None, :] == jnp.arange(groups, dtype=jnp.int32)[:, None], numbers
    )
    every_map = index_map.reshape(2, 1, block_count * n_rows)
    my_roots = jnp.arange(root_rows, dtype=jnp.int32) * groups + group
    sender = place_of(
        jnp.arange(2, dtype=jnp.int32)[:, None, None] * n_rows
        + (jnp.arange(block_count * n_rows, dtype=jnp.int32) % n_rows)[None, None, :]
    )
    got_slots, got_there = locate(every_map == my_roots[None, :, None], sender)

    def extend_add(base, received):
        shape = (-1,) + (1,) * (received.ndim - 1)
        for half in range(2):
            picked = jnp.take(received, got_slots[half], axis=0)
            base = base + jnp.where(got_there[half].reshape(shape), picked, 0.0)
        return base

    panel_got = exchange(jnp.take(panel_update, sent_blocks, axis=0), joined)

    def even(values):
        return jnp.concatenate([values[1:], values[-1:]])

    rest_slots = even(source_slots)
    rest_columns = solve_columns(rest_slots, after(borders, panel_update), inverse)
    own_panel = extend_add(root_view[:, :, 0, :], after(panel_got, rest_columns))

    swaps = [(r * n_cols + c, c * n_rows + r) for r in range(n_rows) for c in range(n_cols)]
    swapped = lax.ppermute(own_panel, row + col, swaps)
    column_panel = lax.all_gather(swapped, ("z_hi", "half", "x"), axis=0, tiled=False).reshape(
        n_z, 2, n_x, root_rows, BLOCK, BLOCK
    )

    sent_place = place_of(row_map % groups)
    sent_z, sent_x = (sent_place // n_x - z_index) % n_zs, sent_place % n_x
    rest_sent = update_columns(
        rest_slots,
        even(source_there.astype(jnp.int32)),
        jnp.stack([sent_x * n_zs + sent_z, sent_z * n_x + sent_x]),
        own_factor,
        after(rest_columns, swapped),
        updates,
        groups,
        root_cols - 1,
    )

    corner = jnp.where(sibling == 0, own_panel[0], shift(own_panel[0], "half", 2, 1))
    corner = in_order(ring(after(corner, swapped), "z_hi", n_z), "z_hi")
    leading_column = in_order(ring(after(corner, rest_sent), "x", n_x), "x").reshape(n_rows, BLOCK, BLOCK)
    kept = n_cols // 2 + 1
    kept_rows = (col_index - jnp.arange(kept, dtype=jnp.int32)) % n_cols
    kept_blocks = jnp.take(leading_column, kept_rows, axis=0)
    leading = in_order(ring(kept_blocks, "y", n_y), "y")
    other_core = shift(leading, "core", 2, 1)
    is_first = lax.axis_index("core") == 0
    leading = jnp.stack(
        [jnp.where(is_first, leading, other_core), jnp.where(is_first, other_core, leading)]
    )

    upper = rest_sent[0].reshape((n_x, n_zs) + rest_sent[0].shape[1:])
    lower = rest_sent[1].reshape((n_zs, n_x) + rest_sent[1].shape[1:])
    lower = [lower[d] for d in range(n_zs)]
    column_panel, upper, lower, leading, panel_sent = lax.optimization_barrier(
        (column_panel, upper, lower, leading, own_panel)
    )
    upper = exchange(upper, "x")
    lower = [lower[0]] + [z_shift(lower[d], d) for d in range(1, n_zs)]
    panel_rows = lax.all_gather(panel_sent, col, axis=2, tiled=True)

    root_inverse = inverse_factor(leading, PANEL)
    lower, root_inverse = lax.optimization_barrier((lower, root_inverse))
    column_factor = solve_columns(
        even(jnp.arange(root_cols, dtype=jnp.int32)), column_panel, root_inverse
    )[:, : (root_cols - 1) * BLOCK]
    upper, lower, column_factor = lax.optimization_barrier((upper, lower, column_factor))
    lower = jnp.stack(lower, axis=1)
    upper = after(upper, lower)
    lower = exchange(lower, "x").reshape((groups,) + rest_sent[1].shape[1:])
    upper = [upper[:, d] for d in range(n_zs)]
    upper = [upper[0]] + [z_shift(upper[d], d) for d in range(1, n_zs)]
    upper = jnp.stack(upper).reshape((groups,) + rest_sent[0].shape[1:])
    got_z, got_x = (z_index - got_slots // n_x) % n_zs, got_slots % n_x

    factor_rows = times_transposed(panel_rows.reshape(root_rows * BLOCK, PANEL), root_inverse, exact)
    global_rows = (
        my_roots[:, None] * BLOCK + jnp.arange(BLOCK, dtype=jnp.int32)[None, :]
    ).reshape(-1)
    is_top = global_rows < PANEL
    above = jnp.logical_and(
        is_top[:, None], jnp.arange(PANEL, dtype=jnp.int32)[None, :] > global_rows[:, None]
    )
    factor_rows = jnp.where(above, 0.0, factor_rows)
    panel_part = lax.dynamic_index_in_dim(
        factor_rows.reshape(-1, n_cols, BLOCK), col_index, 1, keepdims=False
    )
    combined = finish(
        jnp.stack([got_z * n_x + got_x, got_x * n_zs + got_z]),
        got_there.astype(jnp.int32),
        (my_roots < n_cols).astype(jnp.int32),
        root_front.reshape(root_rows * BLOCK * root_cols, BLOCK),
        panel_part,
        upper,
        lower,
        jnp.dot(factor_rows, column_factor, precision=close, preferred_element_type=F32),
    )
    return (own_factor.reshape(child_border.shape), combined.reshape(root_front.shape))


def solution(mesh):
    fine = Mesh(mesh.devices.reshape(2, 4, 2, 4, 2), ("half", "x", "z_hi", "y", "core"))
    row, col = ("x", "z_hi"), ("y", "core")
    in_specs = (
        P("half", None, None),
        P("half", None, row, None, None),
        P("half", None, row, None, None, col, None),
        P(),
        P(None, ("half",) + row, None, None, col, None),
    )
    out_specs = (
        P("half", None, row, None, None),
        P(None, ("half",) + row, None, None, col, None),
    )
    return jax.shard_map(
        per_device, mesh=fine, in_specs=in_specs, out_specs=out_specs, check_vma=False
    )
```

```python
import functools

import jax
import jax.numpy as jnp
from jax import lax
from jax.experimental import pallas as pl
from jax.experimental.pallas import tpu as pltpu
from jax.sharding import Mesh, PartitionSpec as P

PANEL = 1024
BLOCK = 128
STRIP = 32
CHUNK = 256
HALF = 64
F32 = jnp.float32
BF16 = jnp.bfloat16

exact = lax.Precision.HIGHEST
close = lax.Precision.HIGH


def split_three(values):
    high = values.astype(BF16)
    rest = values - high.astype(F32)
    middle = rest.astype(BF16)
    low = (rest - middle.astype(F32)).astype(BF16)
    return high, middle, low


def gram_strip(rows):
    high, middle, low = split_three(rows)
    left = jnp.concatenate([high, high, middle, high, middle, low], axis=0)
    right = jnp.concatenate([high, middle, high, low, middle, high], axis=0)
    return lax.dot_general(left, right, (((0,), (0,)), ((), ())), preferred_element_type=F32)


def eliminate_strip(rows, start):
    lanes = lax.broadcasted_iota(jnp.int32, (STRIP, BLOCK), 1)
    sublanes = lax.broadcasted_iota(jnp.int32, (STRIP, BLOCK), 0)

    def spread(values, row, count):
        return jnp.broadcast_to(values[row : row + 1, :], (count, BLOCK))

    columns = [
        jnp.broadcast_to(rows[j // 8 * 8 :, start + j : start + j + 1], (STRIP - j // 8 * 8, BLOCK))
        for j in range(STRIP)
    ]
    inside = jnp.logical_and(lanes >= start, lanes < start + STRIP)
    rows = jnp.where(inside, jnp.where(lanes - start == sublanes, 1.0, 0.0), rows)
    for j in range(STRIP):
        base = j // 8 * 8
        column = columns[j]
        scale = lax.rsqrt(spread(column, j - base, 8))
        factor = column * jnp.concatenate([scale] * ((STRIP - base) // 8), axis=0)
        for k in range(j + 1, STRIP):
            skip, count = k // 8 * 8 - base, STRIP - k // 8 * 8
            change = factor[skip:] * spread(factor, k - base, count)
            columns[k] = columns[k] - change
        solved = spread(rows[j : j + 1, :] * scale[0:1, :], 0, STRIP - base)
        below = jnp.where(sublanes[base:] > j, factor, 0.0)
        lower = jnp.where(sublanes[base:] == j, solved, rows[base:] - below * solved)
        rows = jnp.concatenate([rows[:base], lower], axis=0) if base else lower
    return rows


def eliminate_block(block):
    for start in range(0, BLOCK, STRIP):
        stop = start + STRIP
        rows = eliminate_strip(block[start:stop, :], start)
        block[start:stop, :] = rows
        if stop < BLOCK:
            change = gram_strip(rows)[stop:, :]
            lanes = lax.broadcasted_iota(jnp.int32, (BLOCK - stop, BLOCK), 1)
            inside = jnp.logical_and(lanes >= start, lanes < stop)
            block[stop:, :] = jnp.where(inside, 0.0, block[stop:, :]) - change


def inverse_factor_kernel(source, state, block, scaled, stack):
    order = state.shape[0]
    count = order // BLOCK
    if len(source.shape) == 2:
        state[...] = source[...]
    else:
        kept = source.shape[2]
        for i in range(count):
            for k in range(i, count):
                if k - i < kept:
                    part = source[k % 2, k // 2, k - i]
                else:
                    part = source[i % 2, i // 2, count + i - k].T
                state[i * BLOCK : (i + 1) * BLOCK, k * BLOCK : (k + 1) * BLOCK] = part
    row_ids = lax.broadcasted_iota(jnp.int32, (BLOCK, BLOCK), 0)
    col_ids = lax.broadcasted_iota(jnp.int32, (BLOCK, BLOCK), 1)

    def update(j):
        start = (j + 1) * BLOCK
        high, middle, low = split_three(scaled[:, start:].T)
        left = jnp.concatenate([low, middle, high, middle, high, high], axis=1)
        state[start:, j * BLOCK : start] = jnp.zeros((order - start, BLOCK), F32)
        for first in range(0, order, CHUNK):
            stop = order if first < start else min(order, first + CHUNK)
            state[start:stop, first : first + CHUNK] = state[
                start:stop, first : first + CHUNK
            ] - jnp.dot(
                left[: stop - start], stack[:, first : first + CHUNK], preferred_element_type=F32
            )

    def step(j, _):
        here = pl.ds(pl.multiple_of(j * BLOCK, BLOCK), BLOCK)
        block[...] = state[here, here]
        eliminate_block(block)
        inverse = jnp.where(col_ids <= row_ids, block[...], 0.0)
        state[here, here] = jnp.where(col_ids == row_ids, 1.0, 0.0).astype(F32)
        high, middle, low = split_three(inverse)
        left = jnp.concatenate([low, middle, high, middle, high, high], axis=1)
        high, middle, low = split_three(state[here, :])
        right = jnp.concatenate([high, middle, low, high, middle, high], axis=0)
        rows = jnp.dot(left, right, preferred_element_type=F32)
        scaled[...] = rows
        state[here, :] = rows
        high, middle, low = split_three(rows)
        for place, part in enumerate((high, middle, low, high, middle, high)):
            stack[place * BLOCK : (place + 1) * BLOCK, :] = part
        for known in range(count - 1):
            pl.when(j == known)(functools.partial(update, known))
        return 0

    lax.fori_loop(0, count, step, 0)
    for i in range(count - 1):
        stop = (i + 1) * BLOCK
        state[i * BLOCK : stop, stop:] = jnp.zeros((BLOCK, order - stop), F32)


def inverse_factor(source, order):
    whole = pl.BlockSpec(memory_space=pltpu.VMEM)
    return pl.pallas_call(
        inverse_factor_kernel,
        out_shape=jax.ShapeDtypeStruct((order, order), F32),
        in_specs=[whole],
        out_specs=whole,
        scratch_shapes=[
            pltpu.VMEM((BLOCK, BLOCK), F32),
            pltpu.VMEM((BLOCK, order), F32),
            pltpu.VMEM((6 * BLOCK, order), BF16),
        ],
        compiler_params=pltpu.CompilerParams(vmem_limit_bytes=32 * 1024 * 1024),
        cost_estimate=pl.CostEstimate(
            flops=60_000_000_000, bytes_accessed=8 * order * order, transcendentals=0
        ),
        name="inverse_factor",
    )(source)


def spread_kernel(slots, source, target):
    blocks = source.shape[0] // target.shape[1]
    for b in range(blocks):
        target[slots[b]] = source[pl.ds(b, target.shape[1], stride=blocks), :]


def spread_columns(slots, source, slot_total, blocks):
    rows = source.shape[0] // blocks
    tile = rows // 4
    return pl.pallas_call(
        spread_kernel,
        out_shape=jax.ShapeDtypeStruct((slot_total, rows, BLOCK), F32),
        grid_spec=pltpu.PrefetchScalarGridSpec(
            num_scalar_prefetch=1,
            grid=(4,),
            in_specs=[pl.BlockSpec((tile * blocks, BLOCK), lambda i, s: (i, 0))],
            out_specs=pl.BlockSpec((slot_total, tile, BLOCK), lambda i, s: (0, i, 0)),
        ),
        compiler_params=pltpu.CompilerParams(vmem_limit_bytes=32 * 1024 * 1024),
        cost_estimate=pl.CostEstimate(
            flops=0, bytes_accessed=4 * BLOCK * rows * (blocks + slot_total), transcendentals=0
        ),
        name="spread_columns",
    )(slots, source)


def copy_kernel(slots, source, target):
    target[...] = source[...]


def pick_blocks(slots, source):
    shape = (slots.shape[0],) + source.shape[1:]
    block = (1,) + source.shape[1:]
    return pl.pallas_call(
        copy_kernel,
        out_shape=jax.ShapeDtypeStruct(shape, F32),
        grid_spec=pltpu.PrefetchScalarGridSpec(
            num_scalar_prefetch=1,
            grid=(shape[0],),
            in_specs=[pl.BlockSpec(block, lambda i, s: (s[i], 0, 0))],
            out_specs=pl.BlockSpec(block, lambda i, s: (i, 0, 0)),
        ),
        cost_estimate=pl.CostEstimate(
            flops=0, bytes_accessed=8 * shape[0] * shape[1] * shape[2], transcendentals=0
        ),
        name="pick_blocks",
    )(slots, source)


def split_two(values):
    high = values.astype(BF16)
    return high, (values - high.astype(F32)).astype(BF16)


def solve_kernel(slots, first, second, inverse, target, high, middle, low):
    order = inverse.shape[0]

    @pl.when(pl.program_id(0) == 0)
    def _():
        for n in range(0, order, CHUNK):
            here = slice(n, n + CHUNK)
            high[here, :], middle[here, :], low[here, :] = split_three(inverse[here, :])

    def turned(block):
        if len(block.shape) == 3:
            return block[0].T
        parts = [block[z, 0, x, 0].T for x in range(block.shape[2]) for z in range(block.shape[0])]
        return jnp.concatenate(parts, axis=0)

    rows_high, rows_middle, rows_low = split_three(
        jnp.concatenate([turned(first), turned(second)], axis=1)
    )
    for n in range(0, order, CHUNK):
        here, depth = slice(n, n + CHUNK), n + CHUNK
        inverse_high, inverse_middle, inverse_low = (
            part[here, :depth] for part in (high, middle, low)
        )
        h, m, l = rows_high[:depth], rows_middle[:depth], rows_low[:depth]
        left = jnp.concatenate(
            [inverse_low, inverse_middle, inverse_high, inverse_middle, inverse_high, inverse_high],
            axis=1,
        )
        right = jnp.concatenate([h, m, l, h, m, h], axis=0)
        target[here, :] = jnp.dot(left, right, preferred_element_type=F32)


def solve_columns(slots, source, inverse):
    count, order = slots.shape[0], inverse.shape[0]
    if len(source.shape) == 3:
        block = (1, BLOCK, order)
        place = lambda slot: (slot, 0, 0)
    else:
        block = (source.shape[0], 1, source.shape[2], 1, BLOCK, BLOCK)
        place = lambda slot: (0, slot % 2, 0, slot // 2, 0, 0)
    return pl.pallas_call(
        solve_kernel,
        out_shape=jax.ShapeDtypeStruct((order, count * BLOCK), F32),
        grid_spec=pltpu.PrefetchScalarGridSpec(
            num_scalar_prefetch=1,
            grid=(count // 2,),
            in_specs=[
                pl.BlockSpec(block, lambda i, s: place(s[2 * i])),
                pl.BlockSpec(block, lambda i, s: place(s[2 * i + 1])),
                pl.BlockSpec((order, order), lambda i, s: (0, 0), pipeline_mode=pl.Buffered(1)),
            ],
            out_specs=pl.BlockSpec((order, 2 * BLOCK), lambda i, s: (0, i)),
            scratch_shapes=[pltpu.VMEM((order, order), BF16)] * 3,
        ),
        compiler_params=pltpu.CompilerParams(vmem_limit_bytes=40 * 1024 * 1024),
        cost_estimate=pl.CostEstimate(
            flops=16 * count * BLOCK * order * order,
            bytes_accessed=8 * count * BLOCK * order,
            transcendentals=0,
        ),
        name="solve_columns",
    )(slots, source, source, inverse)


def update_kernel(
    slots, there, dests, own, columns, first, second, upper, lower, stack
):
    t = pl.program_id(0)
    order = own.shape[1]

    @pl.when(t == 0)
    def _():
        for n in range(0, own.shape[0], CHUNK):
            here = slice(n, n + CHUNK)
            high, low = split_two(own[here, :])
            stack[here, :order] = low
            stack[here, order : 2 * order] = high
            stack[here, 2 * order :] = high

    high, low = split_two(columns[...])
    product = jnp.dot(
        stack[...], jnp.concatenate([high, low, high], axis=0), preferred_element_type=F32
    )
    left = jnp.where(there[2 * t] > 0, first[0] - product[:, :BLOCK], 0.0)
    right = jnp.where(there[2 * t + 1] > 0, second[0] - product[:, BLOCK:], 0.0)
    for b in range(own.shape[0] // BLOCK):
        for half, target in enumerate((upper, lower)):
            part = slice(b * BLOCK + half * HALF, b * BLOCK + (half + 1) * HALF)
            target[dests[half, b], 0] = left[part]
            target[dests[half, b], 1] = right[part]


def update_columns(slots, there, dests, own, columns, updates, groups, count):
    rows, order = own.shape
    out = jax.ShapeDtypeStruct((groups, count, HALF, BLOCK), F32)
    out_spec = pl.BlockSpec((groups, 2, HALF, BLOCK), lambda t, s, e, d: (0, t, 0, 0))
    return pl.pallas_call(
        update_kernel,
        out_shape=(out, out),
        grid_spec=pltpu.PrefetchScalarGridSpec(
            num_scalar_prefetch=3,
            grid=(slots.shape[0] // 2,),
            in_specs=[
                pl.BlockSpec(
                    (rows, order), lambda t, s, e, d: (0, 0), pipeline_mode=pl.Buffered(1)
                ),
                pl.BlockSpec((order, 2 * BLOCK), lambda t, s, e, d: (0, t)),
                pl.BlockSpec((1, rows, BLOCK), lambda t, s, e, d: (s[2 * t], 0, 0)),
                pl.BlockSpec((1, rows, BLOCK), lambda t, s, e, d: (s[2 * t + 1], 0, 0)),
            ],
            out_specs=(out_spec, out_spec),
            scratch_shapes=[pltpu.VMEM((rows, 3 * order), BF16)],
        ),
        compiler_params=pltpu.CompilerParams(vmem_limit_bytes=40 * 1024 * 1024),
        cost_estimate=pl.CostEstimate(
            flops=16 * count * BLOCK * rows * order,
            bytes_accessed=4 * count * BLOCK * (2 * rows + order + groups * BLOCK),
            transcendentals=0,
        ),
        name="update_columns",
    )(slots, there, dests, own, columns, updates, updates)


def finish_kernel(
    slots, there, top, root, panel, first_upper, second_upper, first_lower, second_lower, product, target
):
    i = pl.program_id(0)
    columns = first_upper.shape[1] + 1
    target[pl.ds(0, BLOCK, stride=columns), :] = panel[...]
    parts = ((first_upper, second_upper), (first_lower, second_lower))
    for half, (first, second) in enumerate(parts):
        rows = slice(half * HALF, (half + 1) * HALF)
        for k in range(1, columns):
            here = pl.ds(half * HALF * columns + k, HALF, stride=columns)
            total = root[here, :]
            total = total + jnp.where(there[0, i] > 0, first[0, k - 1], 0.0)
            total = total + jnp.where(there[1, i] > 0, second[0, k - 1], 0.0)
            total = total - product[rows, (k - 1) * BLOCK : k * BLOCK]
            target[here, :] = jnp.where(top[i] > 0, 0.0, total)


def finish(slots, there, top, root, panel, upper, lower, product):
    columns = upper.shape[1] + 1
    root_rows = there.shape[1]
    rows = BLOCK * columns
    block = (1,) + upper.shape[1:]

    def received(part, half):
        return pl.BlockSpec(block, lambda i, s, t, p: (s[part, half, i], 0, 0, 0))

    return pl.pallas_call(
        finish_kernel,
        out_shape=jax.ShapeDtypeStruct(root.shape, F32),
        grid_spec=pltpu.PrefetchScalarGridSpec(
            num_scalar_prefetch=3,
            grid=(root_rows,),
            in_specs=[
                pl.BlockSpec((rows, BLOCK), lambda i, s, t, p: (i, 0)),
                pl.BlockSpec((BLOCK, BLOCK), lambda i, s, t, p: (i, 0)),
                received(0, 0),
                received(0, 1),
                received(1, 0),
                received(1, 1),
                pl.BlockSpec((BLOCK, product.shape[1]), lambda i, s, t, p: (i, 0)),
            ],
            out_specs=pl.BlockSpec((rows, BLOCK), lambda i, s, t, p: (i, 0)),
        ),
        cost_estimate=pl.CostEstimate(
            flops=0, bytes_accessed=4 * BLOCK * 5 * rows * root_rows, transcendentals=0
        ),
        name="finish",
    )(slots, there, top, root, panel, upper, upper, lower, lower, product)


def ranks(targets, keys):
    same = targets[..., :, None] == targets[..., None, :]
    before = keys[..., None, :] < keys[..., :, None]
    return jnp.sum(jnp.logical_and(same, before).astype(jnp.int32), axis=-1)


def locate(matches, values):
    matches = matches.astype(jnp.int32)
    return (jnp.sum(matches * values, axis=-1), jnp.sum(matches, axis=-1) > 0)


def times_transposed(left, right, precision):
    return lax.dot_general(
        left, right, (((1,), (1,)), ((), ())), precision=precision, preferred_element_type=F32
    )


def exchange(values, axes):
    return lax.all_to_all(values, axes, split_axis=0, concat_axis=0, tiled=True)


def shift(values, axis, size, step):
    return lax.ppermute(values, axis, [(i, (i + step) % size) for i in range(size)])


def ring(values, axis, size):
    return [values] + [shift(values, axis, size, d) for d in range(1, size)]


def in_order(pieces, axis):
    size = len(pieces)
    return jnp.take(
        jnp.stack(pieces), (lax.axis_index(axis) - jnp.arange(size, dtype=jnp.int32)) % size, axis=0
    )


def after(values, *earlier):
    return lax.optimization_barrier((values,) + earlier)[0]


def per_device(child_pivot, child_border, child_update, index_map, root_front):
    row, col = ("x", "z_hi"), ("y", "core")
    joined = ("z_hi", "half", "x")
    n_x, n_z = lax.axis_size("x"), lax.axis_size("z_hi")
    n_rows = n_x * n_z
    n_y, n_core = lax.axis_size("y"), lax.axis_size("core")
    n_cols = n_y * n_core
    groups = 2 * n_rows
    sibling = lax.axis_index("half")
    row_index = lax.axis_index(row)
    col_index = lax.axis_index(col)
    group = sibling * n_rows + row_index
    block_count = child_border.shape[1]
    pivots = child_border.shape[4]
    local_rows = block_count * BLOCK
    root_rows = root_front.shape[0]
    root_cols = root_front.shape[3]
    numbers = jnp.arange(block_count, dtype=jnp.int32)

    def place_of(groups_of):
        half, x, z = groups_of // n_rows, groups_of // n_z % n_x, groups_of % n_z
        return (z * 2 + half) * n_x + x

    n_zs = 2 * n_z
    z_index = lax.axis_index("z_hi") * 2 + sibling

    def z_shift(values, step):
        spot = lambda z: z % 2 * n_z + z // 2
        pairs = [(spot(z), spot((z + step) % n_zs)) for z in range(n_zs)]
        return lax.ppermute(values, ("half", "z_hi"), pairs)

    child_map = lax.dynamic_index_in_dim(index_map, sibling, 0, keepdims=False).reshape(
        block_count, n_rows
    )
    by_class = child_map.T
    class_dest = by_class % n_cols
    class_rank = ranks(
        class_dest, jnp.where(by_class < n_cols, 0, block_count) + numbers[None, :]
    )
    col_dest = lax.dynamic_index_in_dim(class_dest, col_index, 0, keepdims=False)
    col_rank = lax.dynamic_index_in_dim(class_rank, col_index, 0, keepdims=False)
    row_map = lax.dynamic_index_in_dim(by_class, row_index, 0, keepdims=False)
    row_dest = lax.dynamic_index_in_dim(class_dest, row_index, 0, keepdims=False)
    row_rank = lax.dynamic_index_in_dim(class_rank, row_index, 0, keepdims=False)

    border = child_border.reshape(block_count, BLOCK, pivots)

    wanted, _ = locate(
        jnp.logical_and(
            row_dest[None, :] == col_index,
            row_rank[None, :] == jnp.arange(2, dtype=jnp.int32)[:, None],
        ),
        numbers,
    )
    updates = exchange(
        spread_columns(
            col_dest * 2 + col_rank,
            child_update.reshape(local_rows * block_count, BLOCK),
            2 * n_cols,
            block_count,
        ),
        col,
    )
    borders = lax.all_gather(pick_blocks(wanted, border), row, axis=0, tiled=True)

    flat_source = numbers[:, None] * 2 + class_rank
    wanted_roots = jnp.arange(root_cols, dtype=jnp.int32) * n_cols + col_index
    source_slots, source_there = locate(
        by_class.reshape(1, -1) == wanted_roots[:, None], flat_source.reshape(-1)
    )

    inverse = inverse_factor(child_pivot[0], pivots)
    own_factor = times_transposed(border.reshape(local_rows, pivots), inverse, exact)

    root_view = root_front.reshape(root_rows, BLOCK, root_cols, BLOCK)
    panel_slot = source_slots[0]
    panel_border = lax.dynamic_index_in_dim(borders, panel_slot, 0, keepdims=False)
    panel_factor = times_transposed(panel_border, inverse, exact)
    panel_update = lax.dynamic_index_in_dim(
        updates, panel_slot, 0, keepdims=False
    ) - times_transposed(own_factor, panel_factor, close)
    panel_update = jnp.where(source_there[0], panel_update, 0.0).reshape(block_count, BLOCK, BLOCK)

    sent_blocks, _ = locate(
        place_of(row_map % groups)[None, :] == jnp.arange(groups, dtype=jnp.int32)[:, None], numbers
    )
    every_map = index_map.reshape(2, 1, block_count * n_rows)
    my_roots = jnp.arange(root_rows, dtype=jnp.int32) * groups + group
    sender = place_of(
        jnp.arange(2, dtype=jnp.int32)[:, None, None] * n_rows
        + (jnp.arange(block_count * n_rows, dtype=jnp.int32) % n_rows)[None, None, :]
    )
    got_slots, got_there = locate(every_map == my_roots[None, :, None], sender)

    def extend_add(base, received):
        shape = (-1,) + (1,) * (received.ndim - 1)
        for half in range(2):
            picked = jnp.take(received, got_slots[half], axis=0)
            base = base + jnp.where(got_there[half].reshape(shape), picked, 0.0)
        return base

    panel_got = exchange(jnp.take(panel_update, sent_blocks, axis=0), joined)

    def even(values):
        return jnp.concatenate([values[1:], values[-1:]])

    rest_slots = even(source_slots)
    rest_columns = solve_columns(rest_slots, after(borders, panel_update), inverse)
    own_panel = extend_add(root_view[:, :, 0, :], after(panel_got, rest_columns))

    swaps = [(r * n_cols + c, c * n_rows + r) for r in range(n_rows) for c in range(n_cols)]
    swapped = lax.ppermute(own_panel, row + col, swaps)
    column_panel = lax.all_gather(swapped, ("z_hi", "half", "x"), axis=0, tiled=False).reshape(
        n_z, 2, n_x, root_rows, BLOCK, BLOCK
    )

    sent_place = place_of(row_map % groups)
    sent_z, sent_x = (sent_place // n_x - z_index) % n_zs, sent_place % n_x
    rest_sent = update_columns(
        rest_slots,
        even(source_there.astype(jnp.int32)),
        jnp.stack([sent_x * n_zs + sent_z, sent_z * n_x + sent_x]),
        own_factor,
        after(rest_columns, swapped),
        updates,
        groups,
        root_cols - 1,
    )

    corner = jnp.where(sibling == 0, own_panel[0], shift(own_panel[0], "half", 2, 1))
    corner = in_order(ring(after(corner, swapped), "z_hi", n_z), "z_hi")
    leading_column = in_order(ring(after(corner, rest_sent), "x", n_x), "x").reshape(n_rows, BLOCK, BLOCK)
    kept = n_cols // 2 + 1
    kept_rows = (col_index - jnp.arange(kept, dtype=jnp.int32)) % n_cols
    kept_blocks = jnp.take(leading_column, kept_rows, axis=0)
    leading = in_order(ring(kept_blocks, "y", n_y), "y")
    other_core = shift(leading, "core", 2, 1)
    is_first = lax.axis_index("core") == 0
    leading = jnp.stack(
        [jnp.where(is_first, leading, other_core), jnp.where(is_first, other_core, leading)]
    )

    upper = rest_sent[0].reshape((n_x, n_zs) + rest_sent[0].shape[1:])
    lower = rest_sent[1].reshape((n_zs, n_x) + rest_sent[1].shape[1:])
    lower = [lower[d] for d in range(n_zs)]
    column_panel, upper, lower, leading, panel_sent = lax.optimization_barrier(
        (column_panel, upper, lower, leading, own_panel)
    )
    upper = exchange(upper, "x")
    lower = [lower[0]] + [z_shift(lower[d], d) for d in range(1, n_zs)]
    panel_rows = lax.all_gather(panel_sent, col, axis=2, tiled=True)

    root_inverse = inverse_factor(leading, PANEL)
    upper, lower, root_inverse = lax.optimization_barrier(
        ([upper[:, d] for d in range(n_zs)], jnp.stack(lower, axis=1), root_inverse)
    )
    lower = exchange(lower, "x").reshape((groups,) + rest_sent[1].shape[1:])
    upper = [upper[0]] + [z_shift(upper[d], d) for d in range(1, n_zs)]
    upper = jnp.stack(upper).reshape((groups,) + rest_sent[0].shape[1:])
    column_factor = solve_columns(
        even(jnp.arange(root_cols, dtype=jnp.int32)), column_panel, root_inverse
    )[:, : (root_cols - 1) * BLOCK]
    got_z, got_x = (z_index - got_slots // n_x) % n_zs, got_slots % n_x

    factor_rows = times_transposed(panel_rows.reshape(root_rows * BLOCK, PANEL), root_inverse, exact)
    global_rows = (
        my_roots[:, None] * BLOCK + jnp.arange(BLOCK, dtype=jnp.int32)[None, :]
    ).reshape(-1)
    is_top = global_rows < PANEL
    above = jnp.logical_and(
        is_top[:, None], jnp.arange(PANEL, dtype=jnp.int32)[None, :] > global_rows[:, None]
    )
    factor_rows = jnp.where(above, 0.0, factor_rows)
    panel_part = lax.dynamic_index_in_dim(
        factor_rows.reshape(-1, n_cols, BLOCK), col_index, 1, keepdims=False
    )
    combined = finish(
        jnp.stack([got_z * n_x + got_x, got_x * n_zs + got_z]),
        got_there.astype(jnp.int32),
        (my_roots < n_cols).astype(jnp.int32),
        root_front.reshape(root_rows * BLOCK * root_cols, BLOCK),
        panel_part,
        upper,
        lower,
        jnp.dot(factor_rows, column_factor, precision=close, preferred_element_type=F32),
    )
    return (own_factor.reshape(child_border.shape), combined.reshape(root_front.shape))


def solution(mesh):
    fine = Mesh(mesh.devices.reshape(2, 4, 2, 4, 2), ("half", "x", "z_hi", "y", "core"))
    row, col = ("x", "z_hi"), ("y", "core")
    in_specs = (
        P("half", None, None),
        P("half", None, row, None, None),
        P("half", None, row, None, None, col, None),
        P(),
        P(None, ("half",) + row, None, None, col, None),
    )
    out_specs = (
        P("half", None, row, None, None),
        P(None, ("half",) + row, None, None, col, None),
    )
    return jax.shard_map(
        per_device, mesh=fine, in_specs=in_specs, out_specs=out_specs, check_vma=False
    )
```
